32 devices in a mesh: ctx: 8 (over z, y), wa: 4 (over x, core).
Axes of the slice: x: 2, y: 2, z: 4, core: 2. Of those that a mesh axis runs over, the one named last changes fastest.
Arguments:
- layer_input: bfloat16 [4096, 1536], P('ctx'), may hold values from -6 to 6
- segment_ids: int32 [4096], P('ctx'), may hold values from 0 to 4, as said below
- expert_ids: int32 [4096, 2], P('ctx'), may hold values from 0 to 7, all different within a row; in each aligned block of 512 rows (0 to 511, 512 to 1023, ...) at most 256 rows name the same one
- norm_gain: float32 [1536], replicated, may hold values from 0.1 to 1.9
- query_weight: bfloat16 [1536, 1536], P(None, 'wa'), may hold values from -0.15625 to 0.15625
- key_weight: bfloat16 [1536, 512], P(None, 'wa'), may hold values from -0.15625 to 0.15625
- value_weight: bfloat16 [1536, 512], P(None, 'wa'), may hold values from -0.15625 to 0.15625
- output_weight: bfloat16 [1536, 1536], P('wa'), may hold values from -2.5 to 2.5
- ffn_gain: float32 [1536], replicated, may hold values from 0.1 to 1.9
- router_weight: bfloat16 [1536, 8], replicated, may hold values from -0.078125 to 0.078125
- gate_weight: bfloat16 [8, 1536, 1024], P(None, None, 'wa'), may hold values from -0.15625 to 0.15625
- up_weight: bfloat16 [8, 1536, 1024], P(None, None, 'wa'), may hold values from -0.15625 to 0.15625
- down_weight: bfloat16 [8, 1024, 1536], P(None, 'wa'), may hold values from -0.25 to 0.25
- cotangent: bfloat16 [4096, 1536], P('ctx'), may hold values from -6 to 6
Outputs:
- layer_output: float32 [4096, 1536], P('ctx')
- input_grad: float32 [4096, 1536], P('ctx')
- norm_gain_grad: float32 [1536], P('ctx')
- query_grad: float32 [1536, 1536], P('ctx', 'wa')
- key_grad: float32 [1536, 512], P('ctx', 'wa')
- value_grad: float32 [1536, 512], P('ctx', 'wa')
- output_grad: float32 [1536, 1536], P('wa', 'ctx')
- ffn_gain_grad: float32 [1536], P('ctx')
- router_grad: float32 [1536, 8], P('ctx')
- gate_grad: float32 [8, 1536, 1024], P(None, 'ctx', 'wa')
- up_grad: float32 [8, 1536, 1024], P(None, 'ctx', 'wa')
- down_grad: float32 [8, 1024, 1536], P(None, 'wa', 'ctx')
The draws below stay inside these ranges and needn't reach their ends.
Inputs may be any that keep to these rules, and one draw needn't show every extreme that they name: `segment_ids`: segment ids never fall along the sequence; there are 5 documents, each of 64 tokens or more. `expert_ids`: among the 512 tokens of one index of ctx, no expert is named more than 256 times, a bound that some block reaches; a token's two experts differ.
All inputs are finite; a program needn't handle non-finite values.
Results may differ from the reference program's by a relative error of at most 0.03.
Values may be sent and summed in bfloat16 or wider, within the bound.
No kernel may reach another device: no remote copies, remote signals or barrier semaphores. Data moves between devices by JAX's collectives and lax.ppermute only.
A program may use at most 192 MiB of HBM per device.

```python
import math
import jax
import jax.numpy as jnp
import numpy as np
from jax import lax

D = 1536
H = 24
KV = 8
HD = 64
FE = 1024
EXPERTS = 8
TOK_DEV = 512
CAP = 256
TOKENS = 4096
N_CTX = 8


def draw_segment_ids(key, part):
    key = jax.random.fold_in(key, 11)
    first_key, second_key, third_key, fourth_key = jax.random.split(key, 4)
    eighth = TOK_DEV // 8
    first_cut = jax.random.randint(first_key, (), eighth, 2 * eighth + 1)
    second_cut = first_cut + jax.random.randint(second_key, (), eighth, 2 * eighth + 1)
    middle_base = (TOKENS // TOK_DEV // 2 + 1) * TOK_DEV
    third_cut = middle_base + jax.random.randint(third_key, (), eighth, 7 * eighth + 1)
    fourth_cut = TOKENS - jax.random.randint(fourth_key, (), eighth, 4 * eighth + 1)
    positions = jnp.arange(TOKENS, dtype=jnp.int32)
    ids = (positions >= first_cut).astype(jnp.int32) + (positions >= second_cut).astype(jnp.int32)
    ids = ids + (positions >= third_cut).astype(jnp.int32) + (positions >= fourth_cut).astype(jnp.int32)
    return ids


def with_spikes(drawn, key, source, target, blocks, factor):
    owner, partner = [(jnp.arange(drawn.shape[axis_at]) // (drawn.shape[axis_at] // blocks)).reshape([-1 if axis == axis_at else 1 for axis in range(drawn.ndim)]) for axis_at in (source, target)]
    chosen = jax.random.permutation(key, blocks)[partner]
    strong = (owner == chosen) | (owner == (partner + blocks // 2) % blocks)
    return jnp.where(strong, factor * drawn, drawn)


def shard_levels(own_key, extent, cuts, least, top_value):
    loudness = 1.0
    for dim, parts in cuts:
        heights = jax.random.uniform(jax.random.fold_in(jax.random.fold_in(own_key, 6), dim), (parts,), jnp.float32, least / len(cuts), top_value / len(cuts))
        loudness = loudness * jnp.repeat(jnp.exp(heights), extent[dim] // parts).reshape((-1,) + (1,) * (len(extent) - 1 - dim))
    return loudness


def shared_out(key, own, number, rows, amount, top, bound, skew):
    order = jax.random.permutation(key, amount)
    packed, ordinary = shares(amount, rows * top, bound, skew, True), shares(amount, rows * top, bound, skew, False)
    places = jnp.arange(amount)

    def named(lengths, offset_by):
        used = int((lengths > 0).sum())
        fixed = max(1, used // 4)
        shifted = fixed + (places - fixed + offset_by * (used - fixed)) % max(1, amount - fixed)
        return jnp.zeros((amount,), jnp.int32).at[order[jnp.where(places < fixed, places, shifted)]].set(jnp.asarray(lengths, jnp.int32))

    lengths = jnp.where(number % 4 == 0, named(packed, number // 4), named(ordinary, number - number // 4 - 1))
    mixed = jax.random.permutation(jax.random.fold_in(own, 3), amount)
    donor, sink = mixed[0:amount // 2 * 2:2], mixed[1:amount // 2 * 2:2]
    margin = jnp.minimum(lengths[donor] - 1, bound - lengths[sink]) // 2
    margin = jnp.where((donor == order[0]) | (sink == order[0]) | (lengths[sink] == 0), 0, jnp.maximum(margin, 0))
    shifted = jax.random.randint(jax.random.fold_in(own, 4), (amount // 2,), 0, 1 << 20) % (margin + 1)
    lengths = lengths.at[donor].add(-shifted).at[sink].add(shifted)
    items = jnp.searchsorted(jnp.cumsum(lengths), jnp.arange(rows * top), side="right").astype(jnp.int32)
    listing = items.reshape(top, rows).T
    listing = listing[jax.random.permutation(jax.random.fold_in(own, 1), rows)]
    offset_by = jax.random.randint(jax.random.fold_in(own, 2), (rows, 1), 0, top)
    return jnp.take_along_axis(listing, (jnp.arange(top)[None, :] + offset_by) % top, axis=1)


def shares(count, total, bound, slope, full):
    weights = [(1 << 20) // math.isqrt(standing ** slope) + 1 for standing in range(1, count + 1)]
    largest = bound if full else min(bound, max(-(-total // count), total * weights[0] // sum(weights)))
    least = 1 if total - largest >= count - 1 else 0
    given, spare = [largest] + [least] * (count - 1), total - largest - least * (count - 1)
    while spare > 0:
        candidates = [i for i in range(1, count) if given[i] < largest] or [i for i in range(1, count) if given[i] < bound]
        mass, budget = sum([weights[i] for i in candidates]), spare
        for i in candidates:
            extra = min(bound - given[i], max(1, budget * weights[i] // mass), spare)
            given[i] = given[i] + extra
            spare = spare - extra
    return np.array(given)


def centred(key, extent, deviation, reach, cuts=(), kind=jnp.bfloat16):
    factor_of = shard_levels(key, extent, cuts, -0.22, 0.18) if cuts else 1.0
    drawn = jax.random.normal(key, extent, jnp.float32) * deviation * factor_of
    return jnp.minimum(jnp.maximum(drawn, -reach), reach).astype(kind)


def bell_draw_with(own_key, dims, deviation, bound, pieces, heavy, kind=jnp.bfloat16):
    array = deviation * jax.random.normal(own_key, dims, jnp.float32)
    if pieces:
        array = array * shard_levels(own_key, dims, pieces, -0.22, 0.18)
    return jnp.clip(with_spikes(array, jax.random.fold_in(own_key, 3), *heavy), -bound, bound).astype(kind)


def setup_inputs(seed: int = 0) -> dict:
    splits = jax.random.split(jax.random.key(seed), 15)
    layer_input = bell_draw_with(splits[0], (TOKENS, D), 1.0, 6.0, ((0, 8),), (0, 1, 8, 2.0))
    segment_ids = draw_segment_ids(jax.random.fold_in(splits[14], 71), 0)
    expert_ids_keys = jax.random.split(jax.random.fold_in(splits[2], 1), TOKENS // TOK_DEV)
    expert_ids_turns = jax.random.permutation(jax.random.fold_in(splits[2], 3), TOKENS // TOK_DEV)
    expert_ids = jax.vmap(lambda own, number: shared_out(jax.random.fold_in(splits[2], 2), own, number, TOK_DEV, EXPERTS, 2, CAP, 2))(expert_ids_keys, expert_ids_turns).reshape((TOKENS, 2))
    norm_gain = jnp.clip(1.0 + 0.18 * jax.random.normal(splits[3], (D,), jnp.float32), 0.1, 1.9)
    query_weight = centred(splits[4], (D, H * HD), D ** -0.5, 0.15625, ((1, 4),))
    key_weight = centred(splits[5], (D, KV * HD), D ** -0.5, 0.15625, ((1, 4),))
    value_weight = centred(splits[6], (D, KV * HD), D ** -0.5, 0.15625, ((1, 4),))
    output_weight = centred(splits[7], (H * HD, D), ((TOKENS // 16) ** 0.5 * (H * HD) ** -0.5), 2.5, ((0, 4),))
    ffn_gain = jnp.clip(1.0 + 0.18 * jax.random.normal(splits[8], (D,), jnp.float32), 0.1, 1.9)
    router_weight = centred(splits[9], (D, EXPERTS), (4 * D) ** -0.5, 0.078125)
    gate_weight = centred(splits[10], (EXPERTS, D, FE), D ** -0.5, 0.15625, ((2, 4),))
    up_weight = centred(splits[11], (EXPERTS, D, FE), D ** -0.5, 0.15625, ((2, 4),))
    down_weight = centred(splits[12], (EXPERTS, FE, D), (FE // 2) ** -0.5, 0.25, ((1, 4),))
    cotangent = bell_draw_with(splits[13], (TOKENS, D), 1.0, 6.0, ((0, 8),), (0, 1, 8, 2.0))
    return dict(layer_input=layer_input, segment_ids=segment_ids, expert_ids=expert_ids, norm_gain=norm_gain, query_weight=query_weight, key_weight=key_weight, value_weight=value_weight, output_weight=output_weight, ffn_gain=ffn_gain, router_weight=router_weight, gate_weight=gate_weight, up_weight=up_weight, down_weight=down_weight, cotangent=cotangent)


eps = 1e-05
highest = lax.Precision.HIGHEST

@jax.custom_vjp
def low(v):
    return lax.optimization_barrier(v.astype(jnp.bfloat16)).astype(jnp.float32)

@jax.custom_vjp
def low_back(v):
    return v

def low_keep(v):
    return (low(v), None)

def low_pass(kept, grad):
    return (grad,)

def back_keep(v):
    return (v, None)

def back_low(kept, grad):
    return (low(grad),)
low.defvjp(low_keep, low_pass)
low_back.defvjp(back_keep, back_low)

def both_ways(value):
    return low_back(low(value))

def norm_rows(values, gain):
    factor = lax.rsqrt(lax.optimization_barrier(jnp.mean(values * values, axis=-1, keepdims=True)) + eps)
    return values * factor * gain

def slot_table(routes):
    flat = routes.reshape(-1)
    onehot = (flat[:, None] == jnp.arange(EXPERTS, dtype=jnp.int32)[None, :]).astype(jnp.int32)
    before = jnp.cumsum(onehot, axis=0) - onehot
    slots = lax.optimization_barrier(jnp.sum(before * onehot, axis=1))
    position = (flat * CAP + slots).astype(jnp.int32)
    entries = jnp.arange(flat.shape[0], dtype=jnp.int32)
    owner = jnp.zeros((EXPERTS * CAP,), jnp.int32).at[position].set(entries)
    filled = jnp.zeros((EXPERTS * CAP,), jnp.int32).at[position].set(1)
    return (position, owner, filled)

def pick_rows(block_rows, indices):
    return block_rows[indices]

def attend_rows(query_rows, seg_rows, keys, values, seg_keys):
    scores = jnp.einsum('qngd,knd->ngqk', query_rows, keys, precision=highest) * HD ** (-0.5)
    scores = low_back(scores)
    same = (seg_rows[:, None] == seg_keys[None, :])[None, None]
    scores = jnp.where(same, scores, -1e+30)
    largest = lax.optimization_barrier(jnp.max(scores, axis=-1, keepdims=True))
    weights = jnp.exp(scores - largest)
    probs = weights / lax.optimization_barrier(jnp.sum(weights, axis=-1, keepdims=True))
    return jnp.einsum('ngqk,knd->qngd', low(probs), values, precision=highest)

def layer(layer_input, norm_gain, query_weight, key_weight, value_weight, output_weight, ffn_gain, router_weight, gate_weight, up_weight, down_weight, segment_ids, expert_ids):
    normed_one = low(norm_rows(layer_input, norm_gain))
    queries = both_ways(jnp.dot(normed_one, query_weight, precision=highest))
    keys = both_ways(jnp.dot(normed_one, key_weight, precision=highest)).reshape(TOKENS, KV, HD)
    values = both_ways(jnp.dot(normed_one, value_weight, precision=highest)).reshape(TOKENS, KV, HD)
    block_rows = math.gcd(TOKENS, 512)
    blocks = TOKENS // block_rows
    query_blocks = queries.reshape(blocks, block_rows, KV, H // KV, HD)

    def one_block(block_in):
        return attend_rows(block_in[0], block_in[1], keys, values, segment_ids)
    attended = lax.map(jax.checkpoint(one_block), (query_blocks, segment_ids.reshape(blocks, block_rows)))
    heads = both_ways(attended.reshape(TOKENS, H * HD))
    attention = low_back(jnp.dot(heads, output_weight, precision=highest))
    hidden_one = layer_input + attention
    normed_two = low(norm_rows(hidden_one, ffn_gain))
    logits = jnp.dot(normed_two, router_weight, precision=highest)
    picks = (expert_ids[:, :, None] == jnp.arange(EXPERTS, dtype=jnp.int32)[None, None, :]).astype(jnp.float32)
    chosen = lax.optimization_barrier(jnp.sum(picks * logits[:, None, :], axis=-1))
    gates = jax.nn.softmax(chosen, axis=-1)
    position, owner, filled = jax.vmap(slot_table)(expert_ids.reshape(N_CTX, TOK_DEV, 2))
    token_blocks = normed_two.reshape(N_CTX, TOK_DEV, D)
    expert_in = jax.vmap(pick_rows)(token_blocks, owner // 2) * filled[:, :, None].astype(jnp.float32)
    expert_in = expert_in.reshape(N_CTX, EXPERTS, CAP, D)
    gate_pre = low_back(jnp.einsum('secd,edf->secf', expert_in, gate_weight, precision=highest))
    up_pre = low_back(jnp.einsum('secd,edf->secf', expert_in, up_weight, precision=highest))
    mids = low(jax.nn.silu(gate_pre) * up_pre)
    expert_out = low_back(jnp.einsum('secf,efd->secd', mids, down_weight, precision=highest))
    per_token = jax.vmap(pick_rows)(expert_out.reshape(N_CTX, EXPERTS * CAP, D), position)
    per_token = per_token.reshape(TOKENS, 2, D)
    return hidden_one + lax.optimization_barrier(jnp.sum(gates[:, :, None] * per_token, axis=1))

def reference(layer_input, segment_ids, expert_ids, norm_gain, query_weight, key_weight, value_weight, output_weight, ffn_gain, router_weight, gate_weight, up_weight, down_weight, cotangent):

    def forward(inputs, gain_one, weight_query, weight_key, weight_value, weight_output, gain_two, weight_router, weight_gate, weight_up, weight_down):
        return layer(inputs, gain_one, weight_query, weight_key, weight_value, weight_output, gain_two, weight_router, weight_gate, weight_up, weight_down, segment_ids, expert_ids)
    result, pullback = jax.vjp(forward, layer_input.astype(jnp.float32), norm_gain.astype(jnp.float32), query_weight.astype(jnp.float32), key_weight.astype(jnp.float32), value_weight.astype(jnp.float32), output_weight.astype(jnp.float32), ffn_gain.astype(jnp.float32), router_weight.astype(jnp.float32), gate_weight.astype(jnp.float32), up_weight.astype(jnp.float32), down_weight.astype(jnp.float32))
    grads = pullback(cotangent.astype(jnp.float32))
    return (result, grads[0], grads[1], grads[2], grads[3], grads[4], grads[5], grads[6], grads[7], grads[8], grads[9], grads[10])
```

```python
import functools

import jax
import jax.numpy as jnp
from jax import lax
from jax.experimental import pallas as pl
from jax.experimental.pallas import tpu as pltpu
from jax.sharding import PartitionSpec as P

H = 24
KV = 8
HD = 64
eps = 1e-05
NEG = -1e30
F32 = jnp.float32
BF = jnp.bfloat16
VLIM = 60 * 1024 * 1024
EXTRA = 16
NT = (((1,), (1,)), ((), ()))
TN = (((0,), (0,)), ((), ()))


def digits_of(n):
    out = []
    stride = 1
    while n > 1:
        if stride == 1 and n % 2 == 0:
            radix = 2
        elif n % 4 == 0:
            radix = 4
        else:
            radix = n
        out.append((stride, radix))
        stride *= radix
        n //= radix
    return out


def moved(n, digit, shift):
    stride, radix = digit
    pairs = []
    for i in range(n):
        d = (i // stride) % radix
        pairs.append((i, i + ((d + shift) % radix - d) * stride))
    return pairs


def hop(x, n, digit, shift=1):
    return lax.ppermute(x, "ctx", moved(n, digit, shift))


def other_core(x):
    return lax.ppermute(x, "wa", [(i, i ^ 1) for i in range(4)])


def other_chip(x):
    return lax.ppermute(x, "wa", [(i, i ^ 2) for i in range(4)])


def rel_keys(digits):
    keys = [()]
    for _, radix in digits:
        keys = [k + (r,) for r in range(radix) for k in keys]
    return keys


def set_digit(key, at, value):
    return key[:at] + (value,) + key[at + 1 :]


def gather_ctx(x, n, digits, order):
    blocks = {tuple(0 for _ in digits): x}
    for at in order:
        fresh = {}
        for key, block in blocks.items():
            moving = block
            for s in range(1, digits[at][1]):
                moving = hop(moving, n, digits[at])
                fresh[set_digit(key, at, s)] = moving
        blocks.update(fresh)
    return blocks


def scatter_ctx(blocks, n, digits, order, add):
    for at in order:
        keys = list(blocks)
        rest = [k for k in keys if k[at] == 0]
        moving = {k: blocks[set_digit(k, at, 1 % digits[at][1])] for k in rest}
        for s in range(2, digits[at][1] + 1):
            stacked = jnp.stack([moving[k] for k in rest], 0) if len(rest) > 1 else moving[rest[0]]
            stacked = hop(stacked, n, digits[at])
            for i, k in enumerate(rest):
                got = stacked[i] if len(rest) > 1 else stacked
                moving[k] = add(got, blocks[set_digit(k, at, s % digits[at][1])])
        blocks = moving
    return blocks[tuple(0 for _ in digits)]


def add_bf(a, b):
    return (a.astype(F32) + b.astype(F32)).astype(BF)


def exchange_ctx(stack, n, digits):
    keys = rel_keys(digits)
    for at in range(len(digits)):
        parts = {i: stack[i] for i in range(len(keys))} if not isinstance(stack, dict) else stack
        for s in range(1, digits[at][1]):
            chosen = [i for i, k in enumerate(keys) if k[at] == s]
            bundle = jnp.stack([parts[i] for i in chosen], 0)
            bundle = hop(bundle, n, digits[at], s)
            for place, i in enumerate(chosen):
                parts[i] = bundle[place]
        stack = parts
    return stack


def digit_offset(me, key, digits, sign):
    place = 0
    for (stride, radix), r in zip(digits, key):
        d = (me // stride) % radix
        place = place + ((d + sign * r) % radix) * stride
    return place


def rel_rows(x, me, digits, rows, sign):
    return jnp.stack(
        [
            lax.dynamic_slice_in_dim(x, digit_offset(me, k, digits, sign) * rows, rows, 0)
            for k in rel_keys(digits)
        ],
        0,
    )


def params(**kw):
    return pltpu.CompilerParams(vmem_limit_bytes=VLIM, **kw)


def vspec(n):
    return [pl.BlockSpec(memory_space=pltpu.VMEM)] * n


def project_kernel(core_ref, x_ref, gain_ref, wq_ref, wk_ref, wv_ref, extra_ref, a1_ref, q_ref, kv_ref):
    tok = x_ref.shape[0]
    half = tok // 2
    kvw = wk_ref.shape[1]
    for i in range(2):
        start = pl.multiple_of(((core_ref[0] + i) % 2) * half, half)
        x = x_ref[pl.ds(start, half), :].astype(F32)
        inv = lax.rsqrt(jnp.mean(x * x, axis=-1, keepdims=True) + eps)
        a1 = (x * inv * gain_ref[...]).astype(BF)
        rows = pl.ds(i * half, half)
        a1_ref[rows, :] = a1
        kv_ref[rows, :kvw] = jnp.dot(a1, wk_ref[...], preferred_element_type=F32).astype(BF)
        kv_ref[rows, kvw:] = jnp.dot(a1, wv_ref[...], preferred_element_type=F32).astype(BF)
        q = jnp.dot(a1, wq_ref[...], preferred_element_type=F32).astype(BF)
        q_ref[rows, :] = (q.astype(F32) * HD ** (-0.5)).astype(BF)
    kv_ref[pl.ds(tok, EXTRA), :] = extra_ref[...]


def project(core, x, gain, wq, wk, wv, extra):
    tok, width = x.shape
    return pl.pallas_call(
        project_kernel,
        out_shape=(
            jax.ShapeDtypeStruct((tok, width), BF),
            jax.ShapeDtypeStruct((tok, wq.shape[1]), BF),
            jax.ShapeDtypeStruct((tok + EXTRA, 2 * wk.shape[1]), BF),
        ),
        in_specs=[pl.BlockSpec(memory_space=pltpu.SMEM)] + vspec(6),
        out_specs=tuple(vspec(3)),
        compiler_params=params(),
        name="project",
    )(core, x, gain, wq, wk, wv, extra)


def seg_onehot(row):
    lane = lax.broadcasted_iota(jnp.int32, (16, row.shape[1]), 0).astype(F32)
    return jnp.where(lane == row, 1.0, 0.0).astype(BF)


def seg_rows_of(block, tok):
    width = block.shape[1]
    return [
        block[tok : tok + EXTRA, :].astype(F32)[i : i + 1, :] for i in range(tok // width)
    ]


def attend_kernel(nb, heads, groups, *refs):
    q_ref = refs[0]
    kv_refs = refs[1 : 1 + nb]
    hf_ref, hb_ref, lse_ref = refs[1 + nb : 4 + nb]
    kv_s, q_s, m_s, l_s, acc_s = refs[4 + nb :]
    tok = q_ref.shape[0]
    kvw = kv_refs[0].shape[1] // 2
    for b in range(nb):
        kv_s[b] = kv_refs[b][...]
    for h in range(heads):
        q_s[h] = q_ref[:, h * HD : (h + 1) * HD]
    own = jnp.concatenate(seg_rows_of(kv_s[0], tok), axis=1)
    own_hot = seg_onehot(own)
    own_lo = jnp.min(own)
    own_hi = jnp.max(own)
    m_s[...] = jnp.full(m_s.shape, NEG, F32)
    l_s[...] = jnp.zeros(l_s.shape, F32)
    acc_s[...] = jnp.zeros(acc_s.shape, F32)

    def body(b, masked):
        block = kv_s[b]
        if masked:
            seg = jnp.concatenate(seg_rows_of(block, tok), axis=1)
            same = lax.dot_general(seg_onehot(seg), own_hot, TN, preferred_element_type=F32) > 0.5
        for n in range(heads // groups):
            k = block[:tok, n * HD : (n + 1) * HD]
            v = block[:tok, kvw + n * HD : kvw + (n + 1) * HD]
            for h in range(n * groups, (n + 1) * groups):
                s = lax.dot_general(k, q_s[h], NT, preferred_element_type=F32)
                if masked:
                    s = jnp.where(same, s, NEG)
                m_old = m_s[h : h + 1, :]
                m_new = jnp.maximum(m_old, jnp.max(s, axis=0, keepdims=True))
                p = jnp.exp(s - m_new)
                f = jnp.exp(m_old - m_new)
                m_s[h : h + 1, :] = m_new
                l_s[h : h + 1, :] = l_s[h : h + 1, :] * f + jnp.sum(p, axis=0, keepdims=True)
                acc_s[h] = acc_s[h] * f + lax.dot_general(
                    v, p.astype(BF), TN, preferred_element_type=F32
                )

    def visit(b, carry):
        seg = jnp.concatenate(seg_rows_of(kv_s[b], tok), axis=1)
        lo = jnp.min(seg)
        hi = jnp.max(seg)
        plain = (lo == hi) & (own_lo == own_hi) & (lo == own_lo)
        touch = (lo <= own_hi) & (own_lo <= hi)

        @pl.when(plain)
        def _():
            body(b, False)

        @pl.when(touch & jnp.logical_not(plain))
        def _():
            body(b, True)

        return carry

    lax.fori_loop(0, nb, visit, 0)
    rows = []
    for h in range(heads):
        rows.append(acc_s[h] / l_s[h : h + 1, :])
        lse_ref[h : h + 1, :] = m_s[h : h + 1, :] + jnp.log(l_s[h : h + 1, :])
    out = jnp.concatenate(rows, axis=0).T
    hf_ref[...] = out
    hb_ref[...] = out.astype(BF)


def attend(q, blocks, heads, groups):
    tok = q.shape[0]
    nb = len(blocks)
    return pl.pallas_call(
        functools.partial(attend_kernel, nb, heads, groups),
        out_shape=(
            jax.ShapeDtypeStruct((tok, heads * HD), F32),
            jax.ShapeDtypeStruct((tok, heads * HD), BF),
            jax.ShapeDtypeStruct((8, tok), F32),
        ),
        in_specs=vspec(1 + nb),
        out_specs=tuple(vspec(3)),
        scratch_shapes=[
            pltpu.VMEM((nb,) + blocks[0].shape, BF),
            pltpu.VMEM((heads, tok, HD), BF),
            pltpu.VMEM((8, tok), F32),
            pltpu.VMEM((8, tok), F32),
            pltpu.VMEM((heads, HD, tok), F32),
        ],
        compiler_params=params(),
        name="attend",
    )(q, *blocks)


def attend_back_kernel(nb, heads, groups, *refs):
    q_ref, do_ref, hf_ref, lse_ref = refs[:4]
    kv_refs = refs[4 : 4 + nb]
    dq_ref, dk_ref, dv_ref = refs[4 + nb : 7 + nb]
    kv_s, q_s, do_s, delta_s, dq_s = refs[7 + nb :]
    tok = q_ref.shape[0]
    kvw = kv_refs[0].shape[1] // 2
    for b in range(nb):
        kv_s[b] = kv_refs[b][...]
    for h in range(heads):
        q_s[h] = q_ref[:, h * HD : (h + 1) * HD]
        do_s[h] = do_ref[:, h * HD : (h + 1) * HD]
    prod = (do_ref[...].astype(F32) * hf_ref[...]).T
    for h in range(heads):
        delta_s[h : h + 1, :] = jnp.sum(prod[h * HD : (h + 1) * HD, :], axis=0, keepdims=True)
    own = jnp.concatenate(seg_rows_of(kv_s[0], tok), axis=1)
    own_hot = seg_onehot(own)
    own_lo = jnp.min(own)
    own_hi = jnp.max(own)
    dq_s[...] = jnp.zeros(dq_s.shape, F32)

    def body(b, masked):
        block = kv_s[b]
        if masked:
            seg = jnp.concatenate(seg_rows_of(block, tok), axis=1)
            same = lax.dot_general(seg_onehot(seg), own_hot, TN, preferred_element_type=F32) > 0.5
        for n in range(heads // groups):
            k = block[:tok, n * HD : (n + 1) * HD]
            v = block[:tok, kvw + n * HD : kvw + (n + 1) * HD]
            dk = None
            for h in range(n * groups, (n + 1) * groups):
                s = lax.dot_general(k, q_s[h], NT, preferred_element_type=F32)
                p = jnp.exp(s - lse_ref[h : h + 1, :])
                if masked:
                    p = jnp.where(same, p, 0.0)
                dv_h = jnp.dot(p.astype(BF), do_s[h], preferred_element_type=F32)
                dp = lax.dot_general(v, do_s[h], NT, preferred_element_type=F32)
                ds = (p * (dp - delta_s[h : h + 1, :])).astype(BF)
                dk_h = jnp.dot(ds, q_s[h], preferred_element_type=F32)
                dq_s[h] += lax.dot_general(k, ds, TN, preferred_element_type=F32)
                dk = dk_h if dk is None else dk + dk_h
                dv = dv_h if h == n * groups else dv + dv_h
            dk_ref[b, :, n * HD : (n + 1) * HD] = dk.astype(BF)
            dv_ref[b, :, n * HD : (n + 1) * HD] = dv.astype(BF)

    def visit(b, carry):
        seg = jnp.concatenate(seg_rows_of(kv_s[b], tok), axis=1)
        lo = jnp.min(seg)
        hi = jnp.max(seg)
        plain = (lo == hi) & (own_lo == own_hi) & (lo == own_lo)
        touch = (lo <= own_hi) & (own_lo <= hi)

        @pl.when(plain)
        def _():
            body(b, False)

        @pl.when(touch & jnp.logical_not(plain))
        def _():
            body(b, True)

        @pl.when(jnp.logical_not(touch))
        def _():
            dk_ref[b] = jnp.zeros(dk_ref.shape[1:], BF)
            dv_ref[b] = jnp.zeros(dv_ref.shape[1:], BF)

        return carry

    lax.fori_loop(0, nb, visit, 0)
    out = jnp.concatenate([dq_s[h] for h in range(heads)], axis=0).T
    dq_ref[...] = (out * HD ** (-0.5)).astype(BF)


def attend_back(q, do, hf, lse, blocks, heads, groups):
    tok = q.shape[0]
    nb = len(blocks)
    kvw = blocks[0].shape[1] // 2
    return pl.pallas_call(
        functools.partial(attend_back_kernel, nb, heads, groups),
        out_shape=(
            jax.ShapeDtypeStruct((tok, heads * HD), BF),
            jax.ShapeDtypeStruct((nb, tok, kvw), BF),
            jax.ShapeDtypeStruct((nb, tok, kvw), BF),
        ),
        in_specs=vspec(4 + nb),
        out_specs=tuple(vspec(3)),
        scratch_shapes=[
            pltpu.VMEM((nb,) + blocks[0].shape, BF),
            pltpu.VMEM((heads, tok, HD), BF),
            pltpu.VMEM((heads, tok, HD), BF),
            pltpu.VMEM((8, tok), F32),
            pltpu.VMEM((heads, HD, tok), F32),
        ],
        compiler_params=params(),
        name="attend_back",
    )(q, do, hf, lse, *blocks)


def experts_kernel(
    core_ref,
    ids_ref,
    mine_ref,
    theirs_ref,
    g_ref,
    wr_ref,
    wg_ref,
    wu_ref,
    wd_ref,
    mix_keep_ref,
    mix_send_ref,
    dx_keep_ref,
    dx_send_ref,
    gates_ref,
    ent_a_ref,
    ent_b_ref,
    a2_s,
    g_s,
    mix_s,
    dx_s,
    back_s,
):
    e = pl.program_id(0)
    tok, width = a2_s.shape
    half = tok // 2
    experts = wr_ref.shape[1]
    lane = lax.broadcasted_iota(jnp.int32, (tok, experts), 1)
    first = ids_ref[:, 0:1]
    second = ids_ref[:, 1:2]

    @pl.when(e == 0)
    def _():
        a2_s[:half, :] = mine_ref[...]
        a2_s[half:, :] = theirs_ref[...]
        for i in range(2):
            start = pl.multiple_of(((core_ref[0] + i) % 2) * half, half)
            g_s[pl.ds(i * half, half), :] = g_ref[pl.ds(start, half), :]
        logits = jnp.dot(a2_s[...], wr_ref[...], preferred_element_type=F32)
        one = jnp.sum(jnp.where(lane == first, logits, 0.0), axis=1, keepdims=True)
        two = jnp.sum(jnp.where(lane == second, logits, 0.0), axis=1, keepdims=True)
        top = jnp.maximum(one, two)
        one = jnp.exp(one - top)
        two = jnp.exp(two - top)
        total = one + two
        gates_ref[...] = jnp.where(lane == first, one / total, 0.0) + jnp.where(
            lane == second, two / total, 0.0
        )
        mix_s[...] = jnp.zeros(mix_s.shape, F32)
        dx_s[...] = jnp.zeros(dx_s.shape, F32)
        back_s[...] = jnp.zeros(back_s.shape, F32)
        ent_a_ref[...] = jnp.zeros(ent_a_ref.shape, BF)
        ent_b_ref[...] = jnp.zeros(ent_b_ref.shape, BF)

    wg = wg_ref[0]
    wu = wu_ref[0]
    wd = wd_ref[0]
    for i in range(2):
        rows = pl.ds(i * half, half)
        a2 = a2_s[rows, :]
        u = jnp.dot(a2, wg, preferred_element_type=F32)
        w = jnp.dot(a2, wu, preferred_element_type=F32)
        m = lax.dot_general(g_s[rows, :], wd, NT, preferred_element_type=F32)
        here = lane[:half] == e
        gate = jnp.sum(jnp.where(here, gates_ref[rows, :], 0.0), axis=1, keepdims=True)
        pick_one = (ids_ref[rows, 0:1] == e).astype(F32)
        pick_two = (ids_ref[rows, 1:2] == e).astype(F32)
        sig = 1.0 / (1.0 + jnp.exp(-u))
        act = u * sig
        mid = (act * w).astype(BF).astype(F32)
        back = jnp.sum(mid * m, axis=1, keepdims=True) * (pick_one + pick_two)
        back_s[rows, :] += jnp.where(here, back, 0.0)
        mid = mid * gate
        gm = gate * m
        up_back = gm * act
        pre_back = gm * w * sig * (1.0 + u * (1.0 - sig))
        mid_b = mid.astype(BF)
        up_b = up_back.astype(BF)
        pre_b = pre_back.astype(BF)
        mix_s[rows, :] += jnp.dot(mid_b, wd, preferred_element_type=F32)
        dx_s[rows, :] += lax.dot_general(
            pre_b, wg, NT, preferred_element_type=F32
        ) + lax.dot_general(up_b, wu, NT, preferred_element_type=F32)
        for kind, value in enumerate((mid, pre_back, up_back)):
            for c, pick in enumerate((pick_one, pick_two)):
                part = (value * pick).astype(BF)
                unit = 2 * kind + c
                if unit < 5:
                    ent_a_ref[unit, rows, :] += part
                else:
                    ent_b_ref[0, rows, :] += part

    @pl.when(e == pl.num_programs(0) - 1)
    def _():
        mix_keep_ref[...] = mix_s[:half, :]
        mix_send_ref[...] = mix_s[half:, :].astype(BF)
        dx_keep_ref[:, :width] = dx_s[:half, :]
        dx_send_ref[:, :width] = dx_s[half:, :].astype(BF)
        pad = jnp.zeros((half, 128 - experts), F32)
        dx_keep_ref[:, width:] = jnp.concatenate([back_s[:half, :], pad], axis=1)
        dx_send_ref[:, width:] = jnp.concatenate([back_s[half:, :], pad], axis=1).astype(BF)


def experts_call(core, ids, mine, theirs, g, wr, wg, wu, wd):
    half, width = mine.shape
    tok = 2 * half
    experts, _, hidden = wg.shape

    def whole(*shape):
        return pl.BlockSpec(shape, lambda e, *_: (0,) * len(shape))

    def one(*shape):
        return pl.BlockSpec((1,) + shape, lambda e, *_: (e,) + (0,) * len(shape))

    return pl.pallas_call(
        experts_kernel,
        out_shape=(
            jax.ShapeDtypeStruct((half, width), F32),
            jax.ShapeDtypeStruct((half, width), BF),
            jax.ShapeDtypeStruct((half, width + 128), F32),
            jax.ShapeDtypeStruct((half, width + 128), BF),
            jax.ShapeDtypeStruct((tok, experts), F32),
            jax.ShapeDtypeStruct((5, tok, hidden), BF),
            jax.ShapeDtypeStruct((1, tok, hidden), BF),
        ),
        grid=(experts,),
        in_specs=[
            pl.BlockSpec(memory_space=pltpu.SMEM),
            whole(tok, 2),
            whole(half, width),
            whole(half, width),
            whole(tok, width),
            whole(width, experts),
            one(width, hidden),
            one(width, hidden),
            one(hidden, width),
        ],
        out_specs=(
            whole(half, width),
            whole(half, width),
            whole(half, width + 128),
            whole(half, width + 128),
            whole(tok, experts),
            whole(5, tok, hidden),
            whole(1, tok, hidden),
        ),
        scratch_shapes=[
            pltpu.VMEM((tok, width), BF),
            pltpu.VMEM((tok, width), BF),
            pltpu.VMEM((tok, width), F32),
            pltpu.VMEM((tok, width), F32),
            pltpu.VMEM((tok, experts), F32),
        ],
        compiler_params=params(dimension_semantics=("arbitrary",)),
        name="experts",
    )(core, ids, mine, theirs, g, wr, wg, wu, wd)


def expert_grads_kernel(nb, seeded, *refs):
    ids_refs = refs[:nb]
    a_refs = refs[nb : 2 * nb]
    b_refs = refs[2 * nb : 3 * nb]
    xm_refs = refs[3 * nb : 4 * nb]
    xo_refs = refs[4 * nb : 5 * nb]
    gm_refs = refs[5 * nb : 6 * nb]
    go_refs = refs[6 * nb : 7 * nb]
    prev = refs[7 * nb : 7 * nb + 3] if seeded else None
    outs = refs[-3:]
    e = pl.program_id(0).astype(F32)
    sums = [None, None, None]
    for b in range(nb):
        half = xm_refs[b].shape[1]
        for i in range(2):
            rows = pl.ds(i * half, half)
            one = (ids_refs[b][rows, 0:1] == e).astype(F32)
            two = (ids_refs[b][rows, 1:2] == e).astype(F32)
            xt = (xm_refs if i == 0 else xo_refs)[b][...]
            gt = (gm_refs if i == 0 else go_refs)[b][...]
            for kind in range(3):
                left = a_refs[b][2 * kind, rows, :].astype(F32)
                right = (a_refs[b][2 * kind + 1, rows, :] if kind < 2 else b_refs[b][0, rows, :]).astype(F32)
                value = (left * one + right * two).astype(BF)
                term = jnp.dot(gt if kind == 0 else xt, value, preferred_element_type=F32)
                sums[kind] = term if sums[kind] is None else sums[kind] + term
    for kind in range(3):
        outs[kind][0] = sums[kind] + prev[kind][0] if seeded else sums[kind]


def expert_grads(ids, ent_a, ent_b, xm, xo, gm, go, experts, prev=None):
    nb = len(ids)
    cols = xm[0].shape[0]
    hidden = ent_a[0].shape[-1]
    operands = list(ids) + list(ent_a) + list(ent_b) + list(xm) + list(xo) + list(gm) + list(go)
    specs = [pl.BlockSpec(x.shape, lambda e, nd=x.ndim: (0,) * nd) for x in operands]
    out_spec = pl.BlockSpec((1, cols, hidden), lambda e: (e, 0, 0))
    if prev is not None:
        operands += list(prev)
        specs += [out_spec] * 3
    return pl.pallas_call(
        functools.partial(expert_grads_kernel, nb, prev is not None),
        out_shape=(jax.ShapeDtypeStruct((experts, cols, hidden), F32),) * 3,
        grid=(experts,),
        in_specs=specs,
        out_specs=(out_spec,) * 3,
        compiler_params=params(dimension_semantics=("arbitrary",)),
        name="expert_grads",
    )(*operands)


def per_device(
    n_ctx,
    layer_input,
    segment_ids,
    expert_ids,
    norm_gain,
    query_weight,
    key_weight,
    value_weight,
    output_weight,
    ffn_gain,
    router_weight,
    gate_weight,
    up_weight,
    down_weight,
    cotangent,
):
    tok, width = layer_input.shape
    half = tok // 2
    groups = H // KV
    kv_local = key_weight.shape[1] // HD
    heads = kv_local * groups
    kvw = key_weight.shape[1]
    experts = gate_weight.shape[0]
    cols = width // n_ctx
    digits = digits_of(n_ctx)
    keys = rel_keys(digits)
    upper_first = list(range(1, len(digits))) + [0]
    lower_first = list(range(len(digits)))
    me = lax.axis_index("ctx")
    core = lax.axis_index("wa") % 2
    core_arr = jnp.full((1,), core, jnp.int32)

    def mine_first(x):
        return jnp.where(core == 0, x, jnp.concatenate([x[half:], x[:half]], axis=0))

    def my_half(x):
        return lax.dynamic_slice_in_dim(x, core * half, half, 0)

    def whole_order(mine, theirs):
        return jnp.where(
            core == 0,
            jnp.concatenate([mine, theirs], axis=0),
            jnp.concatenate([theirs, mine], axis=0),
        )

    segs = mine_first(segment_ids).astype(BF)
    ids = mine_first(expert_ids)
    extra = jnp.concatenate([segs, ids[:, 0].astype(BF), ids[:, 1].astype(BF)])
    extra = jnp.pad(extra, (0, EXTRA * 2 * kvw - extra.shape[0])).reshape(EXTRA, 2 * kvw)
    a1, q, kv = project(
        core_arr, layer_input, norm_gain[None, :], query_weight, key_weight, value_weight, extra
    )
    kv_blocks = gather_ctx(kv, n_ctx, digits, upper_first)
    kv_list = [kv_blocks[k] for k in keys]
    heads_f32, heads_b, lse = attend(q, kv_list, heads, groups)

    used = tok // (2 * kvw)
    ids_list = []
    for block in kv_list:
        rows = block[tok + used : tok + 3 * used].astype(F32).reshape(2, tok)
        ids_list.append(rows.T)

    g_mine = my_half(cotangent)
    g_out = rel_rows(g_mine.T, me, digits, cols, 1)
    g_got = exchange_ctx(g_out, n_ctx, digits)
    g_stack = jnp.stack([g_got[i] for i in range(n_ctx)], 0)
    g_far = other_core(g_stack)

    far = jnp.dot(heads_b[half:], output_weight, preferred_element_type=F32).astype(BF)
    got = other_core(far)
    near = jnp.dot(heads_b[:half], output_weight, preferred_element_type=F32)
    near = (near + got.astype(F32)).astype(BF)
    got = other_chip(near)
    hidden_one = my_half(layer_input).astype(F32) + near.astype(F32) + got.astype(F32)
    inv_two = lax.rsqrt(jnp.mean(hidden_one * hidden_one, axis=-1, keepdims=True) + eps)
    a2_mine = (hidden_one * inv_two * ffn_gain).astype(BF)
    a2_far = other_core(a2_mine)
    a2_out = rel_rows(a2_mine.T, me, digits, cols, 1)
    a2_got = exchange_ctx(a2_out, n_ctx, digits)
    a2_stack = jnp.stack([a2_got[i] for i in range(n_ctx)], 0)
    a2_stack_far = other_core(a2_stack)

    mix_keep, mix_send, dx_keep, dx_send, gates, ent_a, ent_b = experts_call(
        core_arr,
        ids,
        a2_mine,
        a2_far,
        cotangent,
        router_weight,
        gate_weight,
        up_weight,
        down_weight,
    )
    ent_a_blocks = gather_ctx(ent_a, n_ctx, digits, upper_first)
    ent_b_blocks = gather_ctx(ent_b, n_ctx, digits, lower_first)

    near = (dx_keep + other_core(dx_send).astype(F32)).astype(BF)
    total = near.astype(F32) + other_chip(near).astype(F32)
    gate_back = total[:, width : width + experts]
    gate_half = gates[:half]
    picked = (
        (ids[:half, 0:1] == jnp.arange(experts)[None, :]) | (ids[:half, 1:2] == jnp.arange(experts)[None, :])
    ).astype(F32)
    logit_grad = picked * gate_half * (
        gate_back - jnp.sum(gate_half * gate_back, axis=-1, keepdims=True)
    )
    logit_b = logit_grad.astype(BF)
    normed_back = total[:, :width] + lax.dot_general(
        logit_b, router_weight, NT, preferred_element_type=F32
    )
    upstream = g_mine.astype(F32)
    ffn_term = jnp.sum(normed_back * hidden_one * inv_two, axis=0)
    scaled = normed_back * ffn_gain
    hidden_grad = upstream + inv_two * (
        scaled
        - hidden_one * inv_two * inv_two * jnp.mean(scaled * hidden_one, axis=-1, keepdims=True)
    )
    att_mine = hidden_grad.astype(BF)
    att_far = other_core(att_mine)
    att = jnp.concatenate([att_mine, att_far], axis=0)
    head_grad = lax.dot_general(att, output_weight, NT, preferred_element_type=F32).astype(BF)

    dq, dk, dv = attend_back(q, head_grad, heads_f32, lse, kv_list, heads, groups)
    dk_sum = scatter_ctx(
        {k: dk[i] for i, k in enumerate(keys)}, n_ctx, digits, lower_first, add_bf
    )
    dv_sum = scatter_ctx(
        {k: dv[i] for i, k in enumerate(keys)}, n_ctx, digits, upper_first, add_bf
    )

    part = (
        lax.dot_general(dq, query_weight, NT, preferred_element_type=F32)
        + lax.dot_general(dk_sum, key_weight, NT, preferred_element_type=F32)
        + lax.dot_general(dv_sum, value_weight, NT, preferred_element_type=F32)
    )
    near = (part[:half] + other_core(part[half:].astype(BF)).astype(F32)).astype(BF)
    normed_back = near.astype(F32) + other_chip(near).astype(F32)
    x_mine = my_half(layer_input).astype(F32)
    inv_one = lax.rsqrt(jnp.mean(x_mine * x_mine, axis=-1, keepdims=True) + eps)
    norm_term = jnp.sum(normed_back * x_mine * inv_one, axis=0)
    scaled = normed_back * norm_gain
    in_mine = hidden_grad + inv_one * (
        scaled - x_mine * inv_one * inv_one * jnp.mean(scaled * x_mine, axis=-1, keepdims=True)
    )
    input_grad = whole_order(in_mine, other_core(in_mine))

    near = (mix_keep + other_core(mix_send).astype(F32)).astype(BF)
    out_mine = hidden_one + near.astype(F32) + other_chip(near).astype(F32)
    layer_output = whole_order(out_mine, other_core(out_mine))

    a1_rel = rel_rows(a1.T, me, digits, cols, -1).reshape(width, tok)
    att_rel = rel_rows(att.T, me, digits, cols, -1).reshape(width, tok)
    a2_rel = rel_rows(a2_mine.T, me, digits, cols, -1).reshape(width, half)
    ffn_rel = rel_rows(ffn_term[:, None], me, digits, cols, -1).reshape(width, 1)
    norm_rel = rel_rows(norm_term[:, None], me, digits, cols, -1).reshape(width, 1)
    out_term = jnp.dot(att_rel, heads_b, preferred_element_type=F32)
    router_term = jnp.dot(a2_rel, logit_b, preferred_element_type=F32)
    pad = jnp.zeros((width, 128 - experts - 1), F32)
    early = jnp.concatenate([out_term, router_term, ffn_rel, pad], axis=1).astype(BF)
    early = early.reshape(n_ctx, cols, early.shape[1])
    rows = jnp.concatenate([dq, dk_sum, dv_sum], axis=1)
    late = jnp.dot(a1_rel, rows, preferred_element_type=F32)
    pad = jnp.zeros((width, 127), F32)
    late = jnp.concatenate([late, norm_rel, pad], axis=1).astype(BF)
    late = late.reshape(n_ctx, cols, late.shape[1])
    early = scatter_ctx(
        {k: early[i] for i, k in enumerate(keys)}, n_ctx, digits, lower_first, add_bf
    ).astype(F32)
    late = scatter_ctx(
        {k: late[i] for i, k in enumerate(keys)}, n_ctx, digits, lower_first, add_bf
    ).astype(F32)
    qw = heads * HD
    output_grad = early[:, :qw].T
    small = jnp.concatenate(
        [early[:, qw : qw + experts + 1], late[:, qw + 2 * kvw : qw + 2 * kvw + 1]], axis=1
    )
    small = small + other_core(small)
    router_grad = small[:, :experts]
    ffn_grad = small[:, experts]
    norm_grad = small[:, experts + 1]
    query_grad = late[:, :qw]
    key_grad = late[:, qw : qw + kvw]
    value_grad = late[:, qw + kvw : qw + 2 * kvw]

    sums = None
    for at in range(0, n_ctx, 8):
        some = range(at, min(at + 8, n_ctx))
        sums = expert_grads(
            [ids_list[i] for i in some],
            [ent_a_blocks[keys[i]] for i in some],
            [ent_b_blocks[keys[i]] for i in some],
            [a2_stack[i] for i in some],
            [a2_stack_far[i] for i in some],
            [g_stack[i] for i in some],
            [g_far[i] for i in some],
            experts,
            sums,
        )
    down_grad, gate_grad, up_grad = sums
    down_grad = jnp.swapaxes(down_grad, 1, 2)
    return (
        layer_output,
        input_grad,
        norm_grad,
        query_grad,
        key_grad,
        value_grad,
        output_grad,
        ffn_grad,
        router_grad,
        gate_grad,
        up_grad,
        down_grad,
    )


def solution(mesh):
    in_specs = (
        P("ctx", None),
        P("ctx"),
        P("ctx", None),
        P(),
        P(None, "wa"),
        P(None, "wa"),
        P(None, "wa"),
        P("wa", None),
        P(),
        P(),
        P(None, None, "wa"),
        P(None, None, "wa"),
        P(None, "wa", None),
        P("ctx", None),
    )
    out_specs = (
        P("ctx", None),
        P("ctx", None),
        P("ctx"),
        P("ctx", "wa"),
        P("ctx", "wa"),
        P("ctx", "wa"),
        P("wa", "ctx"),
        P("ctx"),
        P("ctx", None),
        P(None, "ctx", "wa"),
        P(None, "ctx", "wa"),
        P(None, "wa", "ctx"),
    )
    return jax.shard_map(
        functools.partial(per_device, mesh.shape["ctx"]),
        mesh=mesh,
        in_specs=in_specs,
        out_specs=out_specs,
        check_vma=False,
    )
```

```python
import functools

import jax
import jax.numpy as jnp
from jax import lax
from jax.experimental import pallas as pl
from jax.experimental.pallas import tpu as pltpu
from jax.sharding import PartitionSpec as P

H = 24
KV = 8
HD = 64
eps = 1e-05
NEG = -1e30
F32 = jnp.float32
BF = jnp.bfloat16
VLIM = 60 * 1024 * 1024
EXTRA = 16
NT = (((1,), (1,)), ((), ()))
TN = (((0,), (0,)), ((), ()))


def digits_of(n):
    out = []
    stride = 1
    while n > 1:
        if stride == 1 and n % 2 == 0:
            radix = 2
        elif n % 4 == 0:
            radix = 4
        else:
            radix = n
        out.append((stride, radix))
        stride *= radix
        n //= radix
    return out


def moved(n, digit, shift):
    stride, radix = digit
    pairs = []
    for i in range(n):
        d = (i // stride) % radix
        pairs.append((i, i + ((d + shift) % radix - d) * stride))
    return pairs


def hop(x, n, digit, shift=1):
    return lax.ppermute(x, "ctx", moved(n, digit, shift))


def other_core(x):
    return lax.ppermute(x, "wa", [(i, i ^ 1) for i in range(4)])


def other_chip(x):
    return lax.ppermute(x, "wa", [(i, i ^ 2) for i in range(4)])


def rel_keys(digits):
    keys = [()]
    for _, radix in digits:
        keys = [k + (r,) for r in range(radix) for k in keys]
    return keys


def set_digit(key, at, value):
    return key[:at] + (value,) + key[at + 1 :]


def gather_ctx(x, n, digits, order):
    blocks = {tuple(0 for _ in digits): x}
    for at in order:
        fresh = {}
        for key, block in blocks.items():
            moving = block
            for s in range(1, digits[at][1]):
                moving = hop(moving, n, digits[at])
                fresh[set_digit(key, at, s)] = moving
        blocks.update(fresh)
    return blocks


def scatter_ctx(stack, n, order, add, hold=lambda at, x: x):
    moving = stack
    hops = 0
    for at in reversed(range(len(order))):
        radix = order[at][1]
        if isinstance(moving, (list, tuple)):
            blocks = moving
        else:
            per = moving.shape[0] // radix
            blocks = [moving[r * per : (r + 1) * per] for r in range(radix)]
        moving = blocks[1]
        for s in range(2, radix + 1):
            moving = hold(hops, hop(moving, n, order[at]))
            moving = add(moving, blocks[s % radix])
            hops += 1
    return moving[0]


def add_bf(a, b):
    return (a.astype(F32) + b.astype(F32)).astype(BF)


def stack_kernel(places, *refs):
    for i, (at, unit) in enumerate(places):
        refs[-1][i] = refs[at][unit]


def stacked(pieces):
    arrays = []
    places = []
    for array, unit in pieces:
        at = next((i for i, x in enumerate(arrays) if x is array), None)
        if at is None:
            at = len(arrays)
            arrays.append(array)
        places.append((at, unit))
    shape = (len(pieces),) + arrays[0].shape[1:]
    return pl.pallas_call(
        functools.partial(stack_kernel, tuple(places)),
        out_shape=jax.ShapeDtypeStruct(shape, arrays[0].dtype),
        in_specs=vspec(len(arrays)),
        out_specs=vspec(1)[0],
        compiler_params=params(),
        name="stacked",
        cost_estimate=cost(1),
    )(*arrays)


def exchange_top(groups, n, digits):
    return [groups[0]] + [hop(groups[r], n, digits[-1], r) for r in range(1, len(groups))]


def exchange_rest(groups, n, digits):
    keys = rel_keys(digits)
    per = n // len(groups)
    parts = {i: (groups[i // per], i % per) for i in range(n)}
    for at in reversed(range(len(digits) - 1)):
        for s in range(1, digits[at][1]):
            chosen = [i for i, k in enumerate(keys) if k[at] == s]
            bundle = hop(stacked([parts[i] for i in chosen]), n, digits[at], s)
            for place, i in enumerate(chosen):
                parts[i] = (bundle, place)
    return [parts[i] for i in range(n)]


def swapped(pieces, first):
    arrays = []
    for array, _ in pieces:
        if not any(array is x for x in arrays):
            arrays.append(array)
    held = tie(arrays, first)
    pieces = [(held[next(i for i, x in enumerate(arrays) if x is a)], u) for a, u in pieces]
    near = stacked(pieces)
    return near, other_core(near)


def digit_offset(me, key, digits, sign):
    place = 0
    for (stride, radix), r in zip(digits, key):
        d = (me // stride) % radix
        place = place + ((d + sign * r) % radix) * stride
    return place


def tie_kernel(*refs):
    pass


def tie(xs, first):
    xs, first = list(xs), list(first)
    return pl.pallas_call(
        tie_kernel,
        out_shape=tuple(jax.ShapeDtypeStruct(x.shape, x.dtype) for x in xs),
        in_specs=anywhere(len(xs) + len(first)),
        out_specs=tuple(anywhere(len(xs))),
        input_output_aliases={i: i for i in range(len(xs))},
        name="tie",
    )(*xs, *first)


def diagonal(x):
    return lax.ppermute(x, "wa", [(i, i ^ 3) for i in range(4)])


def all_parts(near, far):
    return [near, other_core(far), other_chip(near), diagonal(far)]


def cost(us):
    return pl.CostEstimate(flops=int(us * 1e9), bytes_accessed=int(us * 3e6), transcendentals=0)


def params(**kw):
    return pltpu.CompilerParams(vmem_limit_bytes=VLIM, **kw)


def vspec(n):
    return [pl.BlockSpec(memory_space=pltpu.VMEM)] * n


def drop_first(kernel, at, count):
    if not count:
        return kernel

    def waiting(*refs):
        kernel(*refs[:at], *refs[at + count :])

    return waiting


def anywhere(count):
    return [pl.BlockSpec(memory_space=pl.ANY)] * count


def project_kernel(core_ref, x_ref, gain_ref, wq_ref, wk_ref, wv_ref, extra_ref, a1_ref, q_ref, kv_ref):
    tok = x_ref.shape[0]
    half = tok // 2
    kvw = wk_ref.shape[1]
    for i in range(2):
        start = pl.multiple_of(((core_ref[0] + i) % 2) * half, half)
        x = x_ref[pl.ds(start, half), :].astype(F32)
        inv = lax.rsqrt(jnp.mean(x * x, axis=-1, keepdims=True) + eps)
        a1 = (x * inv * gain_ref[...][None, :]).astype(BF)
        rows = pl.ds(i * half, half)
        a1_ref[rows, :] = a1
        kv_ref[rows, :kvw] = jnp.dot(a1, wk_ref[...], preferred_element_type=F32).astype(BF)
        kv_ref[rows, kvw:] = jnp.dot(a1, wv_ref[...], preferred_element_type=F32).astype(BF)
        q = jnp.dot(a1, wq_ref[...], preferred_element_type=F32).astype(BF)
        q_ref[rows, :] = (q.astype(F32) * HD ** (-0.5)).astype(BF)
    kv_ref[pl.ds(tok, EXTRA), :] = extra_ref[...]


def project(core, x, gain, wq, wk, wv, extra):
    tok, width = x.shape
    return pl.pallas_call(
        project_kernel,
        out_shape=(
            jax.ShapeDtypeStruct((tok, width), BF),
            jax.ShapeDtypeStruct((tok, wq.shape[1]), BF),
            jax.ShapeDtypeStruct((tok + EXTRA, 2 * wk.shape[1]), BF),
        ),
        in_specs=[pl.BlockSpec(memory_space=pltpu.SMEM)] + vspec(6),
        out_specs=tuple(vspec(3)),
        compiler_params=params(),
        name="project",
        cost_estimate=cost(5),
    )(core, x, gain, wq, wk, wv, extra)


def seg_onehot(row):
    lane = lax.broadcasted_iota(jnp.int32, (16, row.shape[1]), 0).astype(F32)
    return jnp.where(lane == row, 1.0, 0.0).astype(BF)


def seg_rows_of(block, tok):
    width = block.shape[1]
    return [
        block[tok : tok + EXTRA, :].astype(F32)[i : i + 1, :] for i in range(tok // width)
    ]


def attend_kernel(nb, heads, groups, *refs):
    q_ref = refs[0]
    kv_refs = refs[1 : 1 + nb]
    hf_ref, near_ref, far_ref, lse_ref = refs[1 + nb : 5 + nb]
    kv_s, q_s, m_s, l_s, acc_s = refs[5 + nb :]
    tok = q_ref.shape[0]
    kvw = kv_refs[0].shape[1] // 2
    for b in range(nb):
        kv_s[b] = kv_refs[b][...]
    for h in range(heads):
        q_s[h] = q_ref[:, h * HD : (h + 1) * HD]
    own = jnp.concatenate(seg_rows_of(kv_s[0], tok), axis=1)
    own_hot = seg_onehot(own)
    own_lo = jnp.min(own)
    own_hi = jnp.max(own)
    m_s[...] = jnp.full(m_s.shape, NEG, F32)
    l_s[...] = jnp.zeros(l_s.shape, F32)
    acc_s[...] = jnp.zeros(acc_s.shape, F32)

    def body(b, masked):
        block = kv_s[b]
        if masked:
            seg = jnp.concatenate(seg_rows_of(block, tok), axis=1)
            same = lax.dot_general(seg_onehot(seg), own_hot, TN, preferred_element_type=F32) > 0.5
        for n in range(heads // groups):
            k = block[:tok, n * HD : (n + 1) * HD]
            v = block[:tok, kvw + n * HD : kvw + (n + 1) * HD]
            for h in range(n * groups, (n + 1) * groups):
                s = lax.dot_general(k, q_s[h], NT, preferred_element_type=F32)
                if masked:
                    s = jnp.where(same, s, NEG)
                m_old = m_s[h : h + 1, :]
                m_new = jnp.maximum(m_old, jnp.max(s, axis=0, keepdims=True))
                p = jnp.exp(s - m_new)
                f = jnp.exp(m_old - m_new)
                m_s[h : h + 1, :] = m_new
                l_s[h : h + 1, :] = l_s[h : h + 1, :] * f + jnp.sum(p, axis=0, keepdims=True)
                acc_s[h] = acc_s[h] * f + lax.dot_general(
                    v, p.astype(BF), TN, preferred_element_type=F32
                )

    def visit(b, carry):
        seg = jnp.concatenate(seg_rows_of(kv_s[b], tok), axis=1)
        lo = jnp.min(seg)
        hi = jnp.max(seg)
        plain = (lo == hi) & (own_lo == own_hi) & (lo == own_lo)
        touch = (lo <= own_hi) & (own_lo <= hi)

        @pl.when(plain)
        def _():
            body(b, False)

        @pl.when(touch & jnp.logical_not(plain))
        def _():
            body(b, True)

        return carry

    lax.fori_loop(0, nb, visit, 0)
    rows = []
    for h in range(heads):
        rows.append(acc_s[h] / l_s[h : h + 1, :])
        lse_ref[h : h + 1, :] = m_s[h : h + 1, :] + jnp.log(l_s[h : h + 1, :])
    out = jnp.concatenate(rows, axis=0).T
    hf_ref[...] = out
    near_ref[...] = out[: tok // 2].astype(BF)
    far_ref[...] = out[tok // 2 :].astype(BF)


def attend(q, blocks, heads, groups, first=()):
    tok = q.shape[0]
    nb = len(blocks)
    return pl.pallas_call(
        drop_first(functools.partial(attend_kernel, nb, heads, groups), 1 + nb, len(first)),
        out_shape=(
            jax.ShapeDtypeStruct((tok, heads * HD), F32),
            jax.ShapeDtypeStruct((tok // 2, heads * HD), BF),
            jax.ShapeDtypeStruct((tok // 2, heads * HD), BF),
            jax.ShapeDtypeStruct((8, tok), F32),
        ),
        in_specs=vspec(1 + nb) + anywhere(len(first)),
        out_specs=tuple(vspec(4)),
        scratch_shapes=[
            pltpu.VMEM((nb,) + blocks[0].shape, BF),
            pltpu.VMEM((heads, tok, HD), BF),
            pltpu.VMEM((8, tok), F32),
            pltpu.VMEM((8, tok), F32),
            pltpu.VMEM((heads, HD, tok), F32),
        ],
        compiler_params=params(),
        name="attend",
        cost_estimate=cost(27),
    )(q, *blocks, *first)


def attend_back_kernel(pairs, heads, groups, start, end, *refs):
    q_ref, own_ref, lse_ref = refs[:3]
    nb = 2 * pairs
    kv_refs = refs[3 : 3 + nb]
    at = 3 + nb
    if start:
        att_near_ref, att_far_ref, wo_ref, hf_ref = refs[at : at + 4]
        at += 4
    else:
        grad_in_ref, delta_in_ref, dq_in_ref = refs[at : at + 3]
        at += 3
    dkv_refs = refs[at : at + pairs]
    at += pairs
    if start:
        grad_ref, delta_ref = refs[at : at + 2]
        at += 2
    if end:
        dq_near_ref, dq_far_ref = refs[at : at + 2]
        at += 2
    else:
        dq_out_ref = refs[at]
        at += 1
    kv_s, q_s, do_s, delta_s, dq_s, dkv_s = refs[at:]
    tok = q_ref.shape[0]
    kvw = own_ref.shape[1] // 2
    if start:
        grad = jnp.concatenate(
            [
                lax.dot_general(ref[...], wo_ref[...], NT, preferred_element_type=F32)
                for ref in (att_near_ref, att_far_ref)
            ],
            axis=0,
        ).astype(BF)
        grad_ref[...] = grad
        prod = (grad.astype(F32) * hf_ref[...]).T
        for h in range(heads):
            delta_s[h : h + 1, :] = jnp.sum(prod[h * HD : (h + 1) * HD, :], axis=0, keepdims=True)
        delta_ref[...] = delta_s[...]
        dq_s[...] = jnp.zeros(dq_s.shape, F32)
    else:
        grad = grad_in_ref[...]
        delta_s[...] = delta_in_ref[...]
        dq_s[...] = dq_in_ref[...]
    for b in range(nb):
        kv_s[b] = kv_refs[b][...]
    for h in range(heads):
        q_s[h] = q_ref[:, h * HD : (h + 1) * HD]
        do_s[h] = grad[:, h * HD : (h + 1) * HD]
    own = jnp.concatenate(seg_rows_of(own_ref, tok), axis=1)
    own_hot = seg_onehot(own)
    own_lo = jnp.min(own)
    own_hi = jnp.max(own)

    def body(b, masked):
        block = kv_s[b]
        if masked:
            seg = jnp.concatenate(seg_rows_of(block, tok), axis=1)
            same = lax.dot_general(seg_onehot(seg), own_hot, TN, preferred_element_type=F32) > 0.5
        for n in range(heads // groups):
            k = block[:tok, n * HD : (n + 1) * HD]
            v = block[:tok, kvw + n * HD : kvw + (n + 1) * HD]
            dk = None
            for h in range(n * groups, (n + 1) * groups):
                s = lax.dot_general(k, q_s[h], NT, preferred_element_type=F32)
                p = jnp.exp(s - lse_ref[h : h + 1, :])
                if masked:
                    p = jnp.where(same, p, 0.0)
                dv_h = jnp.dot(p.astype(BF), do_s[h], preferred_element_type=F32)
                dp = lax.dot_general(v, do_s[h], NT, preferred_element_type=F32)
                ds = (p * (dp - delta_s[h : h + 1, :])).astype(BF)
                dk_h = jnp.dot(ds, q_s[h], preferred_element_type=F32)
                dq_s[h] += lax.dot_general(k, ds, TN, preferred_element_type=F32)
                dk = dk_h if dk is None else dk + dk_h
                dv = dv_h if h == n * groups else dv + dv_h
            dkv_s[b, :, n * HD : (n + 1) * HD] = dk.astype(BF)
            dkv_s[b, :, kvw + n * HD : kvw + (n + 1) * HD] = dv.astype(BF)

    def visit(b, carry):
        seg = jnp.concatenate(seg_rows_of(kv_s[b], tok), axis=1)
        lo = jnp.min(seg)
        hi = jnp.max(seg)
        plain = (lo == hi) & (own_lo == own_hi) & (lo == own_lo)
        touch = (lo <= own_hi) & (own_lo <= hi)

        @pl.when(plain)
        def _():
            body(b, False)

        @pl.when(touch & jnp.logical_not(plain))
        def _():
            body(b, True)

        @pl.when(jnp.logical_not(touch))
        def _():
            dkv_s[b] = jnp.zeros(dkv_s.shape[1:], BF)

        return carry

    lax.fori_loop(0, nb, visit, 0)
    for i in range(pairs):
        dkv_refs[i][...] = dkv_s[2 * i : 2 * i + 2]
    if end:
        out = jnp.concatenate([dq_s[h] for h in range(heads)], axis=0).T
        out = (out * HD ** (-0.5)).astype(BF)
        dq_near_ref[...] = out[: tok // 2]
        dq_far_ref[...] = out[tok // 2 :]
    else:
        dq_out_ref[...] = dq_s[...]


def attend_back(q, own, lse, blocks, heads, groups, start=None, going=None, end=True, first=()):
    tok = q.shape[0]
    nb = len(blocks)
    pairs = nb // 2
    width = heads * HD
    operands = [q, own, lse] + list(blocks) + list(start if start is not None else going)
    outs = [((2, tok, own.shape[1]), BF)] * pairs
    if start is not None:
        outs += [((tok, width), BF), ((8, tok), F32)]
    outs += [((tok // 2, width), BF)] * 2 if end else [((heads, HD, tok), F32)]
    kernel = functools.partial(
        attend_back_kernel, pairs, heads, groups, start is not None, end
    )
    return pl.pallas_call(
        drop_first(kernel, len(operands), len(first)),
        out_shape=tuple(jax.ShapeDtypeStruct(shape, dtype) for shape, dtype in outs),
        in_specs=vspec(len(operands)) + anywhere(len(first)),
        out_specs=tuple(vspec(len(outs))),
        scratch_shapes=[
            pltpu.VMEM((nb,) + blocks[0].shape, BF),
            pltpu.VMEM((heads, tok, HD), BF),
            pltpu.VMEM((heads, tok, HD), BF),
            pltpu.VMEM((8, tok), F32),
            pltpu.VMEM((heads, HD, tok), F32),
            pltpu.VMEM((nb, tok, own.shape[1]), BF),
        ],
        compiler_params=params(),
        name="attend_back",
        cost_estimate=cost(4.5 * nb),
    )(*operands, *first)


def experts_kernel(
    core_ref,
    ids_ref,
    mine_ref,
    theirs_ref,
    g_ref,
    wr_ref,
    wg_ref,
    wu_ref,
    wd_ref,
    mix_keep_ref,
    mix_send_ref,
    dx_keep_ref,
    dx_send_ref,
    gates_ref,
    ent_ref,
    a2_s,
    g_s,
    mix_s,
    dx_s,
    back_s,
):
    e = pl.program_id(0)
    tok, width = a2_s.shape
    half = tok // 2
    experts = wr_ref.shape[0]
    lane = lax.broadcasted_iota(jnp.int32, (tok, experts), 1)
    first = ids_ref[:, 0:1]
    second = ids_ref[:, 1:2]

    @pl.when(e == 0)
    def _():
        a2_s[:half, :] = mine_ref[...]
        a2_s[half:, :] = theirs_ref[...]
        for i in range(2):
            start = pl.multiple_of(((core_ref[0] + i) % 2) * half, half)
            g_s[pl.ds(i * half, half), :] = g_ref[pl.ds(start, half), :]
        logits = lax.dot_general(a2_s[...], wr_ref[...], NT, preferred_element_type=F32)
        one = jnp.sum(jnp.where(lane == first, logits, 0.0), axis=1, keepdims=True)
        two = jnp.sum(jnp.where(lane == second, logits, 0.0), axis=1, keepdims=True)
        top = jnp.maximum(one, two)
        one = jnp.exp(one - top)
        two = jnp.exp(two - top)
        total = one + two
        gates_ref[...] = jnp.where(lane == first, one / total, 0.0) + jnp.where(
            lane == second, two / total, 0.0
        )
        mix_s[...] = jnp.zeros(mix_s.shape, F32)
        dx_s[...] = jnp.zeros(dx_s.shape, F32)
        back_s[...] = jnp.zeros(back_s.shape, F32)
        ent_ref[...] = jnp.zeros(ent_ref.shape, BF)

    wg = wg_ref[0]
    wu = wu_ref[0]
    wd = wd_ref[0]
    for i in range(2):
        rows = pl.ds(i * half, half)
        a2 = a2_s[rows, :]
        u = jnp.dot(a2, wg, preferred_element_type=F32)
        w = jnp.dot(a2, wu, preferred_element_type=F32)
        m = lax.dot_general(g_s[rows, :], wd, NT, preferred_element_type=F32)
        here = lane[:half] == e
        gate = jnp.sum(jnp.where(here, gates_ref[rows, :], 0.0), axis=1, keepdims=True)
        pick_one = (ids_ref[rows, 0:1] == e).astype(F32)
        pick_two = (ids_ref[rows, 1:2] == e).astype(F32)
        sig = 1.0 / (1.0 + jnp.exp(-u))
        act = u * sig
        mid = (act * w).astype(BF).astype(F32)
        back = jnp.sum(mid * m, axis=1, keepdims=True) * (pick_one + pick_two)
        back_s[rows, :] += jnp.where(here, back, 0.0)
        mid = mid * gate
        gm = gate * m
        up_back = gm * act
        pre_back = gm * w * sig * (1.0 + u * (1.0 - sig))
        mid_b = mid.astype(BF)
        up_b = up_back.astype(BF)
        pre_b = pre_back.astype(BF)
        mix_s[rows, :] += jnp.dot(mid_b, wd, preferred_element_type=F32)
        dx_s[rows, :] += lax.dot_general(
            pre_b, wg, NT, preferred_element_type=F32
        ) + lax.dot_general(up_b, wu, NT, preferred_element_type=F32)
        for kind, value in enumerate((mid, pre_back, up_back)):
            for c, pick in enumerate((pick_one, pick_two)):
                ent_ref[2 * kind + c, rows, :] += (value * pick).astype(BF)

    @pl.when(e == pl.num_programs(0) - 1)
    def _():
        mix_keep_ref[...] = mix_s[:half, :]
        mix_send_ref[...] = mix_s[half:, :].astype(BF)
        dx_keep_ref[:, :width] = dx_s[:half, :]
        dx_send_ref[:, :width] = dx_s[half:, :].astype(BF)
        pad = jnp.zeros((half, 128 - experts), F32)
        dx_keep_ref[:, width:] = jnp.concatenate([back_s[:half, :], pad], axis=1)
        dx_send_ref[:, width:] = jnp.concatenate([back_s[half:, :], pad], axis=1).astype(BF)


def experts_call(core, ids, mine, theirs, g, wr, wg, wu, wd, first=()):
    half, width = mine.shape
    tok = 2 * half
    experts, _, hidden = wg.shape

    def whole(*shape):
        return pl.BlockSpec(shape, lambda e, *_: (0,) * len(shape))

    def one(*shape):
        return pl.BlockSpec((1,) + shape, lambda e, *_: (e,) + (0,) * len(shape))

    return pl.pallas_call(
        drop_first(experts_kernel, 9, len(first)),
        out_shape=(
            jax.ShapeDtypeStruct((half, width), F32),
            jax.ShapeDtypeStruct((half, width), BF),
            jax.ShapeDtypeStruct((half, width + 128), F32),
            jax.ShapeDtypeStruct((half, width + 128), BF),
            jax.ShapeDtypeStruct((tok, experts), F32),
            jax.ShapeDtypeStruct((6, tok, hidden), BF),
        ),
        grid=(experts,),
        in_specs=[
            pl.BlockSpec(memory_space=pltpu.SMEM),
            whole(tok, 2),
            whole(half, width),
            whole(half, width),
            whole(tok, width),
            whole(experts, width),
            one(width, hidden),
            one(width, hidden),
            one(hidden, width),
        ]
        + anywhere(len(first)),
        out_specs=(
            whole(half, width),
            whole(half, width),
            whole(half, width + 128),
            whole(half, width + 128),
            whole(tok, experts),
            whole(6, tok, hidden),
        ),
        scratch_shapes=[
            pltpu.VMEM((tok, width), BF),
            pltpu.VMEM((tok, width), BF),
            pltpu.VMEM((tok, width), F32),
            pltpu.VMEM((tok, width), F32),
            pltpu.VMEM((tok, experts), F32),
        ],
        compiler_params=params(dimension_semantics=("arbitrary",)),
        name="experts",
        cost_estimate=cost(32),
    )(core, ids, mine, theirs, g, wr, wg, wu, wd, *first)


def expert_grads_kernel(at, count, seeded, ids_ref, *refs):
    x_refs = refs[0:2]
    g_refs = refs[2:4]
    ents = refs[4 : 4 + count]
    prev = refs[4 + count : 7 + count] if seeded else None
    outs = refs[-3:]
    e = pl.program_id(0)
    sums = [None, None, None]
    for b in range(count):
        half = x_refs[0].shape[2]
        hidden = ents[b].shape[2]
        for i in range(2):
            rows = pl.ds(i * half, half)
            one = jnp.where(ids_ref[at + b, rows, 0:1] == e, 1.0, 0.0).astype(BF)
            two = jnp.where(ids_ref[at + b, rows, 1:2] == e, 1.0, 0.0).astype(BF)
            one = jnp.broadcast_to(one, (half, hidden))
            two = jnp.broadcast_to(two, (half, hidden))
            xt = x_refs[i][at + b]
            gt = g_refs[i][at + b]
            for kind in range(3):
                value = ents[b][2 * kind, rows, :] * one + ents[b][2 * kind + 1, rows, :] * two
                term = jnp.dot(gt if kind == 0 else xt, value, preferred_element_type=F32)
                sums[kind] = term if sums[kind] is None else sums[kind] + term
    for kind in range(3):
        outs[kind][0] = sums[kind] + prev[kind][0] if seeded else sums[kind]


def expert_grads(at, ids, xm, xo, gm, go, ents, experts, prev=None):
    cols = xm.shape[1]
    hidden = ents[0].shape[-1]
    operands = [ids, xm, xo, gm, go] + list(ents)
    specs = [pl.BlockSpec(x.shape, lambda e, nd=x.ndim: (0,) * nd) for x in operands]
    out_spec = pl.BlockSpec((1, cols, hidden), lambda e: (e, 0, 0))
    if prev is not None:
        operands += list(prev)
        specs += [out_spec] * 3
    return pl.pallas_call(
        functools.partial(expert_grads_kernel, at, len(ents), prev is not None),
        out_shape=(jax.ShapeDtypeStruct((experts, cols, hidden), F32),) * 3,
        grid=(experts,),
        in_specs=specs,
        out_specs=(out_spec,) * 3,
        compiler_params=params(dimension_semantics=("arbitrary",)),
        name="expert_grads",
        cost_estimate=cost(3.5 * len(ents)),
    )(*operands)


def my_rows(core_ref, ref):
    half = ref.shape[0] // 2
    return ref[pl.ds(pl.multiple_of(core_ref[0] * half, half), half), :]


def simple(kernel, name, outs, core, *operands, first=()):
    return pl.pallas_call(
        drop_first(kernel, 1 + len(operands), len(first)),
        out_shape=tuple(jax.ShapeDtypeStruct(shape, dtype) for shape, dtype in outs),
        in_specs=[pl.BlockSpec(memory_space=pltpu.SMEM)] + vspec(len(operands)) + anywhere(len(first)),
        out_specs=tuple(vspec(len(outs))),
        compiler_params=params(),
        name=name,
        cost_estimate=cost(5),
    )(core, *operands, *first)


def middle_kernel(core_ref, x_ref, gain_ref, *refs):
    parts, weights = refs[:4], refs[4:8]
    hidden_ref, a2_ref = refs[8:]
    total = my_rows(core_ref, x_ref).astype(F32)
    for part, weight in zip(parts, weights):
        total = total + jnp.dot(part[...], weight[...], preferred_element_type=F32)
    inv = lax.rsqrt(jnp.mean(total * total, axis=-1, keepdims=True) + eps)
    hidden_ref[...] = total
    a2_ref[...] = (total * inv * gain_ref[...][None, :]).astype(BF)


def back_kernel(
    core_ref,
    near_ref,
    got_ref,
    hidden_ref,
    a2_ref,
    gates_ref,
    ids_ref,
    wr_ref,
    gain_ref,
    g_ref,
    grad_ref,
    att_ref,
    misc_ref,
):
    half, width = hidden_ref.shape
    experts = wr_ref.shape[0]
    total = near_ref[...].astype(F32) + got_ref[...].astype(F32)
    gate_back = total[:, width:][:, :experts]
    gates = gates_ref[:half, :]
    lane = lax.broadcasted_iota(jnp.int32, (half, experts), 1)
    picked = (lane == ids_ref[:half, 0:1]) | (lane == ids_ref[:half, 1:2])
    logit = gates * (gate_back - jnp.sum(gates * gate_back, axis=-1, keepdims=True))
    logit = jnp.where(picked, logit, 0.0).astype(BF)
    back = total[:, :width] + jnp.dot(logit, wr_ref[...], preferred_element_type=F32)
    hidden = hidden_ref[...]
    inv = lax.rsqrt(jnp.mean(hidden * hidden, axis=-1, keepdims=True) + eps)
    upstream = my_rows(core_ref, g_ref).astype(F32)
    scaled = back * gain_ref[...][None, :]
    grad = upstream + inv * (
        scaled - hidden * inv * inv * jnp.mean(scaled * hidden, axis=-1, keepdims=True)
    )
    grad_ref[...] = grad
    att_ref[...] = grad.astype(BF)
    misc_ref[:8, :] = lax.dot_general(logit, a2_ref[...], TN, preferred_element_type=F32)
    ffn = jnp.sum(back * hidden * inv, axis=0, keepdims=True)
    misc_ref[8:, :] = jnp.broadcast_to(ffn, (8, width))


def query_back_kernel(core_ref, *refs):
    parts, weights, out_ref = refs[:4], refs[4:8], refs[8]
    total = None
    for part, weight in zip(parts, weights):
        term = lax.dot_general(
            part[...], weight[:, : part.shape[1]], NT, preferred_element_type=F32
        )
        total = term if total is None else total + term
    out_ref[...] = total


def input_kernel(core_ref, x_ref, gain_ref, grad_ref, query_ref, *refs):
    parts, weights = refs[:4], refs[4:8]
    out_ref, norm_ref = refs[8:]
    back = query_ref[...]
    for part, weight in zip(parts, weights):
        start = weight.shape[1] - part.shape[1]
        back = back + lax.dot_general(
            part[...], weight[:, start:], NT, preferred_element_type=F32
        )
    x = my_rows(core_ref, x_ref).astype(F32)
    inv = lax.rsqrt(jnp.mean(x * x, axis=-1, keepdims=True) + eps)
    scaled = back * gain_ref[...][None, :]
    out_ref[...] = grad_ref[...] + inv * (
        scaled - x * inv * inv * jnp.mean(scaled * x, axis=-1, keepdims=True)
    )
    norm = jnp.sum(back * x * inv, axis=0, keepdims=True)
    norm_ref[...] = jnp.broadcast_to(norm, norm_ref.shape)


def place_kernel(core_ref, mine_ref, theirs_ref, out_ref):
    half = mine_ref.shape[0]
    out_ref[pl.ds(pl.multiple_of(core_ref[0] * half, half), half), :] = mine_ref[...]
    out_ref[pl.ds(pl.multiple_of((1 - core_ref[0]) * half, half), half), :] = theirs_ref[...]


def columns_kernel(waits, owner_ref, core_ref, x_ref, *refs):
    outs, turned = refs[waits:-1], refs[-1]
    per, cols, half = outs[0].shape
    x = my_rows(core_ref, x_ref) if x_ref.shape[0] != half else x_ref[...]
    turned[...] = x.T
    for r, out_ref in enumerate(outs):
        for i in range(per):
            rows = pl.ds(pl.multiple_of(owner_ref[r * per + i] * cols, 16), cols)
            out_ref[i] = turned[rows, :]


def columns(owner, core, x, half, groups, first=()):
    n = owner.shape[0]
    width = x.shape[1]
    smem = pl.BlockSpec(memory_space=pltpu.SMEM)
    out = jax.ShapeDtypeStruct((n // groups, width // n, half), BF)
    return pl.pallas_call(
        functools.partial(columns_kernel, len(first)),
        out_shape=(out,) * groups,
        in_specs=[smem, smem] + vspec(1) + [pl.BlockSpec(memory_space=pl.ANY)] * len(first),
        out_specs=tuple(vspec(groups)),
        scratch_shapes=[pltpu.VMEM((width, half), BF)],
        compiler_params=params(),
        name="columns",
        cost_estimate=cost(2.5),
    )(owner, core, x, *first)


def weight_kernel(shape, extra, owner_ref, *refs):
    out_ref, turned, misc_turned = refs[-3:]
    n, cols, _ = out_ref.shape
    at = 0
    column = 0
    for group, pairs in enumerate(shape):
        lefts, rights = refs[at : at + pairs], refs[at + pairs : at + 2 * pairs]
        at += 2 * pairs
        row = 0
        for left in lefts:
            turned[group, :, row : row + left.shape[0]] = left[...].T
            row += left.shape[0]
        right = jnp.concatenate([r[...] for r in rights], axis=0) if pairs > 1 else rights[0][...]
        for i in range(n):
            rows = pl.ds(pl.multiple_of(owner_ref[i] * cols, 16), cols)
            out_ref[i, :, column : column + right.shape[1]] = jnp.dot(
                turned[group, rows, :], right, preferred_element_type=F32
            ).astype(BF)
        column += right.shape[1]
    if extra:
        misc = refs[at][...]
        spare = jnp.zeros((128 - misc.shape[0], misc.shape[1]), F32)
        misc_turned[...] = jnp.concatenate([misc, spare], axis=0).T
        for i in range(n):
            rows = pl.ds(pl.multiple_of(owner_ref[i] * cols, 16), cols)
            out_ref[i, :, column:] = misc_turned[rows, :].astype(BF)


def weight_terms(owner, groups, misc=None, us=4, first=()):
    n = owner.shape[0]
    width = groups[0][0][0].shape[1]
    rows = sum(x.shape[0] for x in groups[0][0])
    out_width = sum(rights[0].shape[1] for _, rights in groups)
    operands = []
    for lefts, rights in groups:
        operands += list(lefts) + list(rights)
    if misc is not None:
        operands.append(misc)
        out_width += 128
    shape = tuple(len(lefts) for lefts, _ in groups)
    return pl.pallas_call(
        drop_first(
            functools.partial(weight_kernel, shape, misc is not None),
            1 + len(operands),
            len(first),
        ),
        out_shape=jax.ShapeDtypeStruct((n, width // n, out_width), BF),
        in_specs=[pl.BlockSpec(memory_space=pltpu.SMEM)]
        + vspec(len(operands))
        + anywhere(len(first)),
        out_specs=vspec(1)[0],
        scratch_shapes=[pltpu.VMEM((len(groups), width, rows), BF), pltpu.VMEM((width, 128), F32)],
        compiler_params=params(),
        name="weight_terms",
        cost_estimate=cost(us),
    )(owner, *operands, *first)


def per_device(
    n_ctx,
    layer_input,
    segment_ids,
    expert_ids,
    norm_gain,
    query_weight,
    key_weight,
    value_weight,
    output_weight,
    ffn_gain,
    router_weight,
    gate_weight,
    up_weight,
    down_weight,
    cotangent,
):
    tok, width = layer_input.shape
    half = tok // 2
    groups = H // KV
    kv_local = key_weight.shape[1] // HD
    heads = kv_local * groups
    kvw = key_weight.shape[1]
    experts = gate_weight.shape[0]
    cols = width // n_ctx
    digits = digits_of(n_ctx)
    keys = rel_keys(digits)
    upper_first = list(range(1, len(digits))) + [0]
    lower_first = list(range(len(digits)))
    me = lax.axis_index("ctx")
    core = lax.axis_index("wa") % 2
    core_arr = jnp.full((1,), core, jnp.int32)
    owner_to = jnp.stack([digit_offset(me, k, digits, 1) for k in keys]).astype(jnp.int32)
    owner_from = jnp.stack([digit_offset(me, k, digits, -1) for k in keys]).astype(jnp.int32)
    gain_one, gain_two = norm_gain, ffn_gain
    router = router_weight.T

    def mine_first(x):
        return jnp.where(core == 0, x, jnp.concatenate([x[half:], x[:half]], axis=0))

    segs = mine_first(segment_ids).astype(BF)
    ids = mine_first(expert_ids)
    extra = jnp.concatenate([segs, ids[:, 0].astype(BF), ids[:, 1].astype(BF)])
    extra = jnp.pad(extra, (0, EXTRA * 2 * kvw - extra.shape[0])).reshape(EXTRA, 2 * kvw)
    a1, q, kv = project(
        core_arr, layer_input, gain_one, query_weight, key_weight, value_weight, extra
    )
    tops = digits[-1][1]
    staged = n_ctx == 8
    low, top = digits[0], digits[-1]
    turned_digits = digits[1:] + digits[:1]
    turned_keys = [(k[-1],) + k[:-1] for k in rel_keys(turned_digits)]
    owner_turned = jnp.stack(
        [digit_offset(me, k, digits, -1) for k in turned_keys]
    ).astype(jnp.int32)

    wo_chip = other_chip(output_weight)
    kv_weight = jnp.concatenate([key_weight, value_weight], axis=1)
    g_out = columns(owner_to, core_arr, cotangent, half, tops, [kv])
    if staged:
        z, y = [kv], []
        for r in range(tops - 1):
            aside = [g_out[0], kv_weight] if r == tops - 2 else []
            z_next, y_next = tie([hop(z[r], n_ctx, top), hop(z[r], n_ctx, low)], aside)
            z.append(z_next)
            y.append(y_next)
        y.append(hop(z[-1], n_ctx, low))
        kv_list = [block for pair in zip(z, y) for block in pair]
    else:
        kv_blocks = gather_ctx(kv, n_ctx, digits, upper_first)
        kv_list = [kv_blocks[k] for k in keys]

    g_top = exchange_top(g_out, n_ctx, digits)

    heads_f32, heads_near, heads_far, lse = attend(
        q, kv_list, heads, groups, first=[g_out[0]]
    )
    heads_near, heads_far, wo_chip, *rest = tie(
        [heads_near, heads_far, wo_chip] + list(g_top[1:]), []
    )
    g_top = [g_top[0]] + list(rest)
    wo_parts = [output_weight, other_core(output_weight), wo_chip, other_core(wo_chip)]

    parts = all_parts(heads_near, heads_far)
    g_pieces = exchange_rest(g_top, n_ctx, digits)
    hidden_one, a2_mine = simple(
        middle_kernel,
        "middle",
        [((half, width), F32), ((half, width), BF)],
        core_arr,
        layer_input,
        gain_two,
        *parts,
        *wo_parts,
    )
    a2_far = other_core(a2_mine)
    a2_out = columns(owner_to, core_arr, a2_mine, half, tops)
    a2_top = exchange_top(a2_out, n_ctx, digits)
    wq_chip = other_chip(query_weight)

    mix_keep, mix_send, dx_keep, dx_send, gates, ent = experts_call(
        core_arr,
        ids,
        a2_mine,
        a2_far,
        cotangent,
        router,
        gate_weight,
        up_weight,
        down_weight,
        first=[a2_out[0]],
    )
    dx_send, wq_chip, *rest = tie(
        [dx_send, wq_chip] + list(a2_top[1:]), [array for array, _ in g_pieces]
    )
    a2_top = [a2_top[0]] + list(rest)

    near = (dx_keep + other_core(dx_send).astype(F32)).astype(BF)
    got = other_chip(near)
    if staged:
        z_next, y_next = hop(ent, n_ctx, top), hop(ent, n_ctx, low)
        z, y = [ent], []
    hidden_grad, att_near, misc = simple(
        back_kernel,
        "back",
        [((half, width), F32), ((half, width), BF), ((16, width), F32)],
        core_arr,
        near,
        got,
        hidden_one,
        a2_mine,
        gates,
        ids,
        router,
        gain_two,
        cotangent,
    )
    att_far = other_core(att_near)
    (mix_send,) = tie([mix_send], [got])
    mix_near = (mix_keep + other_core(mix_send).astype(F32)).astype(BF)
    mix_got = other_chip(mix_near)
    wq_parts = [query_weight, other_core(query_weight), wq_chip, other_core(wq_chip)]
    a2_pieces = exchange_rest(a2_top, n_ctx, digits)
    if staged:
        z_next, y_next = tie([z_next, y_next], [att_near])
        z.append(z_next)
        y.append(y_next)
        z_next, y_next = hop(z[1], n_ctx, top), hop(z[1], n_ctx, low)

    begin = [att_near, att_far, output_weight, heads_f32]
    if staged:
        dkv_1, dkv_2, dkv_3, head_grad, delta, dq_going = attend_back(
            q,
            kv_list[0],
            lse,
            kv_list[2:8],
            heads,
            groups,
            start=begin,
            end=False,
            first=[z[1], y[0], mix_near],
        )
        z_next, y_next = tie([z_next, y_next], [dq_going])
        z.append(z_next)
        y.append(y_next)
        z_next, y_next = hop(z[2], n_ctx, top), hop(z[2], n_ctx, low)
        dkv_0, dq_near, dq_far = attend_back(
            q,
            kv_list[0],
            lse,
            kv_list[0:2],
            heads,
            groups,
            going=[head_grad, delta, dq_going],
            first=[z[2], y[1]] + [array for array, _ in a2_pieces],
        )
        dkv = [dkv_0, dkv_1, dkv_2, dkv_3]
    else:
        *dkv, head_grad, delta, dq_near, dq_far = attend_back(
            q, kv_list[0], lse, kv_list, heads, groups, start=begin
        )
        dkv = jnp.concatenate(dkv, axis=0)
    (mix_got,) = tie([mix_got], [dq_near])
    a2_stack, a2_stack_far = swapped(a2_pieces, [dq_near])
    g_stack, g_far = swapped(g_pieces, [dq_near])
    out_mine = hidden_one + mix_near.astype(F32) + mix_got.astype(F32)
    (layer_output,) = simple(
        place_kernel, "place", [((tok, width), F32)], core_arr, out_mine, other_core(out_mine)
    )

    terms = weight_terms(
        owner_from,
        [
            ([att_near, att_far], [heads_near, heads_far]),
            ([a1], [jnp.concatenate([dq_near, dq_far], axis=0)]),
        ],
        misc,
        6,
    )
    used = tok // (2 * kvw)
    ids_rows = jnp.stack(
        [b[tok + used : tok + 3 * used].astype(jnp.int32).reshape(2, tok) for b in kv_list], 0
    )
    ids_all = jnp.swapaxes(ids_rows, 1, 2)
    shared = [ids_all, a2_stack, a2_stack_far, g_stack, g_far]
    dq_parts = all_parts(dq_near, dq_far)
    (query_back,) = simple(
        query_back_kernel, "query_back", [((half, width), F32)], core_arr, *dq_parts, *wq_parts
    )
    if staged:
        sums = expert_grads(0, *shared, [z[0], y[0], z[1], y[1]], experts)
        z_next, y_next = tie([z_next, y_next], [sums[0]])
        z.append(z_next)
        y.append(y_next)
        waits = [[dq_near], [terms], [sums[0]], [query_back]]
        dkv_own = scatter_ctx(
            dkv, n_ctx, digits, add_bf, lambda at, x: tie([x], waits[at])[0]
        )
    else:
        dkv_own = scatter_ctx(dkv, n_ctx, digits, add_bf)

    (terms,) = tie([terms], [dkv_own])

    kv_chip = other_chip(kv_weight)
    (kv_chip,) = tie([kv_chip], [query_back])
    kv_weights = [kv_weight, other_core(kv_weight), kv_chip, other_core(kv_chip)]

    late = weight_terms(owner_turned, [([a1], [dkv_own])])
    dkv_parts = all_parts(dkv_own[:half], dkv_own[half:])
    in_mine, norm_row = simple(
        input_kernel,
        "input",
        [((half, width), F32), ((8, width), F32)],
        core_arr,
        layer_input,
        gain_one,
        hidden_grad,
        query_back,
        *dkv_parts,
        *kv_weights,
    )
    norm_rel = norm_row[0].reshape(n_ctx, cols)[owner_turned]
    in_far = other_core(in_mine)

    if staged:
        y.append(hop(tie([z[3]], [late])[0], n_ctx, low))
        sums = expert_grads(4, *shared, [z[2], y[2], z[3], y[3]], experts, sums)
        waits = [[late], [in_mine], [sums[0]], []]
        terms_own = scatter_ctx(
            terms, n_ctx, digits, add_bf, lambda at, x: tie([x], waits[at])[0]
        )
        waits = [[in_mine], [sums[0]], [], []]
        late_own = scatter_ctx(
            late, n_ctx, turned_digits, add_bf, lambda at, x: tie([x], waits[at])[0]
        )
    else:
        terms_own = scatter_ctx(terms, n_ctx, digits, add_bf)
        late_own = scatter_ctx(late, n_ctx, turned_digits, add_bf)
        ents = gather_ctx(ent, n_ctx, digits, upper_first)
        sums = None
        for at in range(0, n_ctx, 4):
            some = range(at, min(at + 4, n_ctx))
            sums = expert_grads(at, *shared, [ents[keys[i]] for i in some], experts, sums)
    (input_grad,) = simple(
        place_kernel, "place", [((tok, width), F32)], core_arr, in_mine, in_far
    )
    norm_own = scatter_ctx(norm_rel, n_ctx, turned_digits, jnp.add)
    terms_own = terms_own.astype(F32)
    late_own = late_own.astype(F32)
    down_grad, gate_grad, up_grad = sums
    down_grad = jnp.swapaxes(down_grad, 1, 2)

    qw = heads * HD
    output_grad = terms_own[:, :qw].T
    query_grad = terms_own[:, qw : 2 * qw]
    small = jnp.concatenate([terms_own[:, 2 * qw : 2 * qw + experts + 1], norm_own[:, None]], axis=1)
    small = small + other_core(small)
    return (
        layer_output,
        input_grad,
        small[:, experts + 1],
        query_grad,
        late_own[:, :kvw],
        late_own[:, kvw:],
        output_grad,
        small[:, experts],
        small[:, :experts],
        gate_grad,
        up_grad,
        down_grad,
    )


def solution(mesh):
    in_specs = (
        P("ctx", None),
        P("ctx"),
        P("ctx", None),
        P(),
        P(None, "wa"),
        P(None, "wa"),
        P(None, "wa"),
        P("wa", None),
        P(),
        P(),
        P(None, None, "wa"),
        P(None, None, "wa"),
        P(None, "wa", None),
        P("ctx", None),
    )
    out_specs = (
        P("ctx", None),
        P("ctx", None),
        P("ctx"),
        P("ctx", "wa"),
        P("ctx", "wa"),
        P("ctx", "wa"),
        P("wa", "ctx"),
        P("ctx"),
        P("ctx", None),
        P(None, "ctx", "wa"),
        P(None, "ctx", "wa"),
        P(None, "wa", "ctx"),
    )
    return jax.shard_map(
        functools.partial(per_device, mesh.shape["ctx"]),
        mesh=mesh,
        in_specs=in_specs,
        out_specs=out_specs,
        check_vma=False,
    )
```

```python
import functools

import jax
import jax.numpy as jnp
from jax import lax
from jax.experimental import pallas as pl
from jax.experimental.pallas import tpu as pltpu
from jax.sharding import PartitionSpec as P

H = 24
KV = 8
HD = 64
eps = 1e-05
NEG = -1e30
F32 = jnp.float32
BF = jnp.bfloat16
VLIM = 60 * 1024 * 1024
EXTRA = 16
NT = (((1,), (1,)), ((), ()))
TN = (((0,), (0,)), ((), ()))


def digits_of(n):
    out = []
    stride = 1
    while n > 1:
        if stride == 1 and n % 2 == 0:
            radix = 2
        elif n % 4 == 0:
            radix = 4
        else:
            radix = n
        out.append((stride, radix))
        stride *= radix
        n //= radix
    return out


def moved(n, digit, shift):
    stride, radix = digit
    pairs = []
    for i in range(n):
        d = (i // stride) % radix
        pairs.append((i, i + ((d + shift) % radix - d) * stride))
    return pairs


def hop(x, n, digit, shift=1):
    return lax.ppermute(x, "ctx", moved(n, digit, shift))


def other_core(x):
    return lax.ppermute(x, "wa", [(i, i ^ 1) for i in range(4)])


def other_chip(x):
    return lax.ppermute(x, "wa", [(i, i ^ 2) for i in range(4)])


def rel_keys(digits):
    keys = [()]
    for _, radix in digits:
        keys = [k + (r,) for r in range(radix) for k in keys]
    return keys


def set_digit(key, at, value):
    return key[:at] + (value,) + key[at + 1 :]


def gather_ctx(x, n, digits, order):
    blocks = {tuple(0 for _ in digits): x}
    for at in order:
        fresh = {}
        for key, block in blocks.items():
            moving = block
            for s in range(1, digits[at][1]):
                moving = hop(moving, n, digits[at])
                fresh[set_digit(key, at, s)] = moving
        blocks.update(fresh)
    return blocks


def scatter_sends(blocks, n, digit):
    return [blocks[0]] + [hop(blocks[r], n, digit, -r) for r in range(1, len(blocks))]


def total(parts):
    return functools.reduce(jnp.add, [x.astype(F32) for x in parts])


def cut(stack, radix):
    per = stack.shape[0] // radix
    return [stack[r * per : (r + 1) * per] for r in range(radix)]


def scatter_ctx(stack, n, order, hold=lambda at, xs: xs, kind=BF):
    moving = stack
    for at in reversed(range(len(order))):
        parts = scatter_sends(cut(moving, order[at][1]), n, order[at])
        parts = parts[:1] + list(hold(at, parts[1:]))
        moving = total(parts)
        if at:
            moving = moving.astype(kind)
    return moving[0]


def stack_kernel(places, *refs):
    for i, (at, unit) in enumerate(places):
        refs[-1][i] = refs[at][unit]


def stacked(pieces):
    arrays = []
    places = []
    for array, unit in pieces:
        at = next((i for i, x in enumerate(arrays) if x is array), None)
        if at is None:
            at = len(arrays)
            arrays.append(array)
        places.append((at, unit))
    shape = (len(pieces),) + arrays[0].shape[1:]
    return pl.pallas_call(
        functools.partial(stack_kernel, tuple(places)),
        out_shape=jax.ShapeDtypeStruct(shape, arrays[0].dtype),
        in_specs=vspec(len(arrays)),
        out_specs=vspec(1)[0],
        compiler_params=params(),
        name="stacked",
        cost_estimate=cost(1),
    )(*arrays)


def exchange_top(groups, n, digits):
    return [groups[0]] + [hop(groups[r], n, digits[-1], r) for r in range(1, len(groups))]


def exchange_rest(groups, n, digits):
    keys = rel_keys(digits[1:])
    n_up = len(keys)
    per = n_up // len(groups)
    parts = {i: (groups[i // per], i % per) for i in range(n_up)}
    for at in reversed(range(1, len(digits) - 1)):
        for s in range(1, digits[at][1]):
            chosen = [i for i, k in enumerate(keys) if k[at - 1] == s]
            bundle = hop(stacked([parts[i] for i in chosen]), n, digits[at], s)
            for place, i in enumerate(chosen):
                parts[i] = (bundle, place)
    return [parts[i] for i in range(n_up)]


def swapped(pieces, first):
    arrays = []
    for array, _ in pieces:
        if not any(array is x for x in arrays):
            arrays.append(array)
    held = tie(arrays, first)
    pieces = [(held[next(i for i, x in enumerate(arrays) if x is a)], u) for a, u in pieces]
    near = stacked(pieces)
    return near, other_core(near)


def digit_offset(me, key, digits, sign):
    place = 0
    for (stride, radix), r in zip(digits, key):
        d = (me // stride) % radix
        place = place + ((d + sign * r) % radix) * stride
    return place


def tie_kernel(*refs):
    pass


def tie(xs, first):
    xs, first = list(xs), list(first)
    return pl.pallas_call(
        tie_kernel,
        out_shape=tuple(jax.ShapeDtypeStruct(x.shape, x.dtype) for x in xs),
        in_specs=anywhere(len(xs) + len(first)),
        out_specs=tuple(anywhere(len(xs))),
        input_output_aliases={i: i for i in range(len(xs))},
        name="tie",
    )(*xs, *first)


def diagonal(x):
    return lax.ppermute(x, "wa", [(i, i ^ 3) for i in range(4)])


def all_parts(near, far):
    return [near, other_core(far), other_chip(near), diagonal(far)]


def cost(us):
    return pl.CostEstimate(flops=int(us * 3e8), bytes_accessed=int(us * 9e5), transcendentals=0)


def params(**kw):
    return pltpu.CompilerParams(vmem_limit_bytes=VLIM, **kw)


def vspec(n):
    return [pl.BlockSpec(memory_space=pltpu.VMEM)] * n


def drop_first(kernel, at, count):
    if not count:
        return kernel

    def waiting(*refs):
        kernel(*refs[:at], *refs[at + count :])

    return waiting


def anywhere(count):
    return [pl.BlockSpec(memory_space=pl.ANY)] * count


def project_kernel(core_ref, x_ref, gain_ref, wq_ref, wk_ref, wv_ref, extra_ref, a1_ref, q_ref, kv_ref):
    tok = x_ref.shape[0]
    half = tok // 2
    kvw = wk_ref.shape[1]
    for i in range(2):
        start = pl.multiple_of(((core_ref[0] + i) % 2) * half, half)
        x = x_ref[pl.ds(start, half), :].astype(F32)
        inv = lax.rsqrt(jnp.mean(x * x, axis=-1, keepdims=True) + eps)
        a1 = (x * inv * gain_ref[...][None, :]).astype(BF)
        rows = pl.ds(i * half, half)
        a1_ref[rows, :] = a1
        kv_ref[rows, :kvw] = jnp.dot(a1, wk_ref[...], preferred_element_type=F32).astype(BF)
        kv_ref[rows, kvw:] = jnp.dot(a1, wv_ref[...], preferred_element_type=F32).astype(BF)
        q = jnp.dot(a1, wq_ref[...], preferred_element_type=F32).astype(BF)
        q_ref[rows, :] = (q.astype(F32) * HD ** (-0.5)).astype(BF)
    kv_ref[pl.ds(tok, EXTRA), :] = extra_ref[...]


def project(core, x, gain, wq, wk, wv, extra):
    tok, width = x.shape
    return pl.pallas_call(
        project_kernel,
        out_shape=(
            jax.ShapeDtypeStruct((tok, width), BF),
            jax.ShapeDtypeStruct((tok, wq.shape[1]), BF),
            jax.ShapeDtypeStruct((tok + EXTRA, 2 * wk.shape[1]), BF),
        ),
        in_specs=[pl.BlockSpec(memory_space=pltpu.SMEM)] + vspec(6),
        out_specs=tuple(vspec(3)),
        compiler_params=params(),
        name="project",
        cost_estimate=cost(5),
    )(core, x, gain, wq, wk, wv, extra)


def seg_onehot(row):
    lane = lax.broadcasted_iota(jnp.int32, (16, row.shape[1]), 0).astype(F32)
    return jnp.where(lane == row, 1.0, 0.0).astype(BF)


def seg_rows_of(block, tok):
    width = block.shape[1]
    return [
        block[tok : tok + EXTRA, :].astype(F32)[i : i + 1, :] for i in range(tok // width)
    ]


ROWS = 256


def block_segs(block, tok):
    return jnp.concatenate(seg_rows_of(block, tok), axis=1)


def turned_groups(x, out, heads, groups):
    x = x.astype(F32).T.astype(BF)
    pairs = heads // groups
    for r in range(x.shape[1] // ROWS):
        for h in range(heads):
            n, g = h // groups, h % groups
            out[r * pairs + n, :, g * ROWS : (g + 1) * ROWS] = x[
                h * HD : (h + 1) * HD, r * ROWS : (r + 1) * ROWS
            ]


def straight_groups(x, out, heads, groups):
    pairs = heads // groups
    for r in range(x.shape[0] // ROWS):
        for h in range(heads):
            n, g = h // groups, h % groups
            out[r * pairs + n, g * ROWS : (g + 1) * ROWS, :] = x[
                r * ROWS : (r + 1) * ROWS, h * HD : (h + 1) * HD
            ]


def head_rows(ref, r, n, groups):
    rows = slice(r * ROWS, (r + 1) * ROWS)
    return jnp.concatenate(
        [ref[h : h + 1, rows] for h in range(n * groups, (n + 1) * groups)], axis=1
    )


def visit_tiles(kv_s, own, tok, body, before, behind):
    tiles = tok // ROWS
    lows = [jnp.min(own[:, r * ROWS : (r + 1) * ROWS]) for r in range(tiles)]
    highs = [jnp.max(own[:, r * ROWS : (r + 1) * ROWS]) for r in range(tiles)]

    def visit(b, carry):
        seg = block_segs(kv_s[b], tok)
        lo = jnp.min(seg)
        hi = jnp.max(seg)
        before(b)
        for r in range(tiles):
            plain = (lo == hi) & (lows[r] == highs[r]) & (lo == lows[r])
            touch = (lo <= highs[r]) & (lows[r] <= hi)
            pl.when(plain)(functools.partial(body, b, r, False))
            pl.when(touch & jnp.logical_not(plain))(functools.partial(body, b, r, True))
        behind(b)
        return carry

    lax.fori_loop(0, kv_s.shape[0], visit, 0)


def same_tile(block, own_hot, r, tok, groups):
    same = lax.dot_general(
        seg_onehot(block_segs(block, tok)),
        own_hot[:, r * ROWS : (r + 1) * ROWS],
        TN,
        preferred_element_type=F32,
    )
    return jnp.concatenate([same] * groups, axis=1) > 0.5


def attend_kernel(nb, heads, groups, *refs):
    q_ref = refs[0]
    kv_refs = refs[1 : 1 + nb]
    hf_ref, near_ref, far_ref, lse_ref = refs[1 + nb : 5 + nb]
    kv_s, q_s, m_s, acc_s = refs[5 + nb :]
    tok = q_ref.shape[0]
    kvw = kv_refs[0].shape[1] // 2
    pairs = heads // groups
    for b in range(nb):
        kv_s[b] = kv_refs[b][...]
    turned_groups(q_ref[...], q_s, heads, groups)
    own = block_segs(kv_s[0], tok)
    own_hot = seg_onehot(own)
    m_s[...] = jnp.full(m_s.shape, NEG, F32)
    acc_s[...] = jnp.zeros(acc_s.shape, F32)

    def body(b, r, masked):
        block = kv_s[b]
        if masked:
            same = same_tile(block, own_hot, r, tok, groups)
        scores = []
        for n in range(pairs):
            k = block[:tok, n * HD : (n + 1) * HD]
            s = jnp.dot(k, q_s[r * pairs + n], preferred_element_type=F32)
            scores.append(jnp.where(same, s, NEG) if masked else s)
        old = [m_s[r * pairs + n : r * pairs + n + 1, :] for n in range(pairs)]
        new = [
            jnp.maximum(old[n], jnp.max(scores[n], axis=0, keepdims=True)) for n in range(pairs)
        ]
        for n in range(pairs):
            i = r * pairs + n
            m_s[i : i + 1, :] = new[n]
            p = jnp.exp(scores[n] - new[n]).astype(BF)
            v = block[:tok, kvw + n * HD : kvw + (n + 1) * HD]
            v = jnp.concatenate([v, jnp.ones((tok, 16), BF)], axis=1)
            acc_s[i] = acc_s[i] * jnp.exp(old[n] - new[n]) + lax.dot_general(
                v, p, TN, preferred_element_type=F32
            )

    def nothing(b):
        pass

    visit_tiles(kv_s, own, tok, body, nothing, nothing)
    tiles = []
    for r in range(tok // ROWS):
        rows = []
        for n in range(pairs):
            i = r * pairs + n
            total = acc_s[i, HD : HD + 1, :]
            out = acc_s[i, :HD, :] / total
            lse = m_s[i : i + 1, :] + jnp.log(total)
            for g in range(groups):
                h = n * groups + g
                lanes = slice(g * ROWS, (g + 1) * ROWS)
                rows.append(out[:, lanes])
                lse_ref[h : h + 1, r * ROWS : (r + 1) * ROWS] = lse[:, lanes]
        tiles.append(jnp.concatenate(rows, axis=0))
    out = jnp.concatenate(tiles, axis=1).T
    hf_ref[...] = out
    near_ref[...] = out[: tok // 2].astype(BF)
    far_ref[...] = out[tok // 2 :].astype(BF)


def attend(q, blocks, heads, groups, first=()):
    tok = q.shape[0]
    nb = len(blocks)
    units = (tok // ROWS) * (heads // groups)
    return pl.pallas_call(
        drop_first(functools.partial(attend_kernel, nb, heads, groups), 1 + nb, len(first)),
        out_shape=(
            jax.ShapeDtypeStruct((tok, heads * HD), F32),
            jax.ShapeDtypeStruct((tok // 2, heads * HD), BF),
            jax.ShapeDtypeStruct((tok // 2, heads * HD), BF),
            jax.ShapeDtypeStruct((8, tok), F32),
        ),
        in_specs=vspec(1 + nb) + anywhere(len(first)),
        out_specs=tuple(vspec(4)),
        scratch_shapes=[
            pltpu.VMEM((nb,) + blocks[0].shape, BF),
            pltpu.VMEM((units, HD, groups * ROWS), BF),
            pltpu.VMEM((max(8, units), groups * ROWS), F32),
            pltpu.VMEM((units, HD + 16, groups * ROWS), F32),
        ],
        compiler_params=params(),
        name="attend",
        cost_estimate=cost(27),
    )(q, *blocks, *first)


def attend_back_kernel(nb, heads, groups, start, end, *refs):
    q_ref, own_ref, lse_ref = refs[:3]
    kv_refs = refs[3 : 3 + nb]
    at = 3 + nb
    if start:
        att_near_ref, att_far_ref, wo_ref, hf_ref = refs[at : at + 4]
        at += 4
    else:
        grad_in_ref, delta_in_ref, dq_in_ref = refs[at : at + 3]
        at += 3
    dkv_ref = refs[at]
    at += 1
    if start:
        grad_ref, delta_ref = refs[at : at + 2]
        at += 2
    if end:
        dq_near_ref, dq_far_ref = refs[at : at + 2]
        at += 2
    else:
        dq_out_ref = refs[at]
        at += 1
    kv_s, qt_s, q_s, dot_s, do_s, delta_s, dq_s, acc_s = refs[at:]
    tok = q_ref.shape[0]
    kvw = own_ref.shape[1] // 2
    key_heads = heads // groups
    if start:
        grad = jnp.concatenate(
            [
                lax.dot_general(ref[...], wo_ref[...], NT, preferred_element_type=F32)
                for ref in (att_near_ref, att_far_ref)
            ],
            axis=0,
        ).astype(BF)
        grad_ref[...] = grad
        prod = (grad.astype(F32) * hf_ref[...]).T
        for h in range(heads):
            delta_s[h : h + 1, :] = jnp.sum(prod[h * HD : (h + 1) * HD, :], axis=0, keepdims=True)
        delta_ref[...] = delta_s[...]
        dq_s[...] = jnp.zeros(dq_s.shape, F32)
    else:
        grad = grad_in_ref[...]
        delta_s[...] = delta_in_ref[...]
        dq_s[...] = dq_in_ref[...]
    for b in range(nb):
        kv_s[b] = kv_refs[b][...]
    turned_groups(q_ref[...], qt_s, heads, groups)
    straight_groups(q_ref[...], q_s, heads, groups)
    turned_groups(grad, dot_s, heads, groups)
    straight_groups(grad, do_s, heads, groups)
    own = block_segs(own_ref[...], tok)
    own_hot = seg_onehot(own)

    def body(b, r, masked):
        block = kv_s[b]
        if masked:
            same = same_tile(block, own_hot, r, tok, groups)
        for n in range(key_heads):
            i = r * key_heads + n
            k = block[:tok, n * HD : (n + 1) * HD]
            v = block[:tok, kvw + n * HD : kvw + (n + 1) * HD]
            s = jnp.dot(k, qt_s[i], preferred_element_type=F32)
            dp = jnp.dot(v, dot_s[i], preferred_element_type=F32)
            p = jnp.exp(s - head_rows(lse_ref, r, n, groups))
            if masked:
                p = jnp.where(same, p, 0.0)
            ds = (p * (dp - head_rows(delta_s, r, n, groups))).astype(BF)
            acc_s[n] += jnp.dot(ds, q_s[i], preferred_element_type=F32)
            acc_s[key_heads + n] += jnp.dot(p.astype(BF), do_s[i], preferred_element_type=F32)
            dq_s[i] += lax.dot_general(k, ds, TN, preferred_element_type=F32)

    def before(b):
        acc_s[...] = jnp.zeros(acc_s.shape, F32)

    def behind(b):
        sums = jnp.concatenate([acc_s[i] for i in range(2 * key_heads)], axis=1)
        dkv_ref[b] = sums.astype(BF)

    visit_tiles(kv_s, own, tok, body, before, behind)
    if end:
        tiles = []
        for r in range(tok // ROWS):
            rows = [
                dq_s[r * key_heads + h // groups, :, (h % groups) * ROWS : (h % groups + 1) * ROWS]
                for h in range(heads)
            ]
            tiles.append(jnp.concatenate(rows, axis=0))
        out = (jnp.concatenate(tiles, axis=1).T * HD ** (-0.5)).astype(BF)
        dq_near_ref[...] = out[: tok // 2]
        dq_far_ref[...] = out[tok // 2 :]
    else:
        dq_out_ref[...] = dq_s[...]


def attend_back(q, own, lse, blocks, heads, groups, start=None, going=None, end=True, first=()):
    tok = q.shape[0]
    nb = len(blocks)
    width = heads * HD
    key_heads = heads // groups
    units = (tok // ROWS) * key_heads
    operands = [q, own, lse] + list(blocks) + list(start if start is not None else going)
    outs = [((nb, tok, own.shape[1]), BF)]
    if start is not None:
        outs += [((tok, width), BF), ((8, tok), F32)]
    outs += [((tok // 2, width), BF)] * 2 if end else [((units, HD, groups * ROWS), F32)]
    kernel = functools.partial(
        attend_back_kernel, nb, heads, groups, start is not None, end
    )
    return pl.pallas_call(
        drop_first(kernel, len(operands), len(first)),
        out_shape=tuple(jax.ShapeDtypeStruct(shape, dtype) for shape, dtype in outs),
        in_specs=vspec(len(operands)) + anywhere(len(first)),
        out_specs=tuple(vspec(len(outs))),
        scratch_shapes=[
            pltpu.VMEM((nb,) + blocks[0].shape, BF),
            pltpu.VMEM((units, HD, groups * ROWS), BF),
            pltpu.VMEM((units, groups * ROWS, HD), BF),
            pltpu.VMEM((units, HD, groups * ROWS), BF),
            pltpu.VMEM((units, groups * ROWS, HD), BF),
            pltpu.VMEM((8, tok), F32),
            pltpu.VMEM((units, HD, groups * ROWS), F32),
            pltpu.VMEM((2 * key_heads, tok, HD), F32),
        ],
        compiler_params=params(),
        name="attend_back",
        cost_estimate=cost(4.5 * nb),
    )(*operands, *first)


def routes_kernel(at, *refs):
    out_ref = refs[-1]
    tok = out_ref.shape[1]
    for b, ref in enumerate(refs[:-1]):
        rows = ref[tok : tok + EXTRA, :].astype(F32)
        both = [
            jnp.concatenate([rows[i : i + 1, :] for i in range(c * at, (c + 1) * at)], axis=1)
            for c in (1, 2)
        ]
        out_ref[b] = jnp.concatenate(both + [jnp.zeros((6, tok), F32)], axis=0).T


def routes(blocks, tok, first=()):
    return pl.pallas_call(
        drop_first(
            functools.partial(routes_kernel, tok // blocks[0].shape[1]), len(blocks), len(first)
        ),
        out_shape=jax.ShapeDtypeStruct((len(blocks), tok, 8), F32),
        in_specs=vspec(len(blocks)) + anywhere(len(first)),
        out_specs=vspec(1)[0],
        compiler_params=params(),
        name="routes",
        cost_estimate=cost(2),
    )(*blocks, *first)


def experts_kernel(
    core_ref,
    ids_ref,
    mine_ref,
    theirs_ref,
    g_ref,
    wr_ref,
    wg_ref,
    wu_ref,
    wd_ref,
    mix_keep_ref,
    mix_send_ref,
    dx_keep_ref,
    dx_send_ref,
    gates_ref,
    ent_ref,
    a2_s,
    g_s,
    mix_s,
    dx_s,
    back_s,
):
    e = pl.program_id(0)
    tok, width = a2_s.shape
    half = tok // 2
    experts = wr_ref.shape[0]
    lane = lax.broadcasted_iota(jnp.int32, (tok, experts), 1)
    first = ids_ref[:, 0:1]
    second = ids_ref[:, 1:2]

    @pl.when(e == 0)
    def _():
        a2_s[:half, :] = mine_ref[...]
        a2_s[half:, :] = theirs_ref[...]
        for i in range(2):
            start = pl.multiple_of(((core_ref[0] + i) % 2) * half, half)
            g_s[pl.ds(i * half, half), :] = g_ref[pl.ds(start, half), :]
        logits = lax.dot_general(a2_s[...], wr_ref[...], NT, preferred_element_type=F32)
        one = jnp.sum(jnp.where(lane == first, logits, 0.0), axis=1, keepdims=True)
        two = jnp.sum(jnp.where(lane == second, logits, 0.0), axis=1, keepdims=True)
        top = jnp.maximum(one, two)
        one = jnp.exp(one - top)
        two = jnp.exp(two - top)
        total = one + two
        gates_ref[...] = jnp.where(lane == first, one / total, 0.0) + jnp.where(
            lane == second, two / total, 0.0
        )
        mix_s[...] = jnp.zeros(mix_s.shape, F32)
        dx_s[...] = jnp.zeros(dx_s.shape, F32)
        back_s[...] = jnp.zeros(back_s.shape, F32)
        ent_ref[...] = jnp.zeros(ent_ref.shape, BF)

    wg = wg_ref[0]
    wu = wu_ref[0]
    wd = wd_ref[0]
    for i in range(2):
        rows = pl.ds(i * half, half)
        a2 = a2_s[rows, :]
        u = jnp.dot(a2, wg, preferred_element_type=F32)
        w = jnp.dot(a2, wu, preferred_element_type=F32)
        m = lax.dot_general(g_s[rows, :], wd, NT, preferred_element_type=F32)
        here = lane[:half] == e
        gate = jnp.sum(jnp.where(here, gates_ref[rows, :], 0.0), axis=1, keepdims=True)
        pick_one = (ids_ref[rows, 0:1] == e).astype(F32)
        pick_two = (ids_ref[rows, 1:2] == e).astype(F32)
        sig = 1.0 / (1.0 + jnp.exp(-u))
        act = u * sig
        mid = (act * w).astype(BF).astype(F32)
        back = jnp.sum(mid * m, axis=1, keepdims=True) * (pick_one + pick_two)
        back_s[rows, :] += jnp.where(here, back, 0.0)
        mid = mid * gate
        gm = gate * m
        up_back = gm * act
        pre_back = gm * w * sig * (1.0 + u * (1.0 - sig))
        mid_b = mid.astype(BF)
        up_b = up_back.astype(BF)
        pre_b = pre_back.astype(BF)
        mix_s[rows, :] += jnp.dot(mid_b, wd, preferred_element_type=F32)
        dx_s[rows, :] += lax.dot_general(
            pre_b, wg, NT, preferred_element_type=F32
        ) + lax.dot_general(up_b, wu, NT, preferred_element_type=F32)
        for kind, value in enumerate((mid, pre_back, up_back)):
            for c, pick in enumerate((pick_one, pick_two)):
                ent_ref[2 * kind + c, rows, :] += (value * pick).astype(BF)

    @pl.when(e == pl.num_programs(0) - 1)
    def _():
        mix_keep_ref[...] = mix_s[:half, :]
        mix_send_ref[...] = mix_s[half:, :].astype(BF)
        dx_keep_ref[:, :width] = dx_s[:half, :]
        dx_send_ref[:, :width] = dx_s[half:, :].astype(BF)
        pad = jnp.zeros((half, 128 - experts), F32)
        dx_keep_ref[:, width:] = jnp.concatenate([back_s[:half, :], pad], axis=1)
        dx_send_ref[:, width:] = jnp.concatenate([back_s[half:, :], pad], axis=1).astype(BF)


def experts_call(core, ids, mine, theirs, g, wr, wg, wu, wd, first=()):
    half, width = mine.shape
    tok = 2 * half
    experts, _, hidden = wg.shape

    def whole(*shape):
        return pl.BlockSpec(shape, lambda e, *_: (0,) * len(shape))

    def one(*shape):
        return pl.BlockSpec((1,) + shape, lambda e, *_: (e,) + (0,) * len(shape))

    return pl.pallas_call(
        drop_first(experts_kernel, 9, len(first)),
        out_shape=(
            jax.ShapeDtypeStruct((half, width), F32),
            jax.ShapeDtypeStruct((half, width), BF),
            jax.ShapeDtypeStruct((half, width + 128), F32),
            jax.ShapeDtypeStruct((half, width + 128), BF),
            jax.ShapeDtypeStruct((tok, experts), F32),
            jax.ShapeDtypeStruct((6, tok, hidden), BF),
        ),
        grid=(experts,),
        in_specs=[
            pl.BlockSpec(memory_space=pltpu.SMEM),
            whole(tok, 2),
            whole(half, width),
            whole(half, width),
            whole(tok, width),
            whole(experts, width),
            one(width, hidden),
            one(width, hidden),
            one(hidden, width),
        ]
        + anywhere(len(first)),
        out_specs=(
            whole(half, width),
            whole(half, width),
            whole(half, width + 128),
            whole(half, width + 128),
            whole(tok, experts),
            whole(6, tok, hidden),
        ),
        scratch_shapes=[
            pltpu.VMEM((tok, width), BF),
            pltpu.VMEM((tok, width), BF),
            pltpu.VMEM((tok, width), F32),
            pltpu.VMEM((tok, width), F32),
            pltpu.VMEM((tok, experts), F32),
        ],
        compiler_params=params(dimension_semantics=("arbitrary",)),
        name="experts",
        cost_estimate=cost(32),
    )(core, ids, mine, theirs, g, wr, wg, wu, wd, *first)


def expert_grads_kernel(count, base, places, ids_ref, *refs):
    x_refs = refs[0:2]
    g_refs = refs[2:4]
    ents = refs[4 : 4 + count]
    outs, theirs_ref = refs[-4:-1], refs[-1]
    e = (pl.program_id(0) + base).astype(F32)
    cols = outs[0].shape[1]
    sums = [None, None, None]
    for b in range(count):
        half = x_refs[0].shape[2]
        hidden = ents[b].shape[2]
        for i in range(2):
            rows = pl.ds(i * half, half)
            one = jnp.where(ids_ref[places[b], rows, 0:1] == e, 1.0, 0.0).astype(BF)
            two = jnp.where(ids_ref[places[b], rows, 1:2] == e, 1.0, 0.0).astype(BF)
            one = jnp.broadcast_to(one, (half, hidden))
            two = jnp.broadcast_to(two, (half, hidden))
            xt = x_refs[i][b]
            gt = g_refs[i][b]
            for kind in range(3):
                value = ents[b][2 * kind, rows, :] * one + ents[b][2 * kind + 1, rows, :] * two
                term = jnp.dot(gt if kind == 0 else xt, value, preferred_element_type=F32)
                sums[kind] = term if sums[kind] is None else sums[kind] + term
    for kind in range(3):
        outs[kind][0] = sums[kind][:cols]
        theirs_ref[kind, 0] = sums[kind][cols:].astype(BF)


def expert_grads(base, experts, ids, places, xm, xo, gm, go, ents, first=()):
    cols = xm.shape[1] // 2
    hidden = ents[0].shape[-1]
    operands = [ids, xm, xo, gm, go] + list(ents)
    specs = [pl.BlockSpec(x.shape, lambda e, nd=x.ndim: (0,) * nd) for x in operands]
    out_spec = pl.BlockSpec((1, cols, hidden), lambda e: (e, 0, 0))
    kernel = functools.partial(expert_grads_kernel, len(ents), base, places)
    return pl.pallas_call(
        drop_first(kernel, len(operands), len(first)),
        out_shape=(jax.ShapeDtypeStruct((experts, cols, hidden), F32),) * 3
        + (jax.ShapeDtypeStruct((3, experts, cols, hidden), BF),),
        grid=(experts,),
        in_specs=specs + anywhere(len(first)),
        out_specs=(out_spec,) * 3
        + (pl.BlockSpec((3, 1, cols, hidden), lambda e: (0, e, 0, 0)),),
        compiler_params=params(dimension_semantics=("arbitrary",)),
        name="expert_grads",
        cost_estimate=cost(1.2 * experts),
    )(*operands, *first)


def finish_kernel(*refs):
    mine, got_ref, outs = refs[:3], refs[3], refs[-3:]
    for kind in range(3):
        value = mine[kind][0] + got_ref[kind, 0].astype(F32)
        outs[kind][0] = value.T if kind == 0 else value


def finish(base, experts, mine, got, outs=None, first=()):
    some, cols, hidden = mine[0].shape
    kept = [] if outs is None else list(outs)
    part = pl.BlockSpec((1, cols, hidden), lambda e: (e, 0, 0))
    place = pl.BlockSpec((1, cols, hidden), lambda e: (base + e, 0, 0))
    turned = pl.BlockSpec((1, hidden, cols), lambda e: (base + e, 0, 0))
    waits = kept + list(first)
    return pl.pallas_call(
        drop_first(finish_kernel, 4, len(waits)),
        out_shape=(
            jax.ShapeDtypeStruct((experts, hidden, cols), F32),
            jax.ShapeDtypeStruct((experts, cols, hidden), F32),
            jax.ShapeDtypeStruct((experts, cols, hidden), F32),
        ),
        grid=(some,),
        in_specs=[part] * 3
        + [pl.BlockSpec((3, 1, cols, hidden), lambda e: (0, e, 0, 0))]
        + anywhere(len(waits)),
        out_specs=(turned, place, place),
        input_output_aliases={4 + i: i for i in range(len(kept))},
        compiler_params=params(dimension_semantics=("arbitrary",)),
        name="finish",
        cost_estimate=cost(3),
    )(*mine, got, *waits)


def my_rows(core_ref, ref):
    half = ref.shape[0] // 2
    return ref[pl.ds(pl.multiple_of(core_ref[0] * half, half), half), :]


def simple(kernel, name, outs, core, *operands, first=()):
    return pl.pallas_call(
        drop_first(kernel, 1 + len(operands), len(first)),
        out_shape=tuple(jax.ShapeDtypeStruct(shape, dtype) for shape, dtype in outs),
        in_specs=[pl.BlockSpec(memory_space=pltpu.SMEM)] + vspec(len(operands)) + anywhere(len(first)),
        out_specs=tuple(vspec(len(outs))),
        compiler_params=params(),
        name=name,
        cost_estimate=cost(5),
    )(core, *operands, *first)


def middle_kernel(core_ref, x_ref, gain_ref, *refs):
    parts, weights = refs[:4], refs[4:8]
    hidden_ref, a2_ref = refs[8:]
    total = my_rows(core_ref, x_ref).astype(F32)
    for part, weight in zip(parts, weights):
        total = total + jnp.dot(part[...], weight[...], preferred_element_type=F32)
    inv = lax.rsqrt(jnp.mean(total * total, axis=-1, keepdims=True) + eps)
    hidden_ref[...] = total
    a2_ref[...] = (total * inv * gain_ref[...][None, :]).astype(BF)


def back_kernel(
    core_ref,
    near_ref,
    got_ref,
    hidden_ref,
    a2_ref,
    gates_ref,
    ids_ref,
    wr_ref,
    gain_ref,
    g_ref,
    grad_ref,
    att_ref,
    misc_ref,
):
    half, width = hidden_ref.shape
    experts = wr_ref.shape[0]
    total = near_ref[...].astype(F32) + got_ref[...].astype(F32)
    gate_back = total[:, width:][:, :experts]
    gates = gates_ref[:half, :]
    lane = lax.broadcasted_iota(jnp.int32, (half, experts), 1)
    picked = (lane == ids_ref[:half, 0:1]) | (lane == ids_ref[:half, 1:2])
    logit = gates * (gate_back - jnp.sum(gates * gate_back, axis=-1, keepdims=True))
    logit = jnp.where(picked, logit, 0.0).astype(BF)
    back = total[:, :width] + jnp.dot(logit, wr_ref[...], preferred_element_type=F32)
    hidden = hidden_ref[...]
    inv = lax.rsqrt(jnp.mean(hidden * hidden, axis=-1, keepdims=True) + eps)
    upstream = my_rows(core_ref, g_ref).astype(F32)
    scaled = back * gain_ref[...][None, :]
    grad = upstream + inv * (
        scaled - hidden * inv * inv * jnp.mean(scaled * hidden, axis=-1, keepdims=True)
    )
    grad_ref[...] = grad
    att_ref[...] = grad.astype(BF)
    misc_ref[:8, :] = lax.dot_general(logit, a2_ref[...], TN, preferred_element_type=F32)
    ffn = jnp.sum(back * hidden * inv, axis=0, keepdims=True)
    misc_ref[8:, :] = jnp.broadcast_to(ffn, (8, width))


def query_back_kernel(core_ref, *refs):
    pairs, weights, out_ref = refs[:2], refs[2:6], refs[6]
    total = None
    for i, weight in enumerate(weights):
        term = lax.dot_general(
            pairs[i // 2][i % 2], weight[...], NT, preferred_element_type=F32
        )
        total = term if total is None else total + term
    out_ref[...] = total


def input_kernel(core_ref, x_ref, gain_ref, grad_ref, query_ref, *refs):
    parts, weights = refs[:4], refs[4:8]
    out_ref, norm_ref = refs[8:]
    back = query_ref[...]
    for part, weight in zip(parts, weights):
        start = weight.shape[1] - part.shape[1]
        back = back + lax.dot_general(
            part[...], weight[:, start:], NT, preferred_element_type=F32
        )
    x = my_rows(core_ref, x_ref).astype(F32)
    inv = lax.rsqrt(jnp.mean(x * x, axis=-1, keepdims=True) + eps)
    scaled = back * gain_ref[...][None, :]
    out_ref[...] = grad_ref[...] + inv * (
        scaled - x * inv * inv * jnp.mean(scaled * x, axis=-1, keepdims=True)
    )
    norm = jnp.sum(back * x * inv, axis=0, keepdims=True)
    norm_ref[...] = jnp.broadcast_to(norm, norm_ref.shape)


def place_kernel(core_ref, mine_ref, theirs_ref, out_ref):
    half = mine_ref.shape[0]
    out_ref[pl.ds(pl.multiple_of(core_ref[0] * half, half), half), :] = mine_ref[...]
    out_ref[pl.ds(pl.multiple_of((1 - core_ref[0]) * half, half), half), :] = theirs_ref[...]


def columns_kernel(waits, owner_ref, core_ref, x_ref, *refs):
    outs, turned = refs[waits:-1], refs[-1]
    per, rows_out, half = outs[0].shape
    side = owner_ref.shape[0] // (per * len(outs))
    cols = rows_out // side
    x = my_rows(core_ref, x_ref) if x_ref.shape[0] != half else x_ref[...]
    turned[...] = x.T
    for r, out_ref in enumerate(outs):
        for i in range(per * side):
            rows = pl.ds(pl.multiple_of(owner_ref[r * per * side + i] * cols, 16), cols)
            out_ref[i // side, (i % side) * cols : (i % side + 1) * cols, :] = turned[rows, :]


def columns(owner, core, x, half, groups, side, first=()):
    n = owner.shape[0]
    width = x.shape[1]
    smem = pl.BlockSpec(memory_space=pltpu.SMEM)
    out = jax.ShapeDtypeStruct((n // (groups * side), side * (width // n), half), BF)
    return pl.pallas_call(
        functools.partial(columns_kernel, len(first)),
        out_shape=(out,) * groups,
        in_specs=[smem, smem] + vspec(1) + [pl.BlockSpec(memory_space=pl.ANY)] * len(first),
        out_specs=tuple(vspec(groups)),
        scratch_shapes=[pltpu.VMEM((width, half), BF)],
        compiler_params=params(),
        name="columns",
        cost_estimate=cost(2.5),
    )(owner, core, x, *first)


def weight_kernel(shape, extra, owner_ref, *refs):
    out_ref, turned, misc_turned = refs[-3:]
    n, cols, _ = out_ref.shape
    at = 0
    column = 0
    for group, pairs in enumerate(shape):
        lefts, rights = refs[at : at + pairs], refs[at + pairs : at + 2 * pairs]
        at += 2 * pairs
        row = 0
        for left in lefts:
            turned[group, :, row : row + left.shape[0]] = left[...].T
            row += left.shape[0]
        right = jnp.concatenate([r[...] for r in rights], axis=0) if pairs > 1 else rights[0][...]
        for i in range(n):
            rows = pl.ds(pl.multiple_of(owner_ref[i] * cols, 16), cols)
            out_ref[i, :, column : column + right.shape[1]] = jnp.dot(
                turned[group, rows, :], right, preferred_element_type=F32
            ).astype(BF)
        column += right.shape[1]
    if extra:
        misc = refs[at][...]
        spare = jnp.zeros((128 - misc.shape[0], misc.shape[1]), F32)
        misc_turned[...] = jnp.concatenate([misc, spare], axis=0).T
        for i in range(n):
            rows = pl.ds(pl.multiple_of(owner_ref[i] * cols, 16), cols)
            out_ref[i, :, column:] = misc_turned[rows, :].astype(BF)


def weight_terms(owner, groups, misc=None, us=4, first=()):
    n = owner.shape[0]
    width = groups[0][0][0].shape[1]
    rows = sum(x.shape[0] for x in groups[0][0])
    out_width = sum(rights[0].shape[1] for _, rights in groups)
    operands = []
    for lefts, rights in groups:
        operands += list(lefts) + list(rights)
    if misc is not None:
        operands.append(misc)
        out_width += 128
    shape = tuple(len(lefts) for lefts, _ in groups)
    return pl.pallas_call(
        drop_first(
            functools.partial(weight_kernel, shape, misc is not None),
            1 + len(operands),
            len(first),
        ),
        out_shape=jax.ShapeDtypeStruct((n, width // n, out_width), BF),
        in_specs=[pl.BlockSpec(memory_space=pltpu.SMEM)]
        + vspec(len(operands))
        + anywhere(len(first)),
        out_specs=vspec(1)[0],
        scratch_shapes=[pltpu.VMEM((len(groups), width, rows), BF), pltpu.VMEM((width, 128), F32)],
        compiler_params=params(),
        name="weight_terms",
        cost_estimate=cost(us),
    )(owner, *operands, *first)


def per_device(
    n_ctx,
    layer_input,
    segment_ids,
    expert_ids,
    norm_gain,
    query_weight,
    key_weight,
    value_weight,
    output_weight,
    ffn_gain,
    router_weight,
    gate_weight,
    up_weight,
    down_weight,
    cotangent,
):
    tok, width = layer_input.shape
    half = tok // 2
    groups = H // KV
    kv_local = key_weight.shape[1] // HD
    heads = kv_local * groups
    kvw = key_weight.shape[1]
    experts = gate_weight.shape[0]
    cols = width // n_ctx
    digits = digits_of(n_ctx)
    keys = rel_keys(digits)
    upper_first = list(range(1, len(digits))) + [0]
    lower_first = list(range(len(digits)))
    me = lax.axis_index("ctx")
    core = lax.axis_index("wa") % 2
    core_arr = jnp.full((1,), core, jnp.int32)
    owner_to = jnp.stack([digit_offset(me, k, digits, 1) for k in keys]).astype(jnp.int32)
    owner_from = jnp.stack([digit_offset(me, k, digits, -1) for k in keys]).astype(jnp.int32)
    gain_one, gain_two = norm_gain, ffn_gain
    router = router_weight.T

    def mine_first(x):
        return jnp.where(core == 0, x, jnp.concatenate([x[half:], x[:half]], axis=0))

    segs = mine_first(segment_ids).astype(BF)
    ids = mine_first(expert_ids)
    extra = jnp.concatenate([segs, ids[:, 0].astype(BF), ids[:, 1].astype(BF)])
    extra = jnp.pad(extra, (0, EXTRA * 2 * kvw - extra.shape[0])).reshape(EXTRA, 2 * kvw)
    a1, q, kv = project(
        core_arr, layer_input, gain_one, query_weight, key_weight, value_weight, extra
    )
    tops = digits[-1][1]
    staged = len(digits) == 2
    side = digits[0][1]
    low, top = digits[0], digits[-1]
    turned_digits = digits[1:] + digits[:1]
    turned_keys = [(k[-1],) + k[:-1] for k in rel_keys(turned_digits)]
    owner_turned = jnp.stack(
        [digit_offset(me, k, digits, -1) for k in turned_keys]
    ).astype(jnp.int32)

    wo_chip = other_chip(output_weight)
    kv_weight = jnp.concatenate([key_weight, value_weight], axis=1)
    g_out = columns(owner_to, core_arr, cotangent, half, tops, side, [kv])
    if staged:
        z, y = [kv], []
        for r in range(tops - 1):
            aside = [g_out[0], kv_weight] if r == tops - 2 else []
            z_next, y_next = tie([hop(z[r], n_ctx, top), hop(z[r], n_ctx, low)], aside)
            z.append(z_next)
            y.append(y_next)
        y.append(hop(z[-1], n_ctx, low))
        kv_list = [block for pair in zip(z, y) for block in pair]
    else:
        kv_blocks = gather_ctx(kv, n_ctx, digits, upper_first)
        kv_list = [kv_blocks[k] for k in keys]

    g_top = exchange_top(g_out, n_ctx, digits)

    heads_f32, heads_near, heads_far, lse = attend(
        q, kv_list, heads, groups, first=[g_out[0]]
    )
    heads_near, heads_far, wo_chip, *rest = tie(
        [heads_near, heads_far, wo_chip] + list(g_top[1:]), []
    )
    g_top = [g_top[0]] + list(rest)
    wo_parts = [output_weight, other_core(output_weight), wo_chip, other_core(wo_chip)]

    parts = all_parts(heads_near, heads_far)
    g_pieces = exchange_rest(g_top, n_ctx, digits)
    hidden_one, a2_mine = simple(
        middle_kernel,
        "middle",
        [((half, width), F32), ((half, width), BF)],
        core_arr,
        layer_input,
        gain_two,
        *parts,
        *wo_parts,
    )
    a2_far = other_core(a2_mine)
    a2_out = columns(owner_to, core_arr, a2_mine, half, tops, side)
    a2_top = exchange_top(a2_out, n_ctx, digits)
    wq_chip = other_chip(query_weight)

    mix_keep, mix_send, dx_keep, dx_send, gates, ent = experts_call(
        core_arr,
        ids,
        a2_mine,
        a2_far,
        cotangent,
        router,
        gate_weight,
        up_weight,
        down_weight,
        first=[a2_out[0]],
    )
    dx_send, wq_chip, *rest = tie(
        [dx_send, wq_chip] + list(a2_top[1:]), [array for array, _ in g_pieces]
    )
    a2_top = [a2_top[0]] + list(rest)

    near = (dx_keep + other_core(dx_send).astype(F32)).astype(BF)
    got = other_chip(near)
    if staged:
        z = [ent]
        z_next = hop(ent, n_ctx, top)
    wq_parts = [query_weight, other_core(query_weight), wq_chip, other_core(wq_chip)]
    hidden_grad, att_near, misc = simple(
        back_kernel,
        "back",
        [((half, width), F32), ((half, width), BF), ((16, width), F32)],
        core_arr,
        near,
        got,
        hidden_one,
        a2_mine,
        gates,
        ids,
        router,
        gain_two,
        cotangent,
        first=[wq_parts[1], wq_parts[3]],
    )
    att_far = other_core(att_near)
    (mix_send,) = tie([mix_send], [got])
    mix_near = (mix_keep + other_core(mix_send).astype(F32)).astype(BF)
    mix_got = other_chip(mix_near)
    a2_pieces = exchange_rest(a2_top, n_ctx, digits)
    if staged:
        (z_next,) = tie([z_next], [att_near])
        z.append(z_next)
        z_next = hop(z[1], n_ctx, top)

    begin = [att_near, att_far, output_weight, heads_f32]
    sides = [[kv_list[i] for i, k in enumerate(keys) if k[0] == r] for r in range(side)]
    dkv_far, head_grad, delta, dq_going = attend_back(
        q,
        kv_list[0],
        lse,
        [block for r in range(1, side) for block in sides[r]],
        heads,
        groups,
        start=begin,
        end=False,
        first=[mix_near] + ([z[1]] if staged else []),
    )
    (mix_got,) = tie([mix_got], [dq_going])
    dkv_far_got = hop(dkv_far, n_ctx, low)
    ids_all = routes(sides[0], tok, [dq_going])
    a2_stack, a2_stack_far = swapped(a2_pieces, [dq_going])
    g_stack, g_stack_far = swapped(g_pieces, [dq_going])
    terms_o = weight_terms(
        owner_turned,
        [([att_near, att_far], [heads_near, heads_far])],
        misc,
        first=[dq_going, a2_stack, g_stack],
    )
    kv_weight, mix_got = tie([kv_weight, mix_got], [])
    kv_chip = other_chip(kv_weight)
    waits = [ids_all, a2_stack_far, g_stack_far, terms_o]
    if staged:
        (z_next,) = tie([z_next], [terms_o])
        z.append(z_next)
        z_next = hop(z[2], n_ctx, top)
        waits = waits + [z[2]]
    o_sides = cut(terms_o, side)
    o_got = hop(o_sides[1], n_ctx, low)
    dkv_near, dq_near, dq_far = attend_back(
        q,
        kv_list[0],
        lse,
        sides[0],
        heads,
        groups,
        going=[head_grad, delta, dq_going],
        first=waits,
    )
    dkv_far_got, kv_chip, o_got = tie([dkv_far_got, kv_chip, o_got], [dq_near])

    dkv_sides = [
        total([dkv_far_got[i : i + 1], dkv_near[i : i + 1]]).astype(BF)
        for i in range(dkv_near.shape[0])
    ]
    if staged:
        dkv_sent = scatter_sends(dkv_sides, n_ctx, top)
    dq_core = other_core(dq_far)

    terms_q = weight_terms(
        owner_turned,
        [([a1], [jnp.concatenate([dq_near, dq_far], axis=0)])],
        first=[dkv_sides[1 % len(dkv_sides)]],
    )
    dq_core, o_got = tie([dq_core, o_got], [terms_q])
    dq_pair = jnp.stack([dq_near, dq_core], axis=0)
    q_sides = cut(terms_q, side)
    q_got = hop(q_sides[1], n_ctx, low)
    o_sum = total([o_sides[0], o_got])

    if staged:
        z_next, dq_pair = tie([z_next, dq_pair], [terms_q])
        z.append(z_next)
        ents = z
    else:
        upper = gather_ctx(ent, n_ctx, digits, upper_first[:-1])
        ents = [upper[k] for k in keys if k[0] == 0]
    dq_chip = other_chip(dq_pair)
    some = experts // 2
    places = tuple(range(len(ents)))
    shared = [a2_stack, a2_stack_far, g_stack, g_stack_far, ents]
    *grads_a, send_a = expert_grads(0, some, ids_all, places, *shared)
    (q_got,) = tie([q_got], [send_a])
    got_a = hop(send_a, n_ctx, low)
    (dq_chip,) = tie([dq_chip], [send_a])
    (query_back,) = simple(
        query_back_kernel,
        "query_back",
        [((half, width), F32)],
        core_arr,
        dq_pair,
        dq_chip,
        *wq_parts,
    )
    if staged:
        more = tie(dkv_sent[1:], [query_back])
        dkv_own = total([dkv_sent[0]] + list(more))[0].astype(BF)
    else:
        dkv_own = scatter_ctx(jnp.concatenate(dkv_sides, axis=0), n_ctx, digits[1:]).astype(BF)
    kv_weights = [kv_weight, other_core(kv_weight), kv_chip, other_core(kv_chip)]

    dkv_parts = all_parts(dkv_own[:half], dkv_own[half:])
    *grads_b, send_b = expert_grads(
        some,
        experts - some,
        ids_all,
        places,
        *shared,
        first=[send_a, dkv_own, kv_weights[1], kv_weights[3]],
    )
    got_b = hop(send_b, n_ctx, low)
    dkv_parts = [dkv_parts[0]] + list(tie(dkv_parts[1:], [send_b]))
    in_mine, norm_row = simple(
        input_kernel,
        "input",
        [((half, width), F32), ((8, width), F32)],
        core_arr,
        layer_input,
        gain_one,
        hidden_grad,
        query_back,
        *dkv_parts,
        *kv_weights,
    )
    late = weight_terms(owner_from, [([a1], [dkv_own])], norm_row)
    in_ready, got_a = tie([in_mine, got_a], [late])
    in_far = other_core(in_ready)
    out_mine = hidden_one + mix_near.astype(F32) + mix_got.astype(F32)
    (layer_output,) = simple(
        place_kernel,
        "place",
        [((tok, width), F32)],
        core_arr,
        out_mine,
        other_core(out_mine),
        first=[late],
    )
    (input_grad,) = simple(
        place_kernel,
        "place",
        [((tok, width), F32)],
        core_arr,
        in_ready,
        in_far,
        first=[layer_output],
    )
    done = finish(0, experts, grads_a, got_a, first=[input_grad])

    q_sum = total([q_sides[0], q_got])
    terms = jnp.concatenate([o_sum, q_sum], axis=2).astype(BF)
    terms_own = scatter_ctx(terms, n_ctx, digits[1:], lambda at, xs: tie(xs, [late]))
    late_own = scatter_ctx(late, n_ctx, digits)
    down_grad, gate_grad, up_grad = finish(some, experts, grads_b, got_b, done)

    qw = heads * HD
    output_grad = terms_own[:, :qw].T
    small = jnp.concatenate(
        [terms_own[:, qw : qw + experts + 1], late_own[:, 2 * kvw : 2 * kvw + 1]], axis=1
    )
    small = small + other_core(small)
    return (
        layer_output,
        input_grad,
        small[:, experts + 1],
        terms_own[:, qw + 128 :],
        late_own[:, :kvw],
        late_own[:, kvw : 2 * kvw],
        output_grad,
        small[:, experts],
        small[:, :experts],
        gate_grad,
        up_grad,
        down_grad,
    )


def solution(mesh):
    in_specs = (
        P("ctx", None),
        P("ctx"),
        P("ctx", None),
        P(),
        P(None, "wa"),
        P(None, "wa"),
        P(None, "wa"),
        P("wa", None),
        P(),
        P(),
        P(None, None, "wa"),
        P(None, None, "wa"),
        P(None, "wa", None),
        P("ctx", None),
    )
    out_specs = (
        P("ctx", None),
        P("ctx", None),
        P("ctx"),
        P("ctx", "wa"),
        P("ctx", "wa"),
        P("ctx", "wa"),
        P("wa", "ctx"),
        P("ctx"),
        P("ctx", None),
        P(None, "ctx", "wa"),
        P(None, "ctx", "wa"),
        P(None, "wa", "ctx"),
    )
    return jax.shard_map(
        functools.partial(per_device, mesh.shape["ctx"]),
        mesh=mesh,
        in_specs=in_specs,
        out_specs=out_specs,
        check_vma=False,
    )
```

```python
import functools

import jax
import jax.numpy as jnp
from jax import lax
from jax.experimental import pallas as pl
from jax.experimental.pallas import tpu as pltpu
from jax.sharding import PartitionSpec as P

H = 24
KV = 8
HD = 64
eps = 1e-05
NEG = -1e30
F32 = jnp.float32
BF = jnp.bfloat16
VLIM = 60 * 1024 * 1024
EXTRA = 16
NT = (((1,), (1,)), ((), ()))
TN = (((0,), (0,)), ((), ()))


def digits_of(n):
    out = []
    stride = 1
    while n > 1:
        if stride == 1 and n % 2 == 0:
            radix = 2
        elif n % 4 == 0:
            radix = 4
        else:
            radix = n
        out.append((stride, radix))
        stride *= radix
        n //= radix
    return out


def moved(n, digit, shift):
    stride, radix = digit
    pairs = []
    for i in range(n):
        d = (i // stride) % radix
        pairs.append((i, i + ((d + shift) % radix - d) * stride))
    return pairs


def hop(x, n, digit, shift=1):
    return lax.ppermute(x, "ctx", moved(n, digit, shift))


def other_core(x):
    return lax.ppermute(x, "wa", [(i, i ^ 1) for i in range(4)])


def other_chip(x):
    return lax.ppermute(x, "wa", [(i, i ^ 2) for i in range(4)])


def rel_keys(digits):
    keys = [()]
    for _, radix in digits:
        keys = [k + (r,) for r in range(radix) for k in keys]
    return keys


def set_digit(key, at, value):
    return key[:at] + (value,) + key[at + 1 :]


def gather_ctx(x, n, digits, order):
    blocks = {tuple(0 for _ in digits): x}
    for at in order:
        fresh = {}
        for key, block in blocks.items():
            moving = block
            for s in range(1, digits[at][1]):
                moving = hop(moving, n, digits[at])
                fresh[set_digit(key, at, s)] = moving
        blocks.update(fresh)
    return blocks


def scatter_sends(blocks, n, digit):
    return [blocks[0]] + [hop(blocks[r], n, digit, -r) for r in range(1, len(blocks))]


def total(parts):
    return functools.reduce(jnp.add, [x.astype(F32) for x in parts])


def cut(stack, radix):
    per = stack.shape[0] // radix
    return [stack[r * per : (r + 1) * per] for r in range(radix)]


def scatter_ctx(stack, n, order, hold=lambda at, xs: xs, kind=BF):
    moving = stack
    for at in reversed(range(len(order))):
        parts = scatter_sends(cut(moving, order[at][1]), n, order[at])
        parts = parts[:1] + list(hold(at, parts[1:]))
        moving = total(parts)
        if at:
            moving = moving.astype(kind)
    return moving[0]


def stack_kernel(places, *refs):
    for i, (at, unit) in enumerate(places):
        refs[-1][i] = refs[at][unit]


def stacked(pieces):
    arrays = []
    places = []
    for array, unit in pieces:
        at = next((i for i, x in enumerate(arrays) if x is array), None)
        if at is None:
            at = len(arrays)
            arrays.append(array)
        places.append((at, unit))
    shape = (len(pieces),) + arrays[0].shape[1:]
    return pl.pallas_call(
        functools.partial(stack_kernel, tuple(places)),
        out_shape=jax.ShapeDtypeStruct(shape, arrays[0].dtype),
        in_specs=vspec(len(arrays)),
        out_specs=vspec(1)[0],
        compiler_params=params(),
        name="stacked",
        cost_estimate=cost(1),
    )(*arrays)


def exchange_top(groups, n, digits):
    return [groups[0]] + [hop(groups[r], n, digits[-1], r) for r in range(1, len(groups))]


def exchange_rest(groups, n, digits):
    keys = rel_keys(digits[1:])
    n_up = len(keys)
    per = n_up // len(groups)
    parts = {i: (groups[i // per], i % per) for i in range(n_up)}
    for at in reversed(range(1, len(digits) - 1)):
        for s in range(1, digits[at][1]):
            chosen = [i for i, k in enumerate(keys) if k[at - 1] == s]
            bundle = hop(stacked([parts[i] for i in chosen]), n, digits[at], s)
            for place, i in enumerate(chosen):
                parts[i] = (bundle, place)
    return [parts[i] for i in range(n_up)]


def swapped(pieces, first):
    arrays = []
    for array, _ in pieces:
        if not any(array is x for x in arrays):
            arrays.append(array)
    held = tie(arrays, first)
    pieces = [(held[next(i for i, x in enumerate(arrays) if x is a)], u) for a, u in pieces]
    near = stacked(pieces)
    return near, other_core(near)


def digit_offset(me, key, digits, sign):
    place = 0
    for (stride, radix), r in zip(digits, key):
        d = (me // stride) % radix
        place = place + ((d + sign * r) % radix) * stride
    return place


def tie_kernel(*refs):
    pass


def tie(xs, first):
    xs, first = list(xs), list(first)
    return pl.pallas_call(
        tie_kernel,
        out_shape=tuple(jax.ShapeDtypeStruct(x.shape, x.dtype) for x in xs),
        in_specs=anywhere(len(xs) + len(first)),
        out_specs=tuple(anywhere(len(xs))),
        input_output_aliases={i: i for i in range(len(xs))},
        name="tie",
    )(*xs, *first)


def diagonal(x):
    return lax.ppermute(x, "wa", [(i, i ^ 3) for i in range(4)])


def all_parts(near, far):
    return [near, other_core(far), other_chip(near), diagonal(far)]


def cost(us):
    return pl.CostEstimate(flops=int(us * 3e8), bytes_accessed=int(us * 9e5), transcendentals=0)


def params(**kw):
    return pltpu.CompilerParams(vmem_limit_bytes=VLIM, **kw)


def vspec(n):
    return [pl.BlockSpec(memory_space=pltpu.VMEM)] * n


def drop_first(kernel, at, count):
    if not count:
        return kernel

    def waiting(*refs):
        kernel(*refs[:at], *refs[at + count :])

    return waiting


def anywhere(count):
    return [pl.BlockSpec(memory_space=pl.ANY)] * count


def project_kernel(core_ref, x_ref, gain_ref, wq_ref, wk_ref, wv_ref, extra_ref, a1_ref, q_ref, kv_ref):
    tok = x_ref.shape[0]
    half = tok // 2
    kvw = wk_ref.shape[1]
    for i in range(2):
        start = pl.multiple_of(((core_ref[0] + i) % 2) * half, half)
        x = x_ref[pl.ds(start, half), :].astype(F32)
        inv = lax.rsqrt(jnp.mean(x * x, axis=-1, keepdims=True) + eps)
        a1 = (x * inv * gain_ref[...][None, :]).astype(BF)
        rows = pl.ds(i * half, half)
        a1_ref[rows, :] = a1
        kv_ref[rows, :kvw] = jnp.dot(a1, wk_ref[...], preferred_element_type=F32).astype(BF)
        kv_ref[rows, kvw:] = jnp.dot(a1, wv_ref[...], preferred_element_type=F32).astype(BF)
        q = jnp.dot(a1, wq_ref[...], preferred_element_type=F32).astype(BF)
        q_ref[rows, :] = (q.astype(F32) * HD ** (-0.5)).astype(BF)
    kv_ref[pl.ds(tok, EXTRA), :] = extra_ref[...]


def project(core, x, gain, wq, wk, wv, extra):
    tok, width = x.shape
    return pl.pallas_call(
        project_kernel,
        out_shape=(
            jax.ShapeDtypeStruct((tok, width), BF),
            jax.ShapeDtypeStruct((tok, wq.shape[1]), BF),
            jax.ShapeDtypeStruct((tok + EXTRA, 2 * wk.shape[1]), BF),
        ),
        in_specs=[pl.BlockSpec(memory_space=pltpu.SMEM)] + vspec(6),
        out_specs=tuple(vspec(3)),
        compiler_params=params(),
        name="project",
        cost_estimate=cost(5),
    )(core, x, gain, wq, wk, wv, extra)


def seg_onehot(row):
    lane = lax.broadcasted_iota(jnp.int32, (16, row.shape[1]), 0).astype(F32)
    return jnp.where(lane == row, 1.0, 0.0).astype(BF)


def seg_rows_of(block, tok):
    width = block.shape[1]
    return [
        block[tok : tok + EXTRA, :].astype(F32)[i : i + 1, :] for i in range(tok // width)
    ]


ROWS = 256


def block_segs(block, tok):
    return jnp.concatenate(seg_rows_of(block, tok), axis=1)


def turned_groups(x, out, heads, groups):
    x = x.astype(F32).T.astype(BF)
    pairs = heads // groups
    for r in range(x.shape[1] // ROWS):
        for h in range(heads):
            n, g = h // groups, h % groups
            out[r * pairs + n, :, g * ROWS : (g + 1) * ROWS] = x[
                h * HD : (h + 1) * HD, r * ROWS : (r + 1) * ROWS
            ]


def straight_groups(x, out, heads, groups):
    pairs = heads // groups
    for r in range(x.shape[0] // ROWS):
        for h in range(heads):
            n, g = h // groups, h % groups
            out[r * pairs + n, g * ROWS : (g + 1) * ROWS, :] = x[
                r * ROWS : (r + 1) * ROWS, h * HD : (h + 1) * HD
            ]


def head_rows(ref, r, n, groups):
    rows = slice(r * ROWS, (r + 1) * ROWS)
    return jnp.concatenate(
        [ref[h : h + 1, rows] for h in range(n * groups, (n + 1) * groups)], axis=1
    )


def visit_tiles(kv_s, own, tok, body, before, behind):
    tiles = tok // ROWS
    lows = [jnp.min(own[:, r * ROWS : (r + 1) * ROWS]) for r in range(tiles)]
    highs = [jnp.max(own[:, r * ROWS : (r + 1) * ROWS]) for r in range(tiles)]

    def visit(b, carry):
        seg = block_segs(kv_s[b], tok)
        lo = jnp.min(seg)
        hi = jnp.max(seg)
        before(b)
        for r in range(tiles):
            plain = (lo == hi) & (lows[r] == highs[r]) & (lo == lows[r])
            touch = (lo <= highs[r]) & (lows[r] <= hi)
            pl.when(plain)(functools.partial(body, b, r, False))
            pl.when(touch & jnp.logical_not(plain))(functools.partial(body, b, r, True))
        behind(b)
        return carry

    lax.fori_loop(0, kv_s.shape[0], visit, 0)


def same_tile(block, own_hot, r, tok, groups):
    same = lax.dot_general(
        seg_onehot(block_segs(block, tok)),
        own_hot[:, r * ROWS : (r + 1) * ROWS],
        TN,
        preferred_element_type=F32,
    )
    return jnp.concatenate([same] * groups, axis=1) > 0.5


def attend_kernel(nb, heads, groups, *refs):
    q_ref = refs[0]
    kv_refs = refs[1 : 1 + nb]
    hf_ref, near_ref, far_ref, lse_ref = refs[1 + nb : 5 + nb]
    kv_s, q_s, m_s, acc_s = refs[5 + nb :]
    tok = q_ref.shape[0]
    kvw = kv_refs[0].shape[1] // 2
    pairs = heads // groups
    for b in range(nb):
        kv_s[b] = kv_refs[b][...]
    turned_groups(q_ref[...], q_s, heads, groups)
    own = block_segs(kv_s[0], tok)
    own_hot = seg_onehot(own)
    m_s[...] = jnp.full(m_s.shape, NEG, F32)
    acc_s[...] = jnp.zeros(acc_s.shape, F32)

    def body(b, r, masked):
        block = kv_s[b]
        if masked:
            same = same_tile(block, own_hot, r, tok, groups)
        scores = []
        for n in range(pairs):
            k = block[:tok, n * HD : (n + 1) * HD]
            s = jnp.dot(k, q_s[r * pairs + n], preferred_element_type=F32)
            scores.append(jnp.where(same, s, NEG) if masked else s)
        old = [m_s[r * pairs + n : r * pairs + n + 1, :] for n in range(pairs)]
        new = [
            jnp.maximum(old[n], jnp.max(scores[n], axis=0, keepdims=True)) for n in range(pairs)
        ]
        for n in range(pairs):
            i = r * pairs + n
            m_s[i : i + 1, :] = new[n]
            p = jnp.exp(scores[n] - new[n]).astype(BF)
            v = block[:tok, kvw + n * HD : kvw + (n + 1) * HD]
            v = jnp.concatenate([v, jnp.ones((tok, 16), BF)], axis=1)
            acc_s[i] = acc_s[i] * jnp.exp(old[n] - new[n]) + lax.dot_general(
                v, p, TN, preferred_element_type=F32
            )

    def nothing(b):
        pass

    visit_tiles(kv_s, own, tok, body, nothing, nothing)
    tiles = []
    for r in range(tok // ROWS):
        rows = []
        for n in range(pairs):
            i = r * pairs + n
            total = acc_s[i, HD : HD + 1, :]
            out = acc_s[i, :HD, :] / total
            lse = m_s[i : i + 1, :] + jnp.log(total)
            for g in range(groups):
                h = n * groups + g
                lanes = slice(g * ROWS, (g + 1) * ROWS)
                rows.append(out[:, lanes])
                lse_ref[h : h + 1, r * ROWS : (r + 1) * ROWS] = lse[:, lanes]
        tiles.append(jnp.concatenate(rows, axis=0))
    out = jnp.concatenate(tiles, axis=1).T
    hf_ref[...] = out
    near_ref[...] = out[: tok // 2].astype(BF)
    far_ref[...] = out[tok // 2 :].astype(BF)


def attend(q, blocks, heads, groups, first=()):
    tok = q.shape[0]
    nb = len(blocks)
    units = (tok // ROWS) * (heads // groups)
    return pl.pallas_call(
        drop_first(functools.partial(attend_kernel, nb, heads, groups), 1 + nb, len(first)),
        out_shape=(
            jax.ShapeDtypeStruct((tok, heads * HD), F32),
            jax.ShapeDtypeStruct((tok // 2, heads * HD), BF),
            jax.ShapeDtypeStruct((tok // 2, heads * HD), BF),
            jax.ShapeDtypeStruct((8, tok), F32),
        ),
        in_specs=vspec(1 + nb) + anywhere(len(first)),
        out_specs=tuple(vspec(4)),
        scratch_shapes=[
            pltpu.VMEM((nb,) + blocks[0].shape, BF),
            pltpu.VMEM((units, HD, groups * ROWS), BF),
            pltpu.VMEM((max(8, units), groups * ROWS), F32),
            pltpu.VMEM((units, HD + 16, groups * ROWS), F32),
        ],
        compiler_params=params(),
        name="attend",
        cost_estimate=cost(27),
    )(q, *blocks, *first)


def attend_back_kernel(nb, heads, groups, start, end, *refs):
    q_ref, own_ref, lse_ref = refs[:3]
    kv_refs = refs[3 : 3 + nb]
    at = 3 + nb
    if start:
        att_near_ref, att_far_ref, wo_ref, hf_ref = refs[at : at + 4]
        at += 4
    else:
        grad_in_ref, delta_in_ref, dq_in_ref = refs[at : at + 3]
        at += 3
    dkv_ref = refs[at]
    at += 1
    if start:
        grad_ref, delta_ref = refs[at : at + 2]
        at += 2
    if end:
        dq_near_ref, dq_far_ref = refs[at : at + 2]
        at += 2
    else:
        dq_out_ref = refs[at]
        at += 1
    kv_s, qt_s, q_s, dot_s, do_s, delta_s, dq_s, acc_s = refs[at:]
    tok = q_ref.shape[0]
    kvw = own_ref.shape[1] // 2
    key_heads = heads // groups
    if start:
        grad = jnp.concatenate(
            [
                lax.dot_general(ref[...], wo_ref[...], NT, preferred_element_type=F32)
                for ref in (att_near_ref, att_far_ref)
            ],
            axis=0,
        ).astype(BF)
        grad_ref[...] = grad
        prod = (grad.astype(F32) * hf_ref[...]).T
        for h in range(heads):
            delta_s[h : h + 1, :] = jnp.sum(prod[h * HD : (h + 1) * HD, :], axis=0, keepdims=True)
        delta_ref[...] = delta_s[...]
        dq_s[...] = jnp.zeros(dq_s.shape, F32)
    else:
        grad = grad_in_ref[...]
        delta_s[...] = delta_in_ref[...]
        dq_s[...] = dq_in_ref[...]
    for b in range(nb):
        kv_s[b] = kv_refs[b][...]
    turned_groups(q_ref[...], qt_s, heads, groups)
    straight_groups(q_ref[...], q_s, heads, groups)
    turned_groups(grad, dot_s, heads, groups)
    straight_groups(grad, do_s, heads, groups)
    own = block_segs(own_ref[...], tok)
    own_hot = seg_onehot(own)

    def body(b, r, masked):
        block = kv_s[b]
        if masked:
            same = same_tile(block, own_hot, r, tok, groups)
        for n in range(key_heads):
            i = r * key_heads + n
            k = block[:tok, n * HD : (n + 1) * HD]
            v = block[:tok, kvw + n * HD : kvw + (n + 1) * HD]
            s = jnp.dot(k, qt_s[i], preferred_element_type=F32)
            dp = jnp.dot(v, dot_s[i], preferred_element_type=F32)
            p = jnp.exp(s - head_rows(lse_ref, r, n, groups))
            if masked:
                p = jnp.where(same, p, 0.0)
            ds = (p * (dp - head_rows(delta_s, r, n, groups))).astype(BF)
            acc_s[n] += jnp.dot(ds, q_s[i], preferred_element_type=F32)
            acc_s[key_heads + n] += jnp.dot(p.astype(BF), do_s[i], preferred_element_type=F32)
            dq_s[i] += lax.dot_general(k, ds, TN, preferred_element_type=F32)

    def before(b):
        acc_s[...] = jnp.zeros(acc_s.shape, F32)

    def behind(b):
        sums = jnp.concatenate([acc_s[i] for i in range(2 * key_heads)], axis=1)
        dkv_ref[b] = sums.astype(BF)

    visit_tiles(kv_s, own, tok, body, before, behind)
    if end:
        tiles = []
        for r in range(tok // ROWS):
            rows = [
                dq_s[r * key_heads + h // groups, :, (h % groups) * ROWS : (h % groups + 1) * ROWS]
                for h in range(heads)
            ]
            tiles.append(jnp.concatenate(rows, axis=0))
        out = (jnp.concatenate(tiles, axis=1).T * HD ** (-0.5)).astype(BF)
        dq_near_ref[...] = out[: tok // 2]
        dq_far_ref[...] = out[tok // 2 :]
    else:
        dq_out_ref[...] = dq_s[...]


def attend_back(q, own, lse, blocks, heads, groups, start=None, going=None, end=True, first=()):
    tok = q.shape[0]
    nb = len(blocks)
    width = heads * HD
    key_heads = heads // groups
    units = (tok // ROWS) * key_heads
    operands = [q, own, lse] + list(blocks) + list(start if start is not None else going)
    outs = [((nb, tok, own.shape[1]), BF)]
    if start is not None:
        outs += [((tok, width), BF), ((8, tok), F32)]
    outs += [((tok // 2, width), BF)] * 2 if end else [((units, HD, groups * ROWS), F32)]
    kernel = functools.partial(
        attend_back_kernel, nb, heads, groups, start is not None, end
    )
    return pl.pallas_call(
        drop_first(kernel, len(operands), len(first)),
        out_shape=tuple(jax.ShapeDtypeStruct(shape, dtype) for shape, dtype in outs),
        in_specs=vspec(len(operands)) + anywhere(len(first)),
        out_specs=tuple(vspec(len(outs))),
        scratch_shapes=[
            pltpu.VMEM((nb,) + blocks[0].shape, BF),
            pltpu.VMEM((units, HD, groups * ROWS), BF),
            pltpu.VMEM((units, groups * ROWS, HD), BF),
            pltpu.VMEM((units, HD, groups * ROWS), BF),
            pltpu.VMEM((units, groups * ROWS, HD), BF),
            pltpu.VMEM((8, tok), F32),
            pltpu.VMEM((units, HD, groups * ROWS), F32),
            pltpu.VMEM((2 * key_heads, tok, HD), F32),
        ],
        compiler_params=params(),
        name="attend_back",
        cost_estimate=cost(4.5 * nb),
    )(*operands, *first)


def routes_kernel(at, *refs):
    out_ref = refs[-1]
    tok = out_ref.shape[1]
    for b, ref in enumerate(refs[:-1]):
        rows = ref[tok : tok + EXTRA, :].astype(F32)
        both = [
            jnp.concatenate([rows[i : i + 1, :] for i in range(c * at, (c + 1) * at)], axis=1)
            for c in (1, 2)
        ]
        out_ref[b] = jnp.concatenate(both + [jnp.zeros((6, tok), F32)], axis=0).T


def routes(blocks, tok, first=()):
    return pl.pallas_call(
        drop_first(
            functools.partial(routes_kernel, tok // blocks[0].shape[1]), len(blocks), len(first)
        ),
        out_shape=jax.ShapeDtypeStruct((len(blocks), tok, 8), F32),
        in_specs=vspec(len(blocks)) + anywhere(len(first)),
        out_specs=vspec(1)[0],
        compiler_params=params(),
        name="routes",
        cost_estimate=cost(2),
    )(*blocks, *first)


def experts_kernel(
    core_ref,
    ids_ref,
    mine_ref,
    theirs_ref,
    g_ref,
    wr_ref,
    wg_ref,
    wu_ref,
    wd_ref,
    mix_keep_ref,
    mix_send_ref,
    dx_keep_ref,
    dx_send_ref,
    gates_ref,
    ent_ref,
    a2_s,
    g_s,
    mix_s,
    dx_s,
    back_s,
):
    e = pl.program_id(0)
    tok, width = a2_s.shape
    half = tok // 2
    experts = wr_ref.shape[0]
    lane = lax.broadcasted_iota(jnp.int32, (tok, experts), 1)
    first = ids_ref[:, 0:1]
    second = ids_ref[:, 1:2]

    @pl.when(e == 0)
    def _():
        a2_s[:half, :] = mine_ref[...]
        a2_s[half:, :] = theirs_ref[...]
        for i in range(2):
            start = pl.multiple_of(((core_ref[0] + i) % 2) * half, half)
            g_s[pl.ds(i * half, half), :] = g_ref[pl.ds(start, half), :]
        logits = lax.dot_general(a2_s[...], wr_ref[...], NT, preferred_element_type=F32)
        one = jnp.sum(jnp.where(lane == first, logits, 0.0), axis=1, keepdims=True)
        two = jnp.sum(jnp.where(lane == second, logits, 0.0), axis=1, keepdims=True)
        top = jnp.maximum(one, two)
        one = jnp.exp(one - top)
        two = jnp.exp(two - top)
        total = one + two
        gates_ref[...] = jnp.where(lane == first, one / total, 0.0) + jnp.where(
            lane == second, two / total, 0.0
        )
        mix_s[...] = jnp.zeros(mix_s.shape, F32)
        dx_s[...] = jnp.zeros(dx_s.shape, F32)
        back_s[...] = jnp.zeros(back_s.shape, F32)
        ent_ref[...] = jnp.zeros(ent_ref.shape, BF)

    wg = wg_ref[0]
    wu = wu_ref[0]
    wd = wd_ref[0]
    for i in range(2):
        rows = pl.ds(i * half, half)
        a2 = a2_s[rows, :]
        u = jnp.dot(a2, wg, preferred_element_type=F32)
        w = jnp.dot(a2, wu, preferred_element_type=F32)
        m = lax.dot_general(g_s[rows, :], wd, NT, preferred_element_type=F32)
        here = lane[:half] == e
        gate = jnp.sum(jnp.where(here, gates_ref[rows, :], 0.0), axis=1, keepdims=True)
        pick_one = (ids_ref[rows, 0:1] == e).astype(F32)
        pick_two = (ids_ref[rows, 1:2] == e).astype(F32)
        sig = 1.0 / (1.0 + jnp.exp(-u))
        act = u * sig
        mid = (act * w).astype(BF).astype(F32)
        back = jnp.sum(mid * m, axis=1, keepdims=True) * (pick_one + pick_two)
        back_s[rows, :] += jnp.where(here, back, 0.0)
        mid = mid * gate
        gm = gate * m
        up_back = gm * act
        pre_back = gm * w * sig * (1.0 + u * (1.0 - sig))
        mid_b = mid.astype(BF)
        up_b = up_back.astype(BF)
        pre_b = pre_back.astype(BF)
        mix_s[rows, :] += jnp.dot(mid_b, wd, preferred_element_type=F32)
        dx_s[rows, :] += lax.dot_general(
            pre_b, wg, NT, preferred_element_type=F32
        ) + lax.dot_general(up_b, wu, NT, preferred_element_type=F32)
        for kind, value in enumerate((mid, pre_back, up_back)):
            for c, pick in enumerate((pick_one, pick_two)):
                ent_ref[2 * kind + c, rows, :] += (value * pick).astype(BF)

    @pl.when(e == pl.num_programs(0) - 1)
    def _():
        mix_keep_ref[...] = mix_s[:half, :]
        mix_send_ref[...] = mix_s[half:, :].astype(BF)
        dx_keep_ref[:, :width] = dx_s[:half, :]
        dx_send_ref[:, :width] = dx_s[half:, :].astype(BF)
        pad = jnp.zeros((half, 128 - experts), F32)
        dx_keep_ref[:, width:] = jnp.concatenate([back_s[:half, :], pad], axis=1)
        dx_send_ref[:, width:] = jnp.concatenate([back_s[half:, :], pad], axis=1).astype(BF)


def experts_call(core, ids, mine, theirs, g, wr, wg, wu, wd, first=()):
    half, width = mine.shape
    tok = 2 * half
    experts, _, hidden = wg.shape

    def whole(*shape):
        return pl.BlockSpec(shape, lambda e, *_: (0,) * len(shape))

    def one(*shape):
        return pl.BlockSpec((1,) + shape, lambda e, *_: (e,) + (0,) * len(shape))

    return pl.pallas_call(
        drop_first(experts_kernel, 9, len(first)),
        out_shape=(
            jax.ShapeDtypeStruct((half, width), F32),
            jax.ShapeDtypeStruct((half, width), BF),
            jax.ShapeDtypeStruct((half, width + 128), F32),
            jax.ShapeDtypeStruct((half, width + 128), BF),
            jax.ShapeDtypeStruct((tok, experts), F32),
            jax.ShapeDtypeStruct((6, tok, hidden), BF),
        ),
        grid=(experts,),
        in_specs=[
            pl.BlockSpec(memory_space=pltpu.SMEM),
            whole(tok, 2),
            whole(half, width),
            whole(half, width),
            whole(tok, width),
            whole(experts, width),
            one(width, hidden),
            one(width, hidden),
            one(hidden, width),
        ]
        + anywhere(len(first)),
        out_specs=(
            whole(half, width),
            whole(half, width),
            whole(half, width + 128),
            whole(half, width + 128),
            whole(tok, experts),
            whole(6, tok, hidden),
        ),
        scratch_shapes=[
            pltpu.VMEM((tok, width), BF),
            pltpu.VMEM((tok, width), BF),
            pltpu.VMEM((tok, width), F32),
            pltpu.VMEM((tok, width), F32),
            pltpu.VMEM((tok, experts), F32),
        ],
        compiler_params=params(dimension_semantics=("arbitrary",)),
        name="experts",
        cost_estimate=cost(32),
    )(core, ids, mine, theirs, g, wr, wg, wu, wd, *first)


def expert_grads_kernel(count, base, places, ids_ref, *refs):
    x_refs = refs[0:2]
    g_refs = refs[2:4]
    ents = refs[4 : 4 + count]
    outs, theirs_ref = refs[-4:-1], refs[-1]
    e = (pl.program_id(0) + base).astype(F32)
    cols = outs[0].shape[1]
    sums = [None, None, None]
    for b in range(count):
        half = x_refs[0].shape[2]
        hidden = ents[b].shape[2]
        for i in range(2):
            rows = pl.ds(i * half, half)
            one = jnp.where(ids_ref[places[b], rows, 0:1] == e, 1.0, 0.0).astype(BF)
            two = jnp.where(ids_ref[places[b], rows, 1:2] == e, 1.0, 0.0).astype(BF)
            one = jnp.broadcast_to(one, (half, hidden))
            two = jnp.broadcast_to(two, (half, hidden))
            xt = x_refs[i][b]
            gt = g_refs[i][b]
            for kind in range(3):
                value = ents[b][2 * kind, rows, :] * one + ents[b][2 * kind + 1, rows, :] * two
                term = jnp.dot(gt if kind == 0 else xt, value, preferred_element_type=F32)
                sums[kind] = term if sums[kind] is None else sums[kind] + term
    for kind in range(3):
        outs[kind][0] = sums[kind][:cols]
        theirs_ref[kind, 0] = sums[kind][cols:].astype(BF)


def expert_grads(base, experts, ids, places, xm, xo, gm, go, ents, first=()):
    cols = xm.shape[1] // 2
    hidden = ents[0].shape[-1]
    operands = [ids, xm, xo, gm, go] + list(ents)
    specs = [pl.BlockSpec(x.shape, lambda e, nd=x.ndim: (0,) * nd) for x in operands]
    out_spec = pl.BlockSpec((1, cols, hidden), lambda e: (e, 0, 0))
    kernel = functools.partial(expert_grads_kernel, len(ents), base, places)
    return pl.pallas_call(
        drop_first(kernel, len(operands), len(first)),
        out_shape=(jax.ShapeDtypeStruct((experts, cols, hidden), F32),) * 3
        + (jax.ShapeDtypeStruct((3, experts, cols, hidden), BF),),
        grid=(experts,),
        in_specs=specs + anywhere(len(first)),
        out_specs=(out_spec,) * 3
        + (pl.BlockSpec((3, 1, cols, hidden), lambda e: (0, e, 0, 0)),),
        compiler_params=params(dimension_semantics=("arbitrary",)),
        name="expert_grads",
        cost_estimate=cost(1.2 * experts),
    )(*operands, *first)


def finish_kernel(*refs):
    mine, got_ref, outs = refs[:3], refs[3], refs[-3:]
    for kind in range(3):
        value = mine[kind][0] + got_ref[kind, 0].astype(F32)
        outs[kind][0] = value


def finish(base, experts, mine, got, outs=None, first=()):
    some, cols, hidden = mine[0].shape
    kept = [] if outs is None else list(outs)
    part = pl.BlockSpec((1, cols, hidden), lambda e: (e, 0, 0))
    place = pl.BlockSpec((1, cols, hidden), lambda e: (base + e, 0, 0))
    waits = kept + list(first)
    return pl.pallas_call(
        drop_first(finish_kernel, 4, len(waits)),
        out_shape=(jax.ShapeDtypeStruct((experts, cols, hidden), F32),) * 3,
        grid=(some,),
        in_specs=[part] * 3
        + [pl.BlockSpec((3, 1, cols, hidden), lambda e: (0, e, 0, 0))]
        + anywhere(len(waits)),
        out_specs=(place,) * 3,
        input_output_aliases={4 + i: i for i in range(len(kept))},
        compiler_params=params(dimension_semantics=("arbitrary",)),
        name="finish",
        cost_estimate=cost(3),
    )(*mine, got, *waits)


def my_rows(core_ref, ref):
    half = ref.shape[0] // 2
    return ref[pl.ds(pl.multiple_of(core_ref[0] * half, half), half), :]


def simple(kernel, name, outs, core, *operands, first=()):
    return pl.pallas_call(
        drop_first(kernel, 1 + len(operands), len(first)),
        out_shape=tuple(jax.ShapeDtypeStruct(shape, dtype) for shape, dtype in outs),
        in_specs=[pl.BlockSpec(memory_space=pltpu.SMEM)] + vspec(len(operands)) + anywhere(len(first)),
        out_specs=tuple(vspec(len(outs))),
        compiler_params=params(),
        name=name,
        cost_estimate=cost(5),
    )(core, *operands, *first)


def middle_kernel(core_ref, x_ref, gain_ref, *refs):
    parts, weights = refs[:4], refs[4:8]
    hidden_ref, a2_ref = refs[8:]
    total = my_rows(core_ref, x_ref).astype(F32)
    for part, weight in zip(parts, weights):
        total = total + jnp.dot(part[...], weight[...], preferred_element_type=F32)
    inv = lax.rsqrt(jnp.mean(total * total, axis=-1, keepdims=True) + eps)
    hidden_ref[...] = total
    a2_ref[...] = (total * inv * gain_ref[...][None, :]).astype(BF)


def back_kernel(
    core_ref,
    near_ref,
    got_ref,
    hidden_ref,
    a2_ref,
    gates_ref,
    ids_ref,
    wr_ref,
    gain_ref,
    g_ref,
    grad_ref,
    att_ref,
    misc_ref,
):
    half, width = hidden_ref.shape
    experts = wr_ref.shape[0]
    total = near_ref[...].astype(F32) + got_ref[...].astype(F32)
    gate_back = total[:, width:][:, :experts]
    gates = gates_ref[:half, :]
    lane = lax.broadcasted_iota(jnp.int32, (half, experts), 1)
    picked = (lane == ids_ref[:half, 0:1]) | (lane == ids_ref[:half, 1:2])
    logit = gates * (gate_back - jnp.sum(gates * gate_back, axis=-1, keepdims=True))
    logit = jnp.where(picked, logit, 0.0).astype(BF)
    back = total[:, :width] + jnp.dot(logit, wr_ref[...], preferred_element_type=F32)
    hidden = hidden_ref[...]
    inv = lax.rsqrt(jnp.mean(hidden * hidden, axis=-1, keepdims=True) + eps)
    upstream = my_rows(core_ref, g_ref).astype(F32)
    scaled = back * gain_ref[...][None, :]
    grad = upstream + inv * (
        scaled - hidden * inv * inv * jnp.mean(scaled * hidden, axis=-1, keepdims=True)
    )
    grad_ref[...] = grad
    att_ref[...] = grad.astype(BF)
    misc_ref[:8, :] = lax.dot_general(logit, a2_ref[...], TN, preferred_element_type=F32)
    ffn = jnp.sum(back * hidden * inv, axis=0, keepdims=True)
    misc_ref[8:, :] = jnp.broadcast_to(ffn, (8, width))


def query_back_kernel(core_ref, *refs):
    pairs, weights, out_ref = refs[:2], refs[2:6], refs[6]
    total = None
    for i, weight in enumerate(weights):
        term = lax.dot_general(
            pairs[i // 2][i % 2], weight[...], NT, preferred_element_type=F32
        )
        total = term if total is None else total + term
    out_ref[...] = total


def input_kernel(core_ref, x_ref, gain_ref, grad_ref, query_ref, *refs):
    parts, weights = refs[:4], refs[4:8]
    out_ref, norm_ref = refs[8:]
    back = query_ref[...]
    for part, weight in zip(parts, weights):
        start = weight.shape[1] - part.shape[1]
        back = back + lax.dot_general(
            part[...], weight[:, start:], NT, preferred_element_type=F32
        )
    x = my_rows(core_ref, x_ref).astype(F32)
    inv = lax.rsqrt(jnp.mean(x * x, axis=-1, keepdims=True) + eps)
    scaled = back * gain_ref[...][None, :]
    out_ref[...] = grad_ref[...] + inv * (
        scaled - x * inv * inv * jnp.mean(scaled * x, axis=-1, keepdims=True)
    )
    norm = jnp.sum(back * x * inv, axis=0, keepdims=True)
    norm_ref[...] = jnp.broadcast_to(norm, norm_ref.shape)


def place_kernel(core_ref, mine_ref, theirs_ref, out_ref):
    half = mine_ref.shape[0]
    out_ref[pl.ds(pl.multiple_of(core_ref[0] * half, half), half), :] = mine_ref[...]
    out_ref[pl.ds(pl.multiple_of((1 - core_ref[0]) * half, half), half), :] = theirs_ref[...]


def columns_kernel(waits, owner_ref, core_ref, x_ref, *refs):
    outs, turned = refs[waits:-1], refs[-1]
    per, rows_out, half = outs[0].shape
    side = owner_ref.shape[0] // (per * len(outs))
    cols = rows_out // side
    x = my_rows(core_ref, x_ref) if x_ref.shape[0] != half else x_ref[...]
    turned[...] = x.T
    for r, out_ref in enumerate(outs):
        for i in range(per * side):
            rows = pl.ds(pl.multiple_of(owner_ref[r * per * side + i] * cols, 16), cols)
            out_ref[i // side, (i % side) * cols : (i % side + 1) * cols, :] = turned[rows, :]


def columns(owner, core, x, half, groups, side, first=()):
    n = owner.shape[0]
    width = x.shape[1]
    smem = pl.BlockSpec(memory_space=pltpu.SMEM)
    out = jax.ShapeDtypeStruct((n // (groups * side), side * (width // n), half), BF)
    return pl.pallas_call(
        functools.partial(columns_kernel, len(first)),
        out_shape=(out,) * groups,
        in_specs=[smem, smem] + vspec(1) + [pl.BlockSpec(memory_space=pl.ANY)] * len(first),
        out_specs=tuple(vspec(groups)),
        scratch_shapes=[pltpu.VMEM((width, half), BF)],
        compiler_params=params(),
        name="columns",
        cost_estimate=cost(2.5),
    )(owner, core, x, *first)


def weight_kernel(shape, extra, owner_ref, *refs):
    out_ref, turned, misc_turned = refs[-3:]
    n, cols, _ = out_ref.shape
    at = 0
    column = 0
    for group, pairs in enumerate(shape):
        lefts, rights = refs[at : at + pairs], refs[at + pairs : at + 2 * pairs]
        at += 2 * pairs
        row = 0
        for left in lefts:
            turned[group, :, row : row + left.shape[0]] = left[...].T
            row += left.shape[0]
        right = jnp.concatenate([r[...] for r in rights], axis=0) if pairs > 1 else rights[0][...]
        for i in range(n):
            rows = pl.ds(pl.multiple_of(owner_ref[i] * cols, 16), cols)
            out_ref[i, :, column : column + right.shape[1]] = jnp.dot(
                turned[group, rows, :], right, preferred_element_type=F32
            ).astype(BF)
        column += right.shape[1]
    if extra:
        misc = refs[at][...]
        spare = jnp.zeros((128 - misc.shape[0], misc.shape[1]), F32)
        misc_turned[...] = jnp.concatenate([misc, spare], axis=0).T
        for i in range(n):
            rows = pl.ds(pl.multiple_of(owner_ref[i] * cols, 16), cols)
            out_ref[i, :, column:] = misc_turned[rows, :].astype(BF)


def weight_terms(owner, groups, misc=None, us=4, first=()):
    n = owner.shape[0]
    width = groups[0][0][0].shape[1]
    rows = sum(x.shape[0] for x in groups[0][0])
    out_width = sum(rights[0].shape[1] for _, rights in groups)
    operands = []
    for lefts, rights in groups:
        operands += list(lefts) + list(rights)
    if misc is not None:
        operands.append(misc)
        out_width += 128
    shape = tuple(len(lefts) for lefts, _ in groups)
    return pl.pallas_call(
        drop_first(
            functools.partial(weight_kernel, shape, misc is not None),
            1 + len(operands),
            len(first),
        ),
        out_shape=jax.ShapeDtypeStruct((n, width // n, out_width), BF),
        in_specs=[pl.BlockSpec(memory_space=pltpu.SMEM)]
        + vspec(len(operands))
        + anywhere(len(first)),
        out_specs=vspec(1)[0],
        scratch_shapes=[pltpu.VMEM((len(groups), width, rows), BF), pltpu.VMEM((width, 128), F32)],
        compiler_params=params(),
        name="weight_terms",
        cost_estimate=cost(us),
    )(owner, *operands, *first)


def per_device(
    n_ctx,
    layer_input,
    segment_ids,
    expert_ids,
    norm_gain,
    query_weight,
    key_weight,
    value_weight,
    output_weight,
    ffn_gain,
    router_weight,
    gate_weight,
    up_weight,
    down_weight,
    cotangent,
):
    tok, width = layer_input.shape
    half = tok // 2
    groups = H // KV
    kv_local = key_weight.shape[1] // HD
    heads = kv_local * groups
    kvw = key_weight.shape[1]
    experts = gate_weight.shape[0]
    cols = width // n_ctx
    digits = digits_of(n_ctx)
    keys = rel_keys(digits)
    upper_first = list(range(1, len(digits))) + [0]
    lower_first = list(range(len(digits)))
    me = lax.axis_index("ctx")
    core = lax.axis_index("wa") % 2
    core_arr = jnp.full((1,), core, jnp.int32)
    owner_to = jnp.stack([digit_offset(me, k, digits, 1) for k in keys]).astype(jnp.int32)
    owner_from = jnp.stack([digit_offset(me, k, digits, -1) for k in keys]).astype(jnp.int32)
    gain_one, gain_two = norm_gain, ffn_gain
    router = router_weight.T

    def mine_first(x):
        return jnp.where(core == 0, x, jnp.concatenate([x[half:], x[:half]], axis=0))

    segs = mine_first(segment_ids).astype(BF)
    ids = mine_first(expert_ids)
    extra = jnp.concatenate([segs, ids[:, 0].astype(BF), ids[:, 1].astype(BF)])
    extra = jnp.pad(extra, (0, EXTRA * 2 * kvw - extra.shape[0])).reshape(EXTRA, 2 * kvw)
    a1, q, kv = project(
        core_arr, layer_input, gain_one, query_weight, key_weight, value_weight, extra
    )
    tops = digits[-1][1]
    staged = len(digits) == 2
    side = digits[0][1]
    low, top = digits[0], digits[-1]
    turned_digits = digits[1:] + digits[:1]
    turned_keys = [(k[-1],) + k[:-1] for k in rel_keys(turned_digits)]
    owner_turned = jnp.stack(
        [digit_offset(me, k, digits, -1) for k in turned_keys]
    ).astype(jnp.int32)

    wo_chip = other_chip(output_weight)
    kv_weight = jnp.concatenate([key_weight, value_weight], axis=1)
    kv_core = other_core(kv_weight)
    g_out = columns(owner_to, core_arr, cotangent, half, tops, side, [kv])
    if staged:
        z, y = [kv], []
        for r in range(tops - 1):
            aside = [g_out[0], kv_core] if r == tops - 2 else []
            z_next, y_next = tie([hop(z[r], n_ctx, top), hop(z[r], n_ctx, low)], aside)
            z.append(z_next)
            y.append(y_next)
        y.append(hop(z[-1], n_ctx, low))
        kv_list = [block for pair in zip(z, y) for block in pair]
    else:
        kv_blocks = gather_ctx(kv, n_ctx, digits, upper_first)
        kv_list = [kv_blocks[k] for k in keys]

    g_top = exchange_top(g_out, n_ctx, digits)

    heads_f32, heads_near, heads_far, lse = attend(
        q, kv_list, heads, groups, first=[g_out[0]]
    )
    heads_near, heads_far, wo_chip, *rest = tie(
        [heads_near, heads_far, wo_chip] + list(g_top[1:]), []
    )
    g_top = [g_top[0]] + list(rest)
    wo_parts = [output_weight, other_core(output_weight), wo_chip, other_core(wo_chip)]

    parts = all_parts(heads_near, heads_far)
    g_pieces = exchange_rest(g_top, n_ctx, digits)
    hidden_one, a2_mine = simple(
        middle_kernel,
        "middle",
        [((half, width), F32), ((half, width), BF)],
        core_arr,
        layer_input,
        gain_two,
        *parts,
        *wo_parts,
    )
    a2_far = other_core(a2_mine)
    a2_out = columns(owner_to, core_arr, a2_mine, half, tops, side)
    a2_top = exchange_top(a2_out, n_ctx, digits)
    wq_chip = other_chip(query_weight)

    mix_keep, mix_send, dx_keep, dx_send, gates, ent = experts_call(
        core_arr,
        ids,
        a2_mine,
        a2_far,
        cotangent,
        router,
        gate_weight,
        up_weight,
        down_weight,
        first=[a2_out[0]],
    )
    dx_send, wq_chip, *rest = tie(
        [dx_send, wq_chip] + list(a2_top[1:]), [array for array, _ in g_pieces]
    )
    a2_top = [a2_top[0]] + list(rest)

    near = (dx_keep + other_core(dx_send).astype(F32)).astype(BF)
    got = other_chip(near)
    if staged:
        z = [ent]
        z_next = hop(ent, n_ctx, top)
    wq_parts = [query_weight, other_core(query_weight), wq_chip, other_core(wq_chip)]
    hidden_grad, att_near, misc = simple(
        back_kernel,
        "back",
        [((half, width), F32), ((half, width), BF), ((16, width), F32)],
        core_arr,
        near,
        got,
        hidden_one,
        a2_mine,
        gates,
        ids,
        router,
        gain_two,
        cotangent,
        first=[wq_parts[1], wq_parts[3]],
    )
    att_far = other_core(att_near)
    (mix_send,) = tie([mix_send], [got])
    mix_near = (mix_keep + other_core(mix_send).astype(F32)).astype(BF)
    mix_got = other_chip(mix_near)
    a2_pieces = exchange_rest(a2_top, n_ctx, digits)
    if staged:
        (z_next,) = tie([z_next], [att_near])
        z.append(z_next)
        z_next = hop(z[1], n_ctx, top)

    begin = [att_near, att_far, output_weight, heads_f32]
    sides = [[kv_list[i] for i, k in enumerate(keys) if k[0] == r] for r in range(side)]
    dkv_far, head_grad, delta, dq_going = attend_back(
        q,
        kv_list[0],
        lse,
        [block for r in range(1, side) for block in sides[r]],
        heads,
        groups,
        start=begin,
        end=False,
        first=[mix_near] + ([z[1]] if staged else []),
    )
    (mix_got,) = tie([mix_got], [dq_going])
    dkv_far_got = hop(dkv_far, n_ctx, low)
    ids_all = routes(sides[0], tok, [dq_going])
    a2_stack, a2_stack_far = swapped(a2_pieces, [dq_going])
    g_stack, g_stack_far = swapped(g_pieces, [dq_going])
    terms_o = weight_terms(
        owner_turned,
        [([att_near, att_far], [heads_near, heads_far])],
        misc,
        first=[dq_going, a2_stack, g_stack],
    )
    kv_weight, mix_got = tie([kv_weight, mix_got], [])
    kv_chip = other_chip(kv_weight)
    waits = [ids_all, a2_stack_far, g_stack_far, terms_o]
    if staged:
        (z_next,) = tie([z_next], [terms_o])
        z.append(z_next)
        z_next = hop(z[2], n_ctx, top)
        waits = waits + [z[2]]
    o_sides = cut(terms_o, side)
    o_got = hop(o_sides[1], n_ctx, low)
    dkv_near, dq_near, dq_far = attend_back(
        q,
        kv_list[0],
        lse,
        sides[0],
        heads,
        groups,
        going=[head_grad, delta, dq_going],
        first=waits,
    )
    dkv_far_got, kv_chip = tie([dkv_far_got, kv_chip], [dq_near])
    kv_weights = [kv_weight, kv_core, kv_chip, other_core(kv_chip)]


    dkv_sides = [
        total([dkv_far_got[i : i + 1], dkv_near[i : i + 1]]).astype(BF)
        for i in range(dkv_near.shape[0])
    ]
    if staged:
        dkv_sent = scatter_sends(dkv_sides, n_ctx, top)
    dq_core = other_core(dq_far)

    terms_q = weight_terms(
        owner_turned,
        [([a1], [jnp.concatenate([dq_near, dq_far], axis=0)])],
        first=[dkv_sides[1 % len(dkv_sides)]],
    )
    dq_core, o_got = tie([dq_core, o_got], [terms_q, kv_weights[3]])
    dq_pair = jnp.stack([dq_near, dq_core], axis=0)
    q_sides = cut(terms_q, side)
    q_got = hop(q_sides[1], n_ctx, low)

    if staged:
        z_next, dq_pair = tie([z_next, dq_pair], [terms_q])
        z.append(z_next)
        ents = z
    else:
        upper = gather_ctx(ent, n_ctx, digits, upper_first[:-1])
        ents = [upper[k] for k in keys if k[0] == 0]
    dq_chip = other_chip(dq_pair)
    some = experts // 2
    places = tuple(range(len(ents)))
    shared = [a2_stack, a2_stack_far, g_stack, g_stack_far, ents]
    *grads_a, send_a = expert_grads(0, some, ids_all, places, *shared)
    (q_got,) = tie([q_got], [send_a])
    got_a = hop(send_a, n_ctx, low)
    (dq_chip,) = tie([dq_chip], [send_a])
    (query_back,) = simple(
        query_back_kernel,
        "query_back",
        [((half, width), F32)],
        core_arr,
        dq_pair,
        dq_chip,
        *wq_parts,
    )
    if staged:
        more = tie(dkv_sent[1:], [query_back])
        dkv_own = total([dkv_sent[0]] + list(more))[0].astype(BF)
    else:
        dkv_own = scatter_ctx(jnp.concatenate(dkv_sides, axis=0), n_ctx, digits[1:]).astype(BF)

    terms = jnp.concatenate(
        [total([o_sides[0], o_got]), total([q_sides[0], q_got])], axis=2
    ).astype(BF)
    dkv_parts = all_parts(dkv_own[:half], dkv_own[half:])
    late = weight_terms(owner_from, [([a1], [dkv_own])])
    *grads_b, send_b = expert_grads(
        some,
        experts - some,
        ids_all,
        places,
        *shared,
        first=[send_a, dkv_own, terms, late],
    )
    got_b = hop(send_b, n_ctx, low)
    *dkv_rest, got_a = tie(dkv_parts[1:] + [got_a], [send_b])
    dkv_parts = [dkv_parts[0]] + dkv_rest
    in_mine, norm_row = simple(
        input_kernel,
        "input",
        [((half, width), F32), ((8, width), F32)],
        core_arr,
        layer_input,
        gain_one,
        hidden_grad,
        query_back,
        *dkv_parts,
        *kv_weights,
    )
    in_far = other_core(in_mine)
    done = finish(0, experts, grads_a, got_a, first=[norm_row])
    late, mix_got = tie([late, mix_got], [send_b])
    out_mine = hidden_one + mix_near.astype(F32) + mix_got.astype(F32)
    out_far = other_core(out_mine)
    (layer_output,) = simple(
        place_kernel, "place", [((tok, width), F32)], core_arr, out_mine, out_far
    )
    (input_grad,) = simple(
        place_kernel, "place", [((tok, width), F32)], core_arr, in_mine, in_far
    )
    if staged:
        blocks = cut(terms, tops)
        moving = blocks[1]
        waits = [[send_b], [done[0]], [layer_output]]
        for r in range(2, tops + 1):
            (moving,) = tie([hop(moving, n_ctx, top)], waits[r - 2])
            moving = total([moving, blocks[r % tops]]).astype(BF if r < tops else F32)
        terms_own = moving[0]
    else:
        terms_own = scatter_ctx(terms, n_ctx, digits[1:])
    late_own = scatter_ctx(
        late, n_ctx, digits, lambda at, xs: tie(xs, [done[0]] if at else [layer_output, input_grad])
    )
    norm_rel = norm_row[0].reshape(n_ctx, cols)[owner_from]
    norm_own = scatter_ctx(norm_rel, n_ctx, digits, kind=F32)
    down_grad, gate_grad, up_grad = finish(some, experts, grads_b, got_b, done)

    qw = heads * HD
    output_grad = terms_own[:, :qw].T
    small = jnp.concatenate(
        [terms_own[:, qw : qw + experts + 1], norm_own[:, None]], axis=1
    )
    small = small + other_core(small)
    return (
        layer_output,
        input_grad,
        small[:, experts + 1],
        terms_own[:, qw + 128 :],
        late_own[:, :kvw],
        late_own[:, kvw:],
        output_grad,
        small[:, experts],
        small[:, :experts],
        gate_grad,
        up_grad,
        jnp.swapaxes(down_grad, 1, 2),
    )


def solution(mesh):
    in_specs = (
        P("ctx", None),
        P("ctx"),
        P("ctx", None),
        P(),
        P(None, "wa"),
        P(None, "wa"),
        P(None, "wa"),
        P("wa", None),
        P(),
        P(),
        P(None, None, "wa"),
        P(None, None, "wa"),
        P(None, "wa", None),
        P("ctx", None),
    )
    out_specs = (
        P("ctx", None),
        P("ctx", None),
        P("ctx"),
        P("ctx", "wa"),
        P("ctx", "wa"),
        P("ctx", "wa"),
        P("wa", "ctx"),
        P("ctx"),
        P("ctx", None),
        P(None, "ctx", "wa"),
        P(None, "ctx", "wa"),
        P(None, "wa", "ctx"),
    )
    return jax.shard_map(
        functools.partial(per_device, mesh.shape["ctx"]),
        mesh=mesh,
        in_specs=in_specs,
        out_specs=out_specs,
        check_vma=False,
    )
```

```python
import functools

import jax
import jax.numpy as jnp
from jax import lax
from jax.experimental import pallas as pl
from jax.experimental.pallas import tpu as pltpu
from jax.sharding import PartitionSpec as P

H = 24
KV = 8
HD = 64
eps = 1e-05
NEG = -1e30
F32 = jnp.float32
BF = jnp.bfloat16
VLIM = 60 * 1024 * 1024
EXTRA = 16
NT = (((1,), (1,)), ((), ()))
TN = (((0,), (0,)), ((), ()))


def digits_of(n):
    out = []
    stride = 1
    while n > 1:
        if stride == 1 and n % 2 == 0:
            radix = 2
        elif n % 4 == 0:
            radix = 4
        else:
            radix = n
        out.append((stride, radix))
        stride *= radix
        n //= radix
    return out


def moved(n, digit, shift):
    stride, radix = digit
    pairs = []
    for i in range(n):
        d = (i // stride) % radix
        pairs.append((i, i + ((d + shift) % radix - d) * stride))
    return pairs


def hop(x, n, digit, shift=1):
    return lax.ppermute(x, "ctx", moved(n, digit, shift))


def other_core(x):
    return lax.ppermute(x, "wa", [(i, i ^ 1) for i in range(4)])


def other_chip(x):
    return lax.ppermute(x, "wa", [(i, i ^ 2) for i in range(4)])


def rel_keys(digits):
    keys = [()]
    for _, radix in digits:
        keys = [k + (r,) for r in range(radix) for k in keys]
    return keys


def set_digit(key, at, value):
    return key[:at] + (value,) + key[at + 1 :]


def gather_ctx(x, n, digits, order):
    blocks = {tuple(0 for _ in digits): x}
    for at in order:
        fresh = {}
        for key, block in blocks.items():
            moving = block
            for s in range(1, digits[at][1]):
                moving = hop(moving, n, digits[at])
                fresh[set_digit(key, at, s)] = moving
        blocks.update(fresh)
    return blocks


def scatter_sends(blocks, n, digit):
    return [blocks[0]] + [hop(blocks[r], n, digit, -r) for r in range(1, len(blocks))]


def total(parts):
    return functools.reduce(jnp.add, [x.astype(F32) for x in parts])


def cut(stack, radix):
    per = stack.shape[0] // radix
    return [stack[r * per : (r + 1) * per] for r in range(radix)]


def scatter_ctx(stack, n, order, hold=lambda at, xs: xs, kind=BF):
    moving = stack
    for at in reversed(range(len(order))):
        parts = scatter_sends(cut(moving, order[at][1]), n, order[at])
        parts = parts[:1] + list(hold(at, parts[1:]))
        moving = total(parts)
        if at:
            moving = moving.astype(kind)
    return moving[0]


def stack_kernel(places, *refs):
    for i, (at, unit) in enumerate(places):
        refs[-1][i] = refs[at][unit]


def stacked(pieces):
    arrays = []
    places = []
    for array, unit in pieces:
        at = next((i for i, x in enumerate(arrays) if x is array), None)
        if at is None:
            at = len(arrays)
            arrays.append(array)
        places.append((at, unit))
    shape = (len(pieces),) + arrays[0].shape[1:]
    return pl.pallas_call(
        functools.partial(stack_kernel, tuple(places)),
        out_shape=jax.ShapeDtypeStruct(shape, arrays[0].dtype),
        in_specs=vspec(len(arrays)),
        out_specs=vspec(1)[0],
        compiler_params=params(),
        name="stacked",
        cost_estimate=cost(1),
    )(*arrays)


def exchange_top(groups, n, digits):
    return [groups[0]] + [hop(groups[r], n, digits[-1], r) for r in range(1, len(groups))]


def exchange_rest(groups, n, digits):
    keys = rel_keys(digits[1:])
    n_up = len(keys)
    per = n_up // len(groups)
    parts = {i: (groups[i // per], i % per) for i in range(n_up)}
    for at in reversed(range(1, len(digits) - 1)):
        for s in range(1, digits[at][1]):
            chosen = [i for i, k in enumerate(keys) if k[at - 1] == s]
            bundle = hop(stacked([parts[i] for i in chosen]), n, digits[at], s)
            for place, i in enumerate(chosen):
                parts[i] = (bundle, place)
    return [parts[i] for i in range(n_up)]


def swapped(pieces, first):
    arrays = []
    for array, _ in pieces:
        if not any(array is x for x in arrays):
            arrays.append(array)
    held = tie(arrays, first)
    pieces = [(held[next(i for i, x in enumerate(arrays) if x is a)], u) for a, u in pieces]
    near = stacked(pieces)
    return near, other_core(near)


def digit_offset(me, key, digits, sign):
    place = 0
    for (stride, radix), r in zip(digits, key):
        d = (me // stride) % radix
        place = place + ((d + sign * r) % radix) * stride
    return place


def tie_kernel(*refs):
    pass


def tie(xs, first):
    xs, first = list(xs), list(first)
    return pl.pallas_call(
        tie_kernel,
        out_shape=tuple(jax.ShapeDtypeStruct(x.shape, x.dtype) for x in xs),
        in_specs=anywhere(len(xs) + len(first)),
        out_specs=tuple(anywhere(len(xs))),
        input_output_aliases={i: i for i in range(len(xs))},
        name="tie",
    )(*xs, *first)


def diagonal(x):
    return lax.ppermute(x, "wa", [(i, i ^ 3) for i in range(4)])


def all_parts(near, far):
    return [near, other_core(far), other_chip(near), diagonal(far)]


def cost(us):
    return pl.CostEstimate(flops=int(us * 3e8), bytes_accessed=int(us * 9e5), transcendentals=0)


def params(**kw):
    return pltpu.CompilerParams(vmem_limit_bytes=VLIM, **kw)


def vspec(n):
    return [pl.BlockSpec(memory_space=pltpu.VMEM)] * n


def drop_first(kernel, at, count):
    if not count:
        return kernel

    def waiting(*refs):
        kernel(*refs[:at], *refs[at + count :])

    return waiting


def anywhere(count):
    return [pl.BlockSpec(memory_space=pl.ANY)] * count


def project_kernel(core_ref, x_ref, gain_ref, wq_ref, wk_ref, wv_ref, extra_ref, a1_ref, q_ref, kv_ref):
    tok = x_ref.shape[0]
    half = tok // 2
    kvw = wk_ref.shape[1]
    for i in range(2):
        start = pl.multiple_of(((core_ref[0] + i) % 2) * half, half)
        x = x_ref[pl.ds(start, half), :].astype(F32)
        inv = lax.rsqrt(jnp.mean(x * x, axis=-1, keepdims=True) + eps)
        a1 = (x * inv * gain_ref[...][None, :]).astype(BF)
        rows = pl.ds(i * half, half)
        a1_ref[rows, :] = a1
        kv_ref[rows, :kvw] = jnp.dot(a1, wk_ref[...], preferred_element_type=F32).astype(BF)
        kv_ref[rows, kvw:] = jnp.dot(a1, wv_ref[...], preferred_element_type=F32).astype(BF)
        q = jnp.dot(a1, wq_ref[...], preferred_element_type=F32).astype(BF)
        q_ref[rows, :] = (q.astype(F32) * HD ** (-0.5)).astype(BF)
    kv_ref[pl.ds(tok, EXTRA), :] = extra_ref[...]


def project(core, x, gain, wq, wk, wv, extra):
    tok, width = x.shape
    return pl.pallas_call(
        project_kernel,
        out_shape=(
            jax.ShapeDtypeStruct((tok, width), BF),
            jax.ShapeDtypeStruct((tok, wq.shape[1]), BF),
            jax.ShapeDtypeStruct((tok + EXTRA, 2 * wk.shape[1]), BF),
        ),
        in_specs=[pl.BlockSpec(memory_space=pltpu.SMEM)] + vspec(6),
        out_specs=tuple(vspec(3)),
        compiler_params=params(),
        name="project",
        cost_estimate=cost(5),
    )(core, x, gain, wq, wk, wv, extra)


def seg_onehot(row):
    lane = lax.broadcasted_iota(jnp.int32, (16, row.shape[1]), 0).astype(F32)
    return jnp.where(lane == row, 1.0, 0.0).astype(BF)


def seg_rows_of(block, tok):
    width = block.shape[1]
    return [
        block[tok : tok + EXTRA, :].astype(F32)[i : i + 1, :] for i in range(tok // width)
    ]


ROWS = 256


def block_segs(block, tok):
    return jnp.concatenate(seg_rows_of(block, tok), axis=1)


def turned_groups(x, out, heads, groups):
    x = x.astype(F32).T.astype(BF)
    pairs = heads // groups
    for r in range(x.shape[1] // ROWS):
        for h in range(heads):
            n, g = h // groups, h % groups
            out[r * pairs + n, :, g * ROWS : (g + 1) * ROWS] = x[
                h * HD : (h + 1) * HD, r * ROWS : (r + 1) * ROWS
            ]


def straight_groups(x, out, heads, groups):
    pairs = heads // groups
    for r in range(x.shape[0] // ROWS):
        for h in range(heads):
            n, g = h // groups, h % groups
            out[r * pairs + n, g * ROWS : (g + 1) * ROWS, :] = x[
                r * ROWS : (r + 1) * ROWS, h * HD : (h + 1) * HD
            ]


def head_rows(ref, r, n, groups):
    rows = slice(r * ROWS, (r + 1) * ROWS)
    return jnp.concatenate(
        [ref[h : h + 1, rows] for h in range(n * groups, (n + 1) * groups)], axis=1
    )


def visit_tiles(kv_s, own, tok, body, before, behind):
    tiles = tok // ROWS
    lows = [jnp.min(own[:, r * ROWS : (r + 1) * ROWS]) for r in range(tiles)]
    highs = [jnp.max(own[:, r * ROWS : (r + 1) * ROWS]) for r in range(tiles)]

    def visit(b, carry):
        seg = block_segs(kv_s[b], tok)
        lo = jnp.min(seg)
        hi = jnp.max(seg)
        before(b)
        for r in range(tiles):
            plain = (lo == hi) & (lows[r] == highs[r]) & (lo == lows[r])
            touch = (lo <= highs[r]) & (lows[r] <= hi)
            pl.when(plain)(functools.partial(body, b, r, False))
            pl.when(touch & jnp.logical_not(plain))(functools.partial(body, b, r, True))
        behind(b)
        return carry

    lax.fori_loop(0, kv_s.shape[0], visit, 0)


def same_tile(block, own_hot, r, tok, groups):
    same = lax.dot_general(
        seg_onehot(block_segs(block, tok)),
        own_hot[:, r * ROWS : (r + 1) * ROWS],
        TN,
        preferred_element_type=F32,
    )
    return jnp.concatenate([same] * groups, axis=1) > 0.5


def attend_kernel(nb, heads, groups, *refs):
    q_ref = refs[0]
    kv_refs = refs[1 : 1 + nb]
    hf_ref, near_ref, far_ref, lse_ref = refs[1 + nb : 5 + nb]
    kv_s, q_s, m_s, acc_s = refs[5 + nb :]
    tok = q_ref.shape[0]
    kvw = kv_refs[0].shape[1] // 2
    pairs = heads // groups
    for b in range(nb):
        kv_s[b] = kv_refs[b][...]
    turned_groups(q_ref[...], q_s, heads, groups)
    own = block_segs(kv_s[0], tok)
    own_hot = seg_onehot(own)
    m_s[...] = jnp.full(m_s.shape, NEG, F32)
    acc_s[...] = jnp.zeros(acc_s.shape, F32)

    def body(b, r, masked):
        block = kv_s[b]
        if masked:
            same = same_tile(block, own_hot, r, tok, groups)
        scores = []
        for n in range(pairs):
            k = block[:tok, n * HD : (n + 1) * HD]
            s = jnp.dot(k, q_s[r * pairs + n], preferred_element_type=F32)
            scores.append(jnp.where(same, s, NEG) if masked else s)
        old = [m_s[r * pairs + n : r * pairs + n + 1, :] for n in range(pairs)]
        new = [
            jnp.maximum(old[n], jnp.max(scores[n], axis=0, keepdims=True)) for n in range(pairs)
        ]
        for n in range(pairs):
            i = r * pairs + n
            m_s[i : i + 1, :] = new[n]
            p = jnp.exp(scores[n] - new[n]).astype(BF)
            v = block[:tok, kvw + n * HD : kvw + (n + 1) * HD]
            v = jnp.concatenate([v, jnp.ones((tok, 16), BF)], axis=1)
            acc_s[i] = acc_s[i] * jnp.exp(old[n] - new[n]) + lax.dot_general(
                v, p, TN, preferred_element_type=F32
            )

    def nothing(b):
        pass

    visit_tiles(kv_s, own, tok, body, nothing, nothing)
    tiles = []
    for r in range(tok // ROWS):
        rows = []
        for n in range(pairs):
            i = r * pairs + n
            total = acc_s[i, HD : HD + 1, :]
            out = acc_s[i, :HD, :] / total
            lse = m_s[i : i + 1, :] + jnp.log(total)
            for g in range(groups):
                h = n * groups + g
                lanes = slice(g * ROWS, (g + 1) * ROWS)
                rows.append(out[:, lanes])
                lse_ref[h : h + 1, r * ROWS : (r + 1) * ROWS] = lse[:, lanes]
        tiles.append(jnp.concatenate(rows, axis=0))
    out = jnp.concatenate(tiles, axis=1).T
    hf_ref[...] = out
    near_ref[...] = out[: tok // 2].astype(BF)
    far_ref[...] = out[tok // 2 :].astype(BF)


def attend(q, blocks, heads, groups, first=()):
    tok = q.shape[0]
    nb = len(blocks)
    units = (tok // ROWS) * (heads // groups)
    return pl.pallas_call(
        drop_first(functools.partial(attend_kernel, nb, heads, groups), 1 + nb, len(first)),
        out_shape=(
            jax.ShapeDtypeStruct((tok, heads * HD), F32),
            jax.ShapeDtypeStruct((tok // 2, heads * HD), BF),
            jax.ShapeDtypeStruct((tok // 2, heads * HD), BF),
            jax.ShapeDtypeStruct((8, tok), F32),
        ),
        in_specs=vspec(1 + nb) + anywhere(len(first)),
        out_specs=tuple(vspec(4)),
        scratch_shapes=[
            pltpu.VMEM((nb,) + blocks[0].shape, BF),
            pltpu.VMEM((units, HD, groups * ROWS), BF),
            pltpu.VMEM((max(8, units), groups * ROWS), F32),
            pltpu.VMEM((units, HD + 16, groups * ROWS), F32),
        ],
        compiler_params=params(),
        name="attend",
        cost_estimate=cost(27),
    )(q, *blocks, *first)


def attend_back_kernel(nb, heads, groups, start, end, *refs):
    q_ref, own_ref, lse_ref = refs[:3]
    kv_refs = refs[3 : 3 + nb]
    at = 3 + nb
    if start:
        att_near_ref, att_far_ref, wo_ref, hf_ref = refs[at : at + 4]
        at += 4
    else:
        grad_in_ref, delta_in_ref, dq_in_ref = refs[at : at + 3]
        at += 3
    dkv_ref = refs[at]
    at += 1
    if start:
        grad_ref, delta_ref = refs[at : at + 2]
        at += 2
    if end:
        dq_near_ref, dq_far_ref = refs[at : at + 2]
        at += 2
    else:
        dq_out_ref = refs[at]
        at += 1
    kv_s, qt_s, q_s, dot_s, do_s, delta_s, dq_s, acc_s = refs[at:]
    tok = q_ref.shape[0]
    kvw = own_ref.shape[1] // 2
    key_heads = heads // groups
    if start:
        grad = jnp.concatenate(
            [
                lax.dot_general(ref[...], wo_ref[...], NT, preferred_element_type=F32)
                for ref in (att_near_ref, att_far_ref)
            ],
            axis=0,
        ).astype(BF)
        grad_ref[...] = grad
        prod = (grad.astype(F32) * hf_ref[...]).T
        for h in range(heads):
            delta_s[h : h + 1, :] = jnp.sum(prod[h * HD : (h + 1) * HD, :], axis=0, keepdims=True)
        delta_ref[...] = delta_s[...]
        dq_s[...] = jnp.zeros(dq_s.shape, F32)
    else:
        grad = grad_in_ref[...]
        delta_s[...] = delta_in_ref[...]
        dq_s[...] = dq_in_ref[...]
    for b in range(nb):
        kv_s[b] = kv_refs[b][...]
    turned_groups(q_ref[...], qt_s, heads, groups)
    straight_groups(q_ref[...], q_s, heads, groups)
    turned_groups(grad, dot_s, heads, groups)
    straight_groups(grad, do_s, heads, groups)
    own = block_segs(own_ref[...], tok)
    own_hot = seg_onehot(own)

    def body(b, r, masked):
        block = kv_s[b]
        if masked:
            same = same_tile(block, own_hot, r, tok, groups)
        for n in range(key_heads):
            i = r * key_heads + n
            k = block[:tok, n * HD : (n + 1) * HD]
            v = block[:tok, kvw + n * HD : kvw + (n + 1) * HD]
            s = jnp.dot(k, qt_s[i], preferred_element_type=F32)
            dp = jnp.dot(v, dot_s[i], preferred_element_type=F32)
            p = jnp.exp(s - head_rows(lse_ref, r, n, groups))
            if masked:
                p = jnp.where(same, p, 0.0)
            ds = (p * (dp - head_rows(delta_s, r, n, groups))).astype(BF)
            acc_s[n] += jnp.dot(ds, q_s[i], preferred_element_type=F32)
            acc_s[key_heads + n] += jnp.dot(p.astype(BF), do_s[i], preferred_element_type=F32)
            dq_s[i] += lax.dot_general(k, ds, TN, preferred_element_type=F32)

    def before(b):
        acc_s[...] = jnp.zeros(acc_s.shape, F32)

    def behind(b):
        sums = jnp.concatenate([acc_s[i] for i in range(2 * key_heads)], axis=1)
        dkv_ref[b] = sums.astype(BF)

    visit_tiles(kv_s, own, tok, body, before, behind)
    if end:
        tiles = []
        for r in range(tok // ROWS):
            rows = [
                dq_s[r * key_heads + h // groups, :, (h % groups) * ROWS : (h % groups + 1) * ROWS]
                for h in range(heads)
            ]
            tiles.append(jnp.concatenate(rows, axis=0))
        out = (jnp.concatenate(tiles, axis=1).T * HD ** (-0.5)).astype(BF)
        dq_near_ref[...] = out[: tok // 2]
        dq_far_ref[...] = out[tok // 2 :]
    else:
        dq_out_ref[...] = dq_s[...]


def attend_back(q, own, lse, blocks, heads, groups, start=None, going=None, end=True, first=()):
    tok = q.shape[0]
    nb = len(blocks)
    width = heads * HD
    key_heads = heads // groups
    units = (tok // ROWS) * key_heads
    operands = [q, own, lse] + list(blocks) + list(start if start is not None else going)
    outs = [((nb, tok, own.shape[1]), BF)]
    if start is not None:
        outs += [((tok, width), BF), ((8, tok), F32)]
    outs += [((tok // 2, width), BF)] * 2 if end else [((units, HD, groups * ROWS), F32)]
    kernel = functools.partial(
        attend_back_kernel, nb, heads, groups, start is not None, end
    )
    return pl.pallas_call(
        drop_first(kernel, len(operands), len(first)),
        out_shape=tuple(jax.ShapeDtypeStruct(shape, dtype) for shape, dtype in outs),
        in_specs=vspec(len(operands)) + anywhere(len(first)),
        out_specs=tuple(vspec(len(outs))),
        scratch_shapes=[
            pltpu.VMEM((nb,) + blocks[0].shape, BF),
            pltpu.VMEM((units, HD, groups * ROWS), BF),
            pltpu.VMEM((units, groups * ROWS, HD), BF),
            pltpu.VMEM((units, HD, groups * ROWS), BF),
            pltpu.VMEM((units, groups * ROWS, HD), BF),
            pltpu.VMEM((8, tok), F32),
            pltpu.VMEM((units, HD, groups * ROWS), F32),
            pltpu.VMEM((2 * key_heads, tok, HD), F32),
        ],
        compiler_params=params(),
        name="attend_back",
        cost_estimate=cost(4.5 * nb),
    )(*operands, *first)


def routes_kernel(at, *refs):
    out_ref = refs[-1]
    tok = out_ref.shape[1]
    for b, ref in enumerate(refs[:-1]):
        rows = ref[tok : tok + EXTRA, :].astype(F32)
        both = [
            jnp.concatenate([rows[i : i + 1, :] for i in range(c * at, (c + 1) * at)], axis=1)
            for c in (1, 2)
        ]
        out_ref[b] = jnp.concatenate(both + [jnp.zeros((6, tok), F32)], axis=0).T


def routes(blocks, tok, first=()):
    return pl.pallas_call(
        drop_first(
            functools.partial(routes_kernel, tok // blocks[0].shape[1]), len(blocks), len(first)
        ),
        out_shape=jax.ShapeDtypeStruct((len(blocks), tok, 8), F32),
        in_specs=vspec(len(blocks)) + anywhere(len(first)),
        out_specs=vspec(1)[0],
        compiler_params=params(),
        name="routes",
        cost_estimate=cost(2),
    )(*blocks, *first)


def masks(ids_ref, rows, e, count, width):
    return [
        jnp.broadcast_to(
            jnp.where(ids_ref[rows, c : c + 1] == e, 1.0, 0.0).astype(BF), (count, width)
        )
        for c in range(2)
    ]


def experts_kernel(
    per,
    core_ref,
    ids_ref,
    mine_ref,
    theirs_ref,
    g_ref,
    wr_ref,
    wg_ref,
    wu_ref,
    wd_ref,
    dx_keep_ref,
    dx_send_ref,
    gates_ref,
    ent_ref,
    a2_s,
    g_s,
    dx_s,
    back_s,
):
    step = pl.program_id(0)
    tok, width = a2_s.shape
    half = tok // 2
    experts = wr_ref.shape[0]
    lane = lax.broadcasted_iota(jnp.int32, (tok, experts), 1)
    first = ids_ref[:, 0:1]
    second = ids_ref[:, 1:2]

    @pl.when(step == 0)
    def _():
        a2_s[:half, :] = mine_ref[...]
        a2_s[half:, :] = theirs_ref[...]
        for i in range(2):
            start = pl.multiple_of(((core_ref[0] + i) % 2) * half, half)
            g_s[pl.ds(i * half, half), :] = g_ref[pl.ds(start, half), :]
        logits = lax.dot_general(a2_s[...], wr_ref[...], NT, preferred_element_type=F32)
        one = jnp.sum(jnp.where(lane == first, logits, 0.0), axis=1, keepdims=True)
        two = jnp.sum(jnp.where(lane == second, logits, 0.0), axis=1, keepdims=True)
        top = jnp.maximum(one, two)
        one = jnp.exp(one - top)
        two = jnp.exp(two - top)
        both = one + two
        gates_ref[...] = jnp.where(lane == first, one / both, 0.0) + jnp.where(
            lane == second, two / both, 0.0
        )
        dx_s[...] = jnp.zeros(dx_s.shape, F32)
        back_s[...] = jnp.zeros(back_s.shape, F32)
        ent_ref[...] = jnp.zeros(ent_ref.shape, BF)

    for i in range(2):
        rows = pl.ds(i * half, half)
        a2 = a2_s[rows, :]
        g = g_s[rows, :]
        products = []
        for j in range(per):
            u = jnp.dot(a2, wg_ref[j], preferred_element_type=F32)
            w = jnp.dot(a2, wu_ref[j], preferred_element_type=F32)
            m = lax.dot_general(g, wd_ref[j], NT, preferred_element_type=F32)
            products.append((u, w, m))
        dx = None
        back_all = None
        parts = [None] * 6
        for j in range(per):
            e = step * per + j
            u, w, m = products[j]
            here = lane[:half] == e
            gate = jnp.sum(jnp.where(here, gates_ref[rows, :], 0.0), axis=1, keepdims=True)
            picked = (ids_ref[rows, 0:1] == e) | (ids_ref[rows, 1:2] == e)
            sig = 1.0 / (1.0 + jnp.exp(-u))
            act = u * sig
            mid = (act * w).astype(BF).astype(F32)
            back = jnp.sum(mid * m, axis=1, keepdims=True)
            back = jnp.where(here & picked, back, 0.0)
            back_all = back if back_all is None else back_all + back
            gm = gate * m
            up_back = (gm * act).astype(BF)
            pre_back = (gm * w * sig * (1.0 + u * (1.0 - sig))).astype(BF)
            term = lax.dot_general(
                pre_back, wg_ref[j], NT, preferred_element_type=F32
            ) + lax.dot_general(up_back, wu_ref[j], NT, preferred_element_type=F32)
            dx = term if dx is None else dx + term
            chosen = masks(ids_ref, rows, e, half, u.shape[1])
            for kind, value in enumerate(((mid * gate).astype(BF), pre_back, up_back)):
                for c in range(2):
                    part = value * chosen[c]
                    unit = 2 * kind + c
                    parts[unit] = part if parts[unit] is None else parts[unit] + part
        dx_s[rows, :] += dx
        back_s[rows, :] += back_all
        for unit in range(6):
            ent_ref[unit, rows, :] += parts[unit]

    @pl.when(step == pl.num_programs(0) - 1)
    def _():
        dx_keep_ref[:, :width] = dx_s[:half, :]
        dx_send_ref[:, :width] = dx_s[half:, :].astype(BF)
        pad = jnp.zeros((half, 128 - experts), F32)
        dx_keep_ref[:, width:] = jnp.concatenate([back_s[:half, :], pad], axis=1)
        dx_send_ref[:, width:] = jnp.concatenate([back_s[half:, :], pad], axis=1).astype(BF)


def whole(*shape):
    return pl.BlockSpec(shape, lambda e: (0,) * len(shape))


def some_of(*shape):
    return pl.BlockSpec(shape, lambda e: (e,) + (0,) * (len(shape) - 1))


def experts_call(core, ids, mine, theirs, g, wr, wg, wu, wd, first=()):
    half, width = mine.shape
    tok = 2 * half
    experts, _, hidden = wg.shape
    per = 2
    return pl.pallas_call(
        drop_first(functools.partial(experts_kernel, per), 9, len(first)),
        out_shape=(
            jax.ShapeDtypeStruct((half, width + 128), F32),
            jax.ShapeDtypeStruct((half, width + 128), BF),
            jax.ShapeDtypeStruct((tok, experts), F32),
            jax.ShapeDtypeStruct((6, tok, hidden), BF),
        ),
        grid=(experts // per,),
        in_specs=[
            pl.BlockSpec(memory_space=pltpu.SMEM),
            whole(tok, 2),
            whole(half, width),
            whole(half, width),
            whole(tok, width),
            whole(experts, width),
            some_of(per, width, hidden),
            some_of(per, width, hidden),
            some_of(per, hidden, width),
        ]
        + anywhere(len(first)),
        out_specs=(
            whole(half, width + 128),
            whole(half, width + 128),
            whole(tok, experts),
            whole(6, tok, hidden),
        ),
        scratch_shapes=[
            pltpu.VMEM((tok, width), BF),
            pltpu.VMEM((tok, width), BF),
            pltpu.VMEM((tok, width), F32),
            pltpu.VMEM((tok, experts), F32),
        ],
        compiler_params=params(dimension_semantics=("arbitrary",)),
        name="experts",
        cost_estimate=cost(26),
    )(core, ids, mine, theirs, g, wr, wg, wu, wd, *first)


def mix_kernel(per, ids_ref, ent_ref, wd_ref, keep_ref, send_ref, mix_s):
    step = pl.program_id(0)
    half, width = keep_ref.shape

    @pl.when(step == 0)
    def _():
        mix_s[...] = jnp.zeros(mix_s.shape, F32)

    for i in range(2):
        rows = pl.ds(i * half, half)
        out = None
        for j in range(per):
            one, two = masks(ids_ref, rows, step * per + j, half, ent_ref.shape[2])
            mid = ent_ref[0, rows, :] * one + ent_ref[1, rows, :] * two
            term = jnp.dot(mid, wd_ref[j], preferred_element_type=F32)
            out = term if out is None else out + term
        mix_s[rows, :] += out

    @pl.when(step == pl.num_programs(0) - 1)
    def _():
        keep_ref[...] = mix_s[:half, :]
        send_ref[...] = mix_s[half:, :].astype(BF)


def mix_call(ids, ent, wd, first=()):
    _, tok, hidden = ent.shape
    experts, _, width = wd.shape
    half = tok // 2
    per = 2
    return pl.pallas_call(
        drop_first(functools.partial(mix_kernel, per), 3, len(first)),
        out_shape=(
            jax.ShapeDtypeStruct((half, width), F32),
            jax.ShapeDtypeStruct((half, width), BF),
        ),
        grid=(experts // per,),
        in_specs=[
            whole(tok, 2),
            pl.BlockSpec((2, tok, hidden), lambda e: (0, 0, 0)),
            some_of(per, hidden, width),
        ]
        + anywhere(len(first)),
        out_specs=(whole(half, width), whole(half, width)),
        scratch_shapes=[pltpu.VMEM((tok, width), F32)],
        compiler_params=params(dimension_semantics=("arbitrary",)),
        name="mix",
        cost_estimate=cost(8),
    )(ids, ent, wd, *first)


def expert_grads_kernel(count, base, places, ids_ref, *refs):
    x_refs = refs[0:2]
    g_refs = refs[2:4]
    ents = refs[4 : 4 + count]
    outs, theirs_ref = refs[-4:-1], refs[-1]
    e = (pl.program_id(0) + base).astype(F32)
    cols = outs[0].shape[1]
    sums = [None, None, None]
    for b in range(count):
        half = x_refs[0].shape[2]
        hidden = ents[b].shape[2]
        for i in range(2):
            rows = pl.ds(i * half, half)
            one = jnp.where(ids_ref[places[b], rows, 0:1] == e, 1.0, 0.0).astype(BF)
            two = jnp.where(ids_ref[places[b], rows, 1:2] == e, 1.0, 0.0).astype(BF)
            one = jnp.broadcast_to(one, (half, hidden))
            two = jnp.broadcast_to(two, (half, hidden))
            xt = x_refs[i][b]
            gt = g_refs[i][b]
            for kind in range(3):
                value = ents[b][2 * kind, rows, :] * one + ents[b][2 * kind + 1, rows, :] * two
                term = jnp.dot(gt if kind == 0 else xt, value, preferred_element_type=F32)
                sums[kind] = term if sums[kind] is None else sums[kind] + term
    for kind in range(3):
        outs[kind][0] = sums[kind][:cols]
        theirs_ref[kind, 0] = sums[kind][cols:].astype(BF)


def expert_grads(base, experts, ids, places, xm, xo, gm, go, ents, first=()):
    cols = xm.shape[1] // 2
    hidden = ents[0].shape[-1]
    operands = [ids, xm, xo, gm, go] + list(ents)
    specs = [pl.BlockSpec(x.shape, lambda e, nd=x.ndim: (0,) * nd) for x in operands]
    out_spec = pl.BlockSpec((1, cols, hidden), lambda e: (e, 0, 0))
    kernel = functools.partial(expert_grads_kernel, len(ents), base, places)
    return pl.pallas_call(
        drop_first(kernel, len(operands), len(first)),
        out_shape=(jax.ShapeDtypeStruct((experts, cols, hidden), F32),) * 3
        + (jax.ShapeDtypeStruct((3, experts, cols, hidden), BF),),
        grid=(experts,),
        in_specs=specs + anywhere(len(first)),
        out_specs=(out_spec,) * 3
        + (pl.BlockSpec((3, 1, cols, hidden), lambda e: (0, e, 0, 0)),),
        compiler_params=params(dimension_semantics=("arbitrary",)),
        name="expert_grads",
        cost_estimate=cost(1.2 * experts),
    )(*operands, *first)


def finish_kernel(*refs):
    mine, got_ref, outs = refs[:3], refs[3], refs[-3:]
    for kind in range(3):
        value = mine[kind][0] + got_ref[kind, 0].astype(F32)
        outs[kind][0] = value


def finish(base, experts, mine, got, outs=None, first=()):
    some, cols, hidden = mine[0].shape
    kept = [] if outs is None else list(outs)
    part = pl.BlockSpec((1, cols, hidden), lambda e: (e, 0, 0))
    place = pl.BlockSpec((1, cols, hidden), lambda e: (base + e, 0, 0))
    waits = kept + list(first)
    return pl.pallas_call(
        drop_first(finish_kernel, 4, len(waits)),
        out_shape=(jax.ShapeDtypeStruct((experts, cols, hidden), F32),) * 3,
        grid=(some,),
        in_specs=[part] * 3
        + [pl.BlockSpec((3, 1, cols, hidden), lambda e: (0, e, 0, 0))]
        + anywhere(len(waits)),
        out_specs=(place,) * 3,
        input_output_aliases={4 + i: i for i in range(len(kept))},
        compiler_params=params(dimension_semantics=("arbitrary",)),
        name="finish",
        cost_estimate=cost(3),
    )(*mine, got, *waits)


def my_rows(core_ref, ref):
    half = ref.shape[0] // 2
    return ref[pl.ds(pl.multiple_of(core_ref[0] * half, half), half), :]


def simple(kernel, name, outs, core, *operands, first=()):
    return pl.pallas_call(
        drop_first(kernel, 1 + len(operands), len(first)),
        out_shape=tuple(jax.ShapeDtypeStruct(shape, dtype) for shape, dtype in outs),
        in_specs=[pl.BlockSpec(memory_space=pltpu.SMEM)] + vspec(len(operands)) + anywhere(len(first)),
        out_specs=tuple(vspec(len(outs))),
        compiler_params=params(),
        name=name,
        cost_estimate=cost(5),
    )(core, *operands, *first)


def middle_kernel(core_ref, x_ref, gain_ref, *refs):
    parts, weights = refs[:4], refs[4:8]
    hidden_ref, a2_ref = refs[8:]
    total = my_rows(core_ref, x_ref).astype(F32)
    for part, weight in zip(parts, weights):
        total = total + jnp.dot(part[...], weight[...], preferred_element_type=F32)
    inv = lax.rsqrt(jnp.mean(total * total, axis=-1, keepdims=True) + eps)
    hidden_ref[...] = total
    a2_ref[...] = (total * inv * gain_ref[...][None, :]).astype(BF)


def back_kernel(
    core_ref,
    near_ref,
    got_ref,
    hidden_ref,
    a2_ref,
    gates_ref,
    ids_ref,
    wr_ref,
    gain_ref,
    g_ref,
    grad_ref,
    att_ref,
    misc_ref,
):
    half, width = hidden_ref.shape
    experts = wr_ref.shape[0]
    total = near_ref[...].astype(F32) + got_ref[...].astype(F32)
    gate_back = total[:, width:][:, :experts]
    gates = gates_ref[:half, :]
    lane = lax.broadcasted_iota(jnp.int32, (half, experts), 1)
    picked = (lane == ids_ref[:half, 0:1]) | (lane == ids_ref[:half, 1:2])
    logit = gates * (gate_back - jnp.sum(gates * gate_back, axis=-1, keepdims=True))
    logit = jnp.where(picked, logit, 0.0).astype(BF)
    back = total[:, :width] + jnp.dot(logit, wr_ref[...], preferred_element_type=F32)
    hidden = hidden_ref[...]
    inv = lax.rsqrt(jnp.mean(hidden * hidden, axis=-1, keepdims=True) + eps)
    upstream = my_rows(core_ref, g_ref).astype(F32)
    scaled = back * gain_ref[...][None, :]
    grad = upstream + inv * (
        scaled - hidden * inv * inv * jnp.mean(scaled * hidden, axis=-1, keepdims=True)
    )
    grad_ref[...] = grad
    att_ref[...] = grad.astype(BF)
    misc_ref[:8, :] = lax.dot_general(logit, a2_ref[...], TN, preferred_element_type=F32)
    ffn = jnp.sum(back * hidden * inv, axis=0, keepdims=True)
    misc_ref[8:, :] = jnp.broadcast_to(ffn, (8, width))


def query_back_kernel(core_ref, *refs):
    pairs, weights, out_ref = refs[:2], refs[2:6], refs[6]
    total = None
    for i, weight in enumerate(weights):
        term = lax.dot_general(
            pairs[i // 2][i % 2], weight[...], NT, preferred_element_type=F32
        )
        total = term if total is None else total + term
    out_ref[...] = total


def input_kernel(core_ref, x_ref, gain_ref, grad_ref, query_ref, *refs):
    parts, weights = refs[:4], refs[4:8]
    out_ref, norm_ref = refs[8:]
    back = query_ref[...]
    for part, weight in zip(parts, weights):
        start = weight.shape[1] - part.shape[1]
        back = back + lax.dot_general(
            part[...], weight[:, start:], NT, preferred_element_type=F32
        )
    x = my_rows(core_ref, x_ref).astype(F32)
    inv = lax.rsqrt(jnp.mean(x * x, axis=-1, keepdims=True) + eps)
    scaled = back * gain_ref[...][None, :]
    out_ref[...] = grad_ref[...] + inv * (
        scaled - x * inv * inv * jnp.mean(scaled * x, axis=-1, keepdims=True)
    )
    norm = jnp.sum(back * x * inv, axis=0, keepdims=True)
    norm_ref[...] = jnp.broadcast_to(norm, norm_ref.shape)


def place_kernel(core_ref, mine_ref, theirs_ref, out_ref):
    half = mine_ref.shape[0]
    out_ref[pl.ds(pl.multiple_of(core_ref[0] * half, half), half), :] = mine_ref[...]
    out_ref[pl.ds(pl.multiple_of((1 - core_ref[0]) * half, half), half), :] = theirs_ref[...]


def columns_kernel(waits, owner_ref, core_ref, x_ref, *refs):
    outs, turned = refs[waits:-1], refs[-1]
    per, rows_out, half = outs[0].shape
    side = owner_ref.shape[0] // (per * len(outs))
    cols = rows_out // side
    x = my_rows(core_ref, x_ref) if x_ref.shape[0] != half else x_ref[...]
    turned[...] = x.T
    for r, out_ref in enumerate(outs):
        for i in range(per * side):
            rows = pl.ds(pl.multiple_of(owner_ref[r * per * side + i] * cols, 16), cols)
            out_ref[i // side, (i % side) * cols : (i % side + 1) * cols, :] = turned[rows, :]


def columns(owner, core, x, half, groups, side, first=()):
    n = owner.shape[0]
    width = x.shape[1]
    smem = pl.BlockSpec(memory_space=pltpu.SMEM)
    out = jax.ShapeDtypeStruct((n // (groups * side), side * (width // n), half), BF)
    return pl.pallas_call(
        functools.partial(columns_kernel, len(first)),
        out_shape=(out,) * groups,
        in_specs=[smem, smem] + vspec(1) + [pl.BlockSpec(memory_space=pl.ANY)] * len(first),
        out_specs=tuple(vspec(groups)),
        scratch_shapes=[pltpu.VMEM((width, half), BF)],
        compiler_params=params(),
        name="columns",
        cost_estimate=cost(2.5),
    )(owner, core, x, *first)


def weight_kernel(shape, extra, owner_ref, *refs):
    out_ref, turned, misc_turned = refs[-3:]
    n, cols, _ = out_ref.shape
    at = 0
    column = 0
    for group, pairs in enumerate(shape):
        lefts, rights = refs[at : at + pairs], refs[at + pairs : at + 2 * pairs]
        at += 2 * pairs
        row = 0
        for left in lefts:
            turned[group, :, row : row + left.shape[0]] = left[...].T
            row += left.shape[0]
        right = jnp.concatenate([r[...] for r in rights], axis=0) if pairs > 1 else rights[0][...]
        for i in range(n):
            rows = pl.ds(pl.multiple_of(owner_ref[i] * cols, 16), cols)
            out_ref[i, :, column : column + right.shape[1]] = jnp.dot(
                turned[group, rows, :], right, preferred_element_type=F32
            ).astype(BF)
        column += right.shape[1]
    if extra:
        misc = refs[at][...]
        spare = jnp.zeros((128 - misc.shape[0], misc.shape[1]), F32)
        misc_turned[...] = jnp.concatenate([misc, spare], axis=0).T
        for i in range(n):
            rows = pl.ds(pl.multiple_of(owner_ref[i] * cols, 16), cols)
            out_ref[i, :, column:] = misc_turned[rows, :].astype(BF)


def weight_terms(owner, groups, misc=None, us=4, first=()):
    n = owner.shape[0]
    width = groups[0][0][0].shape[1]
    rows = sum(x.shape[0] for x in groups[0][0])
    out_width = sum(rights[0].shape[1] for _, rights in groups)
    operands = []
    for lefts, rights in groups:
        operands += list(lefts) + list(rights)
    if misc is not None:
        operands.append(misc)
        out_width += 128
    shape = tuple(len(lefts) for lefts, _ in groups)
    return pl.pallas_call(
        drop_first(
            functools.partial(weight_kernel, shape, misc is not None),
            1 + len(operands),
            len(first),
        ),
        out_shape=jax.ShapeDtypeStruct((n, width // n, out_width), BF),
        in_specs=[pl.BlockSpec(memory_space=pltpu.SMEM)]
        + vspec(len(operands))
        + anywhere(len(first)),
        out_specs=vspec(1)[0],
        scratch_shapes=[pltpu.VMEM((len(groups), width, rows), BF), pltpu.VMEM((width, 128), F32)],
        compiler_params=params(),
        name="weight_terms",
        cost_estimate=cost(us),
    )(owner, *operands, *first)


def per_device(
    n_ctx,
    layer_input,
    segment_ids,
    expert_ids,
    norm_gain,
    query_weight,
    key_weight,
    value_weight,
    output_weight,
    ffn_gain,
    router_weight,
    gate_weight,
    up_weight,
    down_weight,
    cotangent,
):
    tok, width = layer_input.shape
    half = tok // 2
    groups = H // KV
    kv_local = key_weight.shape[1] // HD
    heads = kv_local * groups
    kvw = key_weight.shape[1]
    experts = gate_weight.shape[0]
    cols = width // n_ctx
    digits = digits_of(n_ctx)
    keys = rel_keys(digits)
    upper_first = list(range(1, len(digits))) + [0]
    lower_first = list(range(len(digits)))
    me = lax.axis_index("ctx")
    core = lax.axis_index("wa") % 2
    core_arr = jnp.full((1,), core, jnp.int32)
    owner_to = jnp.stack([digit_offset(me, k, digits, 1) for k in keys]).astype(jnp.int32)
    owner_from = jnp.stack([digit_offset(me, k, digits, -1) for k in keys]).astype(jnp.int32)
    gain_one, gain_two = norm_gain, ffn_gain
    router = router_weight.T

    def mine_first(x):
        return jnp.where(core == 0, x, jnp.concatenate([x[half:], x[:half]], axis=0))

    segs = mine_first(segment_ids).astype(BF)
    ids = mine_first(expert_ids)
    extra = jnp.concatenate([segs, ids[:, 0].astype(BF), ids[:, 1].astype(BF)])
    extra = jnp.pad(extra, (0, EXTRA * 2 * kvw - extra.shape[0])).reshape(EXTRA, 2 * kvw)
    a1, q, kv = project(
        core_arr, layer_input, gain_one, query_weight, key_weight, value_weight, extra
    )
    tops = digits[-1][1]
    staged = len(digits) == 2
    side = digits[0][1]
    low, top = digits[0], digits[-1]
    turned_digits = digits[1:] + digits[:1]
    turned_keys = [(k[-1],) + k[:-1] for k in rel_keys(turned_digits)]
    owner_turned = jnp.stack(
        [digit_offset(me, k, digits, -1) for k in turned_keys]
    ).astype(jnp.int32)

    wo_chip = other_chip(output_weight)
    kv_weight = jnp.concatenate([key_weight, value_weight], axis=1)
    kv_core = other_core(kv_weight)
    wq_core = other_core(query_weight)
    g_out = columns(owner_to, core_arr, cotangent, half, tops, side, [kv])
    if staged:
        z, y = [kv], []
        for r in range(tops - 1):
            aside = [g_out[0], kv_core, wq_core] if r == tops - 2 else []
            z_next, y_next = tie([hop(z[r], n_ctx, top), hop(z[r], n_ctx, low)], aside)
            z.append(z_next)
            y.append(y_next)
        y.append(hop(z[-1], n_ctx, low))
        kv_list = [block for pair in zip(z, y) for block in pair]
    else:
        kv_blocks = gather_ctx(kv, n_ctx, digits, upper_first)
        kv_list = [kv_blocks[k] for k in keys]

    g_top = exchange_top(g_out, n_ctx, digits)

    heads_f32, heads_near, heads_far, lse = attend(
        q, kv_list, heads, groups, first=[g_out[0]]
    )
    heads_near, heads_far, wo_chip, *rest = tie(
        [heads_near, heads_far, wo_chip] + list(g_top[1:]), []
    )
    g_top = [g_top[0]] + list(rest)
    wo_parts = [output_weight, other_core(output_weight), wo_chip, other_core(wo_chip)]

    parts = all_parts(heads_near, heads_far)
    g_pieces = exchange_rest(g_top, n_ctx, digits)
    hidden_one, a2_mine = simple(
        middle_kernel,
        "middle",
        [((half, width), F32), ((half, width), BF)],
        core_arr,
        layer_input,
        gain_two,
        *parts,
        *wo_parts,
    )
    a2_far = other_core(a2_mine)
    a2_out = columns(owner_to, core_arr, a2_mine, half, tops, side)
    a2_top = exchange_top(a2_out, n_ctx, digits)
    wq_chip = other_chip(query_weight)

    dx_keep, dx_send, gates, ent = experts_call(
        core_arr,
        ids,
        a2_mine,
        a2_far,
        cotangent,
        router,
        gate_weight,
        up_weight,
        down_weight,
        first=[a2_out[0]],
    )
    dx_send, wq_chip, *rest = tie(
        [dx_send, wq_chip] + list(a2_top[1:]), [array for array, _ in g_pieces]
    )
    a2_top = [a2_top[0]] + list(rest)

    near = (dx_keep + other_core(dx_send).astype(F32)).astype(BF)
    got = other_chip(near)
    if staged:
        z = [ent]
        z_next = hop(ent, n_ctx, top)
    wq_parts = [query_weight, wq_core, wq_chip, other_core(wq_chip)]
    hidden_grad, att_near, misc = simple(
        back_kernel,
        "back",
        [((half, width), F32), ((half, width), BF), ((16, width), F32)],
        core_arr,
        near,
        got,
        hidden_one,
        a2_mine,
        gates,
        ids,
        router,
        gain_two,
        cotangent,
        first=[wq_parts[3]],
    )
    att_far = other_core(att_near)
    mix_keep, mix_send = mix_call(ids, ent, down_weight, [att_near])
    mix_near = (mix_keep + other_core(mix_send).astype(F32)).astype(BF)
    mix_got = other_chip(mix_near)
    a2_pieces = exchange_rest(a2_top, n_ctx, digits)
    if staged:
        (z_next,) = tie([z_next], [mix_send])
        z.append(z_next)
        z_next = hop(z[1], n_ctx, top)

    begin = [att_near, att_far, output_weight, heads_f32]
    sides = [[kv_list[i] for i, k in enumerate(keys) if k[0] == r] for r in range(side)]
    dkv_far, head_grad, delta, dq_going = attend_back(
        q,
        kv_list[0],
        lse,
        [block for r in range(1, side) for block in sides[r]],
        heads,
        groups,
        start=begin,
        end=False,
        first=[mix_near] + ([z[1]] if staged else []),
    )
    (mix_got,) = tie([mix_got], [dq_going])
    dkv_far_got = hop(dkv_far, n_ctx, low)
    ids_all = routes(sides[0], tok, [dq_going])
    a2_stack, a2_stack_far = swapped(a2_pieces, [dq_going])
    g_stack, g_stack_far = swapped(g_pieces, [dq_going])
    terms_o = weight_terms(
        owner_turned,
        [([att_near, att_far], [heads_near, heads_far])],
        misc,
        first=[dq_going, a2_stack, g_stack],
    )
    kv_weight, mix_got = tie([kv_weight, mix_got], [])
    kv_chip = other_chip(kv_weight)
    waits = [ids_all, a2_stack_far, g_stack_far, terms_o]
    if staged:
        (z_next,) = tie([z_next], [terms_o])
        z.append(z_next)
        z_next = hop(z[2], n_ctx, top)
        waits = waits + [z[2]]
    o_sides = cut(terms_o, side)
    o_got = hop(o_sides[1], n_ctx, low)
    dkv_near, dq_near, dq_far = attend_back(
        q,
        kv_list[0],
        lse,
        sides[0],
        heads,
        groups,
        going=[head_grad, delta, dq_going],
        first=waits,
    )
    dkv_far_got, kv_chip = tie([dkv_far_got, kv_chip], [dq_near])
    kv_weights = [kv_weight, kv_core, kv_chip, other_core(kv_chip)]


    dkv_sides = [
        total([dkv_far_got[i : i + 1], dkv_near[i : i + 1]]).astype(BF)
        for i in range(dkv_near.shape[0])
    ]
    if staged:
        dkv_sent = scatter_sends(dkv_sides, n_ctx, top)
    dq_core = other_core(dq_far)

    terms_q = weight_terms(
        owner_turned,
        [([a1], [jnp.concatenate([dq_near, dq_far], axis=0)])],
        first=[dkv_sides[1 % len(dkv_sides)]],
    )
    dq_core, o_got = tie([dq_core, o_got], [terms_q, kv_weights[3]])
    dq_pair = jnp.stack([dq_near, dq_core], axis=0)
    q_sides = cut(terms_q, side)
    q_got = hop(q_sides[1], n_ctx, low)

    if staged:
        z_next, dq_pair = tie([z_next, dq_pair], [terms_q])
        z.append(z_next)
        ents = z
    else:
        upper = gather_ctx(ent, n_ctx, digits, upper_first[:-1])
        ents = [upper[k] for k in keys if k[0] == 0]
    dq_chip = other_chip(dq_pair)
    some = experts // 2
    places = tuple(range(len(ents)))
    shared = [a2_stack, a2_stack_far, g_stack, g_stack_far, ents]
    *grads_a, send_a = expert_grads(0, some, ids_all, places, *shared)
    (q_got,) = tie([q_got], [send_a])
    got_a = hop(send_a, n_ctx, low)
    (dq_chip,) = tie([dq_chip], [send_a])
    (query_back,) = simple(
        query_back_kernel,
        "query_back",
        [((half, width), F32)],
        core_arr,
        dq_pair,
        dq_chip,
        *wq_parts,
    )
    if staged:
        more = tie(dkv_sent[1:], [query_back])
        dkv_own = total([dkv_sent[0]] + list(more))[0].astype(BF)
    else:
        dkv_own = scatter_ctx(jnp.concatenate(dkv_sides, axis=0), n_ctx, digits[1:]).astype(BF)

    terms = jnp.concatenate(
        [total([o_sides[0], o_got]), total([q_sides[0], q_got])], axis=2
    ).astype(BF)
    dkv_parts = all_parts(dkv_own[:half], dkv_own[half:])
    late = weight_terms(owner_from, [([a1], [dkv_own])])
    *grads_b, send_b = expert_grads(
        some,
        experts - some,
        ids_all,
        places,
        *shared,
        first=[send_a, dkv_own, terms, late],
    )
    got_b = hop(send_b, n_ctx, low)
    *dkv_rest, got_a = tie(dkv_parts[1:] + [got_a], [send_b])
    dkv_parts = [dkv_parts[0]] + dkv_rest
    in_mine, norm_row = simple(
        input_kernel,
        "input",
        [((half, width), F32), ((8, width), F32)],
        core_arr,
        layer_input,
        gain_one,
        hidden_grad,
        query_back,
        *dkv_parts,
        *kv_weights,
    )
    in_far = other_core(in_mine)
    done = finish(0, experts, grads_a, got_a, first=[norm_row])
    (late,) = tie([late], [send_b])
    (mix_got,) = tie([mix_got], [norm_row])
    out_mine = hidden_one + mix_near.astype(F32) + mix_got.astype(F32)
    out_far = other_core(out_mine)
    (layer_output,) = simple(
        place_kernel, "place", [((tok, width), F32)], core_arr, out_mine, out_far
    )
    (input_grad,) = simple(
        place_kernel, "place", [((tok, width), F32)], core_arr, in_mine, in_far
    )
    if staged:
        blocks = cut(terms, tops)
        moving = blocks[1]
        waits = [[in_mine], [input_grad], [layer_output]]
        for r in range(2, tops + 1):
            (moving,) = tie([hop(moving, n_ctx, top)], waits[r - 2])
            moving = total([moving, blocks[r % tops]]).astype(BF if r < tops else F32)
        terms_own = moving[0]
    else:
        terms_own = scatter_ctx(terms, n_ctx, digits[1:])
    late_own = scatter_ctx(
        late, n_ctx, digits, lambda at, xs: tie(xs, [done[0]] if at else [input_grad])
    )
    norm_rel = norm_row[0].reshape(n_ctx, cols)[owner_from]
    norm_own = scatter_ctx(norm_rel, n_ctx, digits, kind=F32)
    down_grad, gate_grad, up_grad = finish(some, experts, grads_b, got_b, done)

    qw = heads * HD
    output_grad = terms_own[:, :qw].T
    small = jnp.concatenate(
        [terms_own[:, qw : qw + experts + 1], norm_own[:, None]], axis=1
    )
    small = small + other_core(small)
    return (
        layer_output,
        input_grad,
        small[:, experts + 1],
        terms_own[:, qw + 128 :],
        late_own[:, :kvw],
        late_own[:, kvw:],
        output_grad,
        small[:, experts],
        small[:, :experts],
        gate_grad,
        up_grad,
        jnp.swapaxes(down_grad, 1, 2),
    )


def solution(mesh):
    in_specs = (
        P("ctx", None),
        P("ctx"),
        P("ctx", None),
        P(),
        P(None, "wa"),
        P(None, "wa"),
        P(None, "wa"),
        P("wa", None),
        P(),
        P(),
        P(None, None, "wa"),
        P(None, None, "wa"),
        P(None, "wa", None),
        P("ctx", None),
    )
    out_specs = (
        P("ctx", None),
        P("ctx", None),
        P("ctx"),
        P("ctx", "wa"),
        P("ctx", "wa"),
        P("ctx", "wa"),
        P("wa", "ctx"),
        P("ctx"),
        P("ctx", None),
        P(None, "ctx", "wa"),
        P(None, "ctx", "wa"),
        P(None, "wa", "ctx"),
    )
    return jax.shard_map(
        functools.partial(per_device, mesh.shape["ctx"]),
        mesh=mesh,
        in_specs=in_specs,
        out_specs=out_specs,
        check_vma=False,
    )
```

```python
import functools

import jax
import jax.numpy as jnp
from jax import lax
from jax.experimental import pallas as pl
from jax.experimental.pallas import tpu as pltpu
from jax.sharding import PartitionSpec as P

H = 24
KV = 8
HD = 64
eps = 1e-05
NEG = -1e30
F32 = jnp.float32
BF = jnp.bfloat16
VLIM = 60 * 1024 * 1024
EXTRA = 16
NT = (((1,), (1,)), ((), ()))
TN = (((0,), (0,)), ((), ()))


def digits_of(n):
    out = []
    stride = 1
    while n > 1:
        if stride == 1 and n % 2 == 0:
            radix = 2
        elif n % 4 == 0:
            radix = 4
        else:
            radix = n
        out.append((stride, radix))
        stride *= radix
        n //= radix
    return out


def moved(n, digit, shift):
    stride, radix = digit
    pairs = []
    for i in range(n):
        d = (i // stride) % radix
        pairs.append((i, i + ((d + shift) % radix - d) * stride))
    return pairs


def hop(x, n, digit, shift=1):
    return lax.ppermute(x, "ctx", moved(n, digit, shift))


def other_core(x):
    return lax.ppermute(x, "wa", [(i, i ^ 1) for i in range(4)])


def other_chip(x):
    return lax.ppermute(x, "wa", [(i, i ^ 2) for i in range(4)])


def rel_keys(digits):
    keys = [()]
    for _, radix in digits:
        keys = [k + (r,) for r in range(radix) for k in keys]
    return keys


def set_digit(key, at, value):
    return key[:at] + (value,) + key[at + 1 :]


def gather_ctx(x, n, digits, order):
    blocks = {tuple(0 for _ in digits): x}
    for at in order:
        fresh = {}
        for key, block in blocks.items():
            moving = block
            for s in range(1, digits[at][1]):
                moving = hop(moving, n, digits[at])
                fresh[set_digit(key, at, s)] = moving
        blocks.update(fresh)
    return blocks


def scatter_sends(blocks, n, digit):
    return [blocks[0]] + [hop(blocks[r], n, digit, -r) for r in range(1, len(blocks))]


def total(parts):
    return functools.reduce(jnp.add, [x.astype(F32) for x in parts])


def cut(stack, radix):
    per = stack.shape[0] // radix
    return [stack[r * per : (r + 1) * per] for r in range(radix)]


def scatter_ctx(stack, n, order, hold=lambda at, xs: xs, kind=BF):
    moving = stack
    for at in reversed(range(len(order))):
        parts = scatter_sends(cut(moving, order[at][1]), n, order[at])
        parts = parts[:1] + list(hold(at, parts[1:]))
        moving = total(parts)
        if at:
            moving = moving.astype(kind)
    return moving[0]


def stack_kernel(places, *refs):
    for i, (at, unit) in enumerate(places):
        refs[-1][i] = refs[at][unit]


def stacked(pieces):
    arrays = []
    places = []
    for array, unit in pieces:
        at = next((i for i, x in enumerate(arrays) if x is array), None)
        if at is None:
            at = len(arrays)
            arrays.append(array)
        places.append((at, unit))
    shape = (len(pieces),) + arrays[0].shape[1:]
    return pl.pallas_call(
        functools.partial(stack_kernel, tuple(places)),
        out_shape=jax.ShapeDtypeStruct(shape, arrays[0].dtype),
        in_specs=vspec(len(arrays)),
        out_specs=vspec(1)[0],
        compiler_params=params(),
        name="stacked",
        cost_estimate=cost(1),
    )(*arrays)


def exchange_top(groups, n, digits):
    return [groups[0]] + [hop(groups[r], n, digits[-1], r) for r in range(1, len(groups))]


def exchange_rest(groups, n, digits):
    keys = rel_keys(digits[1:])
    n_up = len(keys)
    per = n_up // len(groups)
    parts = {i: (groups[i // per], i % per) for i in range(n_up)}
    for at in reversed(range(1, len(digits) - 1)):
        for s in range(1, digits[at][1]):
            chosen = [i for i, k in enumerate(keys) if k[at - 1] == s]
            bundle = hop(stacked([parts[i] for i in chosen]), n, digits[at], s)
            for place, i in enumerate(chosen):
                parts[i] = (bundle, place)
    return [parts[i] for i in range(n_up)]


def swapped(pieces, first):
    arrays = []
    for array, _ in pieces:
        if not any(array is x for x in arrays):
            arrays.append(array)
    held = tie(arrays, first)
    pieces = [(held[next(i for i, x in enumerate(arrays) if x is a)], u) for a, u in pieces]
    near = stacked(pieces)
    return near, other_core(near)


def digit_offset(me, key, digits, sign):
    place = 0
    for (stride, radix), r in zip(digits, key):
        d = (me // stride) % radix
        place = place + ((d + sign * r) % radix) * stride
    return place


def tie_kernel(*refs):
    pass


def tie(xs, first):
    xs, first = list(xs), list(first)
    return pl.pallas_call(
        tie_kernel,
        out_shape=tuple(jax.ShapeDtypeStruct(x.shape, x.dtype) for x in xs),
        in_specs=anywhere(len(xs) + len(first)),
        out_specs=tuple(anywhere(len(xs))),
        input_output_aliases={i: i for i in range(len(xs))},
        name="tie",
    )(*xs, *first)


def diagonal(x):
    return lax.ppermute(x, "wa", [(i, i ^ 3) for i in range(4)])


def all_parts(near, far):
    return [near, other_core(far), other_chip(near), diagonal(far)]


def cost(us):
    return pl.CostEstimate(flops=int(us * 3e8), bytes_accessed=int(us * 9e5), transcendentals=0)


def params(**kw):
    return pltpu.CompilerParams(vmem_limit_bytes=VLIM, **kw)


def vspec(n):
    return [pl.BlockSpec(memory_space=pltpu.VMEM)] * n


def drop_first(kernel, at, count):
    if not count:
        return kernel

    def waiting(*refs):
        kernel(*refs[:at], *refs[at + count :])

    return waiting


def anywhere(count):
    return [pl.BlockSpec(memory_space=pl.ANY)] * count


def project_kernel(core_ref, x_ref, gain_ref, wq_ref, wk_ref, wv_ref, extra_ref, a1_ref, q_ref, kv_ref):
    tok = x_ref.shape[0]
    half = tok // 2
    kvw = wk_ref.shape[1]
    for i in range(2):
        start = pl.multiple_of(((core_ref[0] + i) % 2) * half, half)
        x = x_ref[pl.ds(start, half), :].astype(F32)
        inv = lax.rsqrt(jnp.mean(x * x, axis=-1, keepdims=True) + eps)
        a1 = (x * inv * gain_ref[...][None, :]).astype(BF)
        rows = pl.ds(i * half, half)
        a1_ref[rows, :] = a1
        kv_ref[rows, :kvw] = jnp.dot(a1, wk_ref[...], preferred_element_type=F32).astype(BF)
        kv_ref[rows, kvw:] = jnp.dot(a1, wv_ref[...], preferred_element_type=F32).astype(BF)
        q = jnp.dot(a1, wq_ref[...], preferred_element_type=F32).astype(BF)
        q_ref[rows, :] = (q.astype(F32) * HD ** (-0.5)).astype(BF)
    kv_ref[pl.ds(tok, EXTRA), :] = extra_ref[...]


def project(core, x, gain, wq, wk, wv, extra):
    tok, width = x.shape
    return pl.pallas_call(
        project_kernel,
        out_shape=(
            jax.ShapeDtypeStruct((tok, width), BF),
            jax.ShapeDtypeStruct((tok, wq.shape[1]), BF),
            jax.ShapeDtypeStruct((tok + EXTRA, 2 * wk.shape[1]), BF),
        ),
        in_specs=[pl.BlockSpec(memory_space=pltpu.SMEM)] + vspec(6),
        out_specs=tuple(vspec(3)),
        compiler_params=params(),
        name="project",
        cost_estimate=cost(5),
    )(core, x, gain, wq, wk, wv, extra)


def seg_onehot(row):
    lane = lax.broadcasted_iota(jnp.int32, (16, row.shape[1]), 0).astype(F32)
    return jnp.where(lane == row, 1.0, 0.0).astype(BF)


def seg_rows_of(block, tok):
    width = block.shape[1]
    return [
        block[tok : tok + EXTRA, :].astype(F32)[i : i + 1, :] for i in range(tok // width)
    ]


ROWS = 256


def block_segs(block, tok):
    return jnp.concatenate(seg_rows_of(block, tok), axis=1)


def turned_groups(x, out, heads, groups):
    x = x.astype(F32).T.astype(BF)
    pairs = heads // groups
    for r in range(x.shape[1] // ROWS):
        for h in range(heads):
            n, g = h // groups, h % groups
            out[r * pairs + n, :, g * ROWS : (g + 1) * ROWS] = x[
                h * HD : (h + 1) * HD, r * ROWS : (r + 1) * ROWS
            ]


def straight_groups(x, out, heads, groups):
    pairs = heads // groups
    for r in range(x.shape[0] // ROWS):
        for h in range(heads):
            n, g = h // groups, h % groups
            out[r * pairs + n, g * ROWS : (g + 1) * ROWS, :] = x[
                r * ROWS : (r + 1) * ROWS, h * HD : (h + 1) * HD
            ]


def head_rows(ref, r, n, groups):
    rows = slice(r * ROWS, (r + 1) * ROWS)
    return jnp.concatenate(
        [ref[h : h + 1, rows] for h in range(n * groups, (n + 1) * groups)], axis=1
    )


def visit_tiles(kv_s, own, tok, body, before, behind):
    tiles = tok // ROWS
    lows = [jnp.min(own[:, r * ROWS : (r + 1) * ROWS]) for r in range(tiles)]
    highs = [jnp.max(own[:, r * ROWS : (r + 1) * ROWS]) for r in range(tiles)]

    def visit(b, carry):
        seg = block_segs(kv_s[b], tok)
        lo = jnp.min(seg)
        hi = jnp.max(seg)
        before(b)
        for r in range(tiles):
            plain = (lo == hi) & (lows[r] == highs[r]) & (lo == lows[r])
            touch = (lo <= highs[r]) & (lows[r] <= hi)
            pl.when(plain)(functools.partial(body, b, r, False))
            pl.when(touch & jnp.logical_not(plain))(functools.partial(body, b, r, True))
        behind(b)
        return carry

    lax.fori_loop(0, kv_s.shape[0], visit, 0)


def same_tile(block, own_hot, r, tok, groups):
    same = lax.dot_general(
        seg_onehot(block_segs(block, tok)),
        own_hot[:, r * ROWS : (r + 1) * ROWS],
        TN,
        preferred_element_type=F32,
    )
    return jnp.concatenate([same] * groups, axis=1) > 0.5


def attend_kernel(nb, heads, groups, *refs):
    q_ref = refs[0]
    kv_refs = refs[1 : 1 + nb]
    hf_ref, near_ref, far_ref, lse_ref = refs[1 + nb : 5 + nb]
    kv_s, q_s, m_s, acc_s = refs[5 + nb :]
    tok = q_ref.shape[0]
    kvw = kv_refs[0].shape[1] // 2
    pairs = heads // groups
    for b in range(nb):
        kv_s[b] = kv_refs[b][...]
    turned_groups(q_ref[...], q_s, heads, groups)
    own = block_segs(kv_s[0], tok)
    own_hot = seg_onehot(own)
    m_s[...] = jnp.full(m_s.shape, NEG, F32)
    acc_s[...] = jnp.zeros(acc_s.shape, F32)

    def body(b, r, masked):
        block = kv_s[b]
        if masked:
            same = same_tile(block, own_hot, r, tok, groups)
        scores = []
        for n in range(pairs):
            k = block[:tok, n * HD : (n + 1) * HD]
            s = jnp.dot(k, q_s[r * pairs + n], preferred_element_type=F32)
            scores.append(jnp.where(same, s, NEG) if masked else s)
        old = [m_s[r * pairs + n : r * pairs + n + 1, :] for n in range(pairs)]
        new = [
            jnp.maximum(old[n], jnp.max(scores[n], axis=0, keepdims=True)) for n in range(pairs)
        ]
        for n in range(pairs):
            i = r * pairs + n
            m_s[i : i + 1, :] = new[n]
            p = jnp.exp(scores[n] - new[n]).astype(BF)
            v = block[:tok, kvw + n * HD : kvw + (n + 1) * HD]
            v = jnp.concatenate([v, jnp.ones((tok, 16), BF)], axis=1)
            acc_s[i] = acc_s[i] * jnp.exp(old[n] - new[n]) + lax.dot_general(
                v, p, TN, preferred_element_type=F32
            )

    def nothing(b):
        pass

    visit_tiles(kv_s, own, tok, body, nothing, nothing)
    tiles = []
    for r in range(tok // ROWS):
        rows = []
        for n in range(pairs):
            i = r * pairs + n
            total = acc_s[i, HD : HD + 1, :]
            out = acc_s[i, :HD, :] / total
            lse = m_s[i : i + 1, :] + jnp.log(total)
            for g in range(groups):
                h = n * groups + g
                lanes = slice(g * ROWS, (g + 1) * ROWS)
                rows.append(out[:, lanes])
                lse_ref[h : h + 1, r * ROWS : (r + 1) * ROWS] = lse[:, lanes]
        tiles.append(jnp.concatenate(rows, axis=0))
    out = jnp.concatenate(tiles, axis=1).T
    hf_ref[...] = out
    near_ref[...] = out[: tok // 2].astype(BF)
    far_ref[...] = out[tok // 2 :].astype(BF)


def attend(q, blocks, heads, groups, first=()):
    tok = q.shape[0]
    nb = len(blocks)
    units = (tok // ROWS) * (heads // groups)
    return pl.pallas_call(
        drop_first(functools.partial(attend_kernel, nb, heads, groups), 1 + nb, len(first)),
        out_shape=(
            jax.ShapeDtypeStruct((tok, heads * HD), F32),
            jax.ShapeDtypeStruct((tok // 2, heads * HD), BF),
            jax.ShapeDtypeStruct((tok // 2, heads * HD), BF),
            jax.ShapeDtypeStruct((8, tok), F32),
        ),
        in_specs=vspec(1 + nb) + anywhere(len(first)),
        out_specs=tuple(vspec(4)),
        scratch_shapes=[
            pltpu.VMEM((nb,) + blocks[0].shape, BF),
            pltpu.VMEM((units, HD, groups * ROWS), BF),
            pltpu.VMEM((max(8, units), groups * ROWS), F32),
            pltpu.VMEM((units, HD + 16, groups * ROWS), F32),
        ],
        compiler_params=params(),
        name="attend",
        cost_estimate=cost(27),
    )(q, *blocks, *first)


def attend_back_kernel(nb, heads, groups, start, end, *refs):
    q_ref, own_ref, lse_ref = refs[:3]
    kv_refs = refs[3 : 3 + nb]
    at = 3 + nb
    if start:
        att_near_ref, att_far_ref, wo_ref, hf_ref = refs[at : at + 4]
        at += 4
    else:
        grad_in_ref, delta_in_ref, dq_in_ref = refs[at : at + 3]
        at += 3
    dkv_ref = refs[at]
    at += 1
    if start:
        grad_ref, delta_ref = refs[at : at + 2]
        at += 2
    if end:
        dq_near_ref, dq_far_ref = refs[at : at + 2]
        at += 2
    else:
        dq_out_ref = refs[at]
        at += 1
    kv_s, qt_s, q_s, dot_s, do_s, delta_s, dq_s, acc_s = refs[at:]
    tok = q_ref.shape[0]
    kvw = own_ref.shape[1] // 2
    key_heads = heads // groups
    if start:
        grad = jnp.concatenate(
            [
                lax.dot_general(ref[...], wo_ref[...], NT, preferred_element_type=F32)
                for ref in (att_near_ref, att_far_ref)
            ],
            axis=0,
        ).astype(BF)
        grad_ref[...] = grad
        prod = (grad.astype(F32) * hf_ref[...]).T
        for h in range(heads):
            delta_s[h : h + 1, :] = jnp.sum(prod[h * HD : (h + 1) * HD, :], axis=0, keepdims=True)
        delta_ref[...] = delta_s[...]
        dq_s[...] = jnp.zeros(dq_s.shape, F32)
    else:
        grad = grad_in_ref[...]
        delta_s[...] = delta_in_ref[...]
        dq_s[...] = dq_in_ref[...]
    for b in range(nb):
        kv_s[b] = kv_refs[b][...]
    turned_groups(q_ref[...], qt_s, heads, groups)
    straight_groups(q_ref[...], q_s, heads, groups)
    turned_groups(grad, dot_s, heads, groups)
    straight_groups(grad, do_s, heads, groups)
    own = block_segs(own_ref[...], tok)
    own_hot = seg_onehot(own)

    def body(b, r, masked):
        block = kv_s[b]
        if masked:
            same = same_tile(block, own_hot, r, tok, groups)
        for n in range(key_heads):
            i = r * key_heads + n
            k = block[:tok, n * HD : (n + 1) * HD]
            v = block[:tok, kvw + n * HD : kvw + (n + 1) * HD]
            s = jnp.dot(k, qt_s[i], preferred_element_type=F32)
            dp = jnp.dot(v, dot_s[i], preferred_element_type=F32)
            p = jnp.exp(s - head_rows(lse_ref, r, n, groups))
            if masked:
                p = jnp.where(same, p, 0.0)
            ds = (p * (dp - head_rows(delta_s, r, n, groups))).astype(BF)
            acc_s[n] += jnp.dot(ds, q_s[i], preferred_element_type=F32)
            acc_s[key_heads + n] += jnp.dot(p.astype(BF), do_s[i], preferred_element_type=F32)
            dq_s[i] += lax.dot_general(k, ds, TN, preferred_element_type=F32)

    def before(b):
        acc_s[...] = jnp.zeros(acc_s.shape, F32)

    def behind(b):
        sums = jnp.concatenate([acc_s[i] for i in range(2 * key_heads)], axis=1)
        dkv_ref[b] = sums.astype(BF)

    visit_tiles(kv_s, own, tok, body, before, behind)
    if end:
        tiles = []
        for r in range(tok // ROWS):
            rows = [
                dq_s[r * key_heads + h // groups, :, (h % groups) * ROWS : (h % groups + 1) * ROWS]
                for h in range(heads)
            ]
            tiles.append(jnp.concatenate(rows, axis=0))
        out = (jnp.concatenate(tiles, axis=1).T * HD ** (-0.5)).astype(BF)
        dq_near_ref[...] = out[: tok // 2]
        dq_far_ref[...] = out[tok // 2 :]
    else:
        dq_out_ref[...] = dq_s[...]


def attend_back(q, own, lse, blocks, heads, groups, start=None, going=None, end=True, first=()):
    tok = q.shape[0]
    nb = len(blocks)
    width = heads * HD
    key_heads = heads // groups
    units = (tok // ROWS) * key_heads
    operands = [q, own, lse] + list(blocks) + list(start if start is not None else going)
    outs = [((nb, tok, own.shape[1]), BF)]
    if start is not None:
        outs += [((tok, width), BF), ((8, tok), F32)]
    outs += [((tok // 2, width), BF)] * 2 if end else [((units, HD, groups * ROWS), F32)]
    kernel = functools.partial(
        attend_back_kernel, nb, heads, groups, start is not None, end
    )
    return pl.pallas_call(
        drop_first(kernel, len(operands), len(first)),
        out_shape=tuple(jax.ShapeDtypeStruct(shape, dtype) for shape, dtype in outs),
        in_specs=vspec(len(operands)) + anywhere(len(first)),
        out_specs=tuple(vspec(len(outs))),
        scratch_shapes=[
            pltpu.VMEM((nb,) + blocks[0].shape, BF),
            pltpu.VMEM((units, HD, groups * ROWS), BF),
            pltpu.VMEM((units, groups * ROWS, HD), BF),
            pltpu.VMEM((units, HD, groups * ROWS), BF),
            pltpu.VMEM((units, groups * ROWS, HD), BF),
            pltpu.VMEM((8, tok), F32),
            pltpu.VMEM((units, HD, groups * ROWS), F32),
            pltpu.VMEM((2 * key_heads, tok, HD), F32),
        ],
        compiler_params=params(),
        name="attend_back",
        cost_estimate=cost(4.5 * nb),
    )(*operands, *first)


def routes_kernel(at, *refs):
    out_ref = refs[-1]
    tok = out_ref.shape[1]
    for b, ref in enumerate(refs[:-1]):
        rows = ref[tok : tok + EXTRA, :].astype(F32)
        both = [
            jnp.concatenate([rows[i : i + 1, :] for i in range(c * at, (c + 1) * at)], axis=1)
            for c in (1, 2)
        ]
        out_ref[b] = jnp.concatenate(both + [jnp.zeros((6, tok), F32)], axis=0).T


def routes(blocks, tok, first=()):
    return pl.pallas_call(
        drop_first(
            functools.partial(routes_kernel, tok // blocks[0].shape[1]), len(blocks), len(first)
        ),
        out_shape=jax.ShapeDtypeStruct((len(blocks), tok, 8), F32),
        in_specs=vspec(len(blocks)) + anywhere(len(first)),
        out_specs=vspec(1)[0],
        compiler_params=params(),
        name="routes",
        cost_estimate=cost(2),
    )(*blocks, *first)


def masks(ids_ref, rows, e, count, width):
    return [
        jnp.broadcast_to(
            jnp.where(ids_ref[rows, c : c + 1] == e, 1.0, 0.0).astype(BF), (count, width)
        )
        for c in range(2)
    ]


def experts_kernel(
    per,
    core_ref,
    ids_ref,
    mine_ref,
    theirs_ref,
    g_ref,
    wr_ref,
    wg_ref,
    wu_ref,
    wd_ref,
    dx_keep_ref,
    dx_send_ref,
    gates_ref,
    ent_ref,
    a2_s,
    g_s,
    dx_s,
    back_s,
):
    step = pl.program_id(0)
    tok, width = a2_s.shape
    half = tok // 2
    experts = wr_ref.shape[0]
    lane = lax.broadcasted_iota(jnp.int32, (tok, experts), 1)
    first = ids_ref[:, 0:1]
    second = ids_ref[:, 1:2]

    @pl.when(step == 0)
    def _():
        a2_s[:half, :] = mine_ref[...]
        a2_s[half:, :] = theirs_ref[...]
        for i in range(2):
            start = pl.multiple_of(((core_ref[0] + i) % 2) * half, half)
            g_s[pl.ds(i * half, half), :] = g_ref[pl.ds(start, half), :]
        logits = lax.dot_general(a2_s[...], wr_ref[...], NT, preferred_element_type=F32)
        one = jnp.sum(jnp.where(lane == first, logits, 0.0), axis=1, keepdims=True)
        two = jnp.sum(jnp.where(lane == second, logits, 0.0), axis=1, keepdims=True)
        top = jnp.maximum(one, two)
        one = jnp.exp(one - top)
        two = jnp.exp(two - top)
        both = one + two
        gates_ref[...] = jnp.where(lane == first, one / both, 0.0) + jnp.where(
            lane == second, two / both, 0.0
        )
        dx_s[...] = jnp.zeros(dx_s.shape, F32)
        back_s[...] = jnp.zeros(back_s.shape, F32)
        ent_ref[...] = jnp.zeros(ent_ref.shape, BF)

    for i in range(2):
        rows = pl.ds(i * half, half)
        a2 = a2_s[rows, :]
        g = g_s[rows, :]
        products = []
        for j in range(per):
            u = jnp.dot(a2, wg_ref[j], preferred_element_type=F32)
            w = jnp.dot(a2, wu_ref[j], preferred_element_type=F32)
            m = lax.dot_general(g, wd_ref[j], NT, preferred_element_type=F32)
            products.append((u, w, m))
        dx = None
        back_all = None
        parts = [None] * 6
        for j in range(per):
            e = step * per + j
            u, w, m = products[j]
            here = lane[:half] == e
            gate = jnp.sum(jnp.where(here, gates_ref[rows, :], 0.0), axis=1, keepdims=True)
            picked = (ids_ref[rows, 0:1] == e) | (ids_ref[rows, 1:2] == e)
            sig = 1.0 / (1.0 + jnp.exp(-u))
            act = u * sig
            mid = (act * w).astype(BF).astype(F32)
            back = jnp.sum(mid * m, axis=1, keepdims=True)
            back = jnp.where(here & picked, back, 0.0)
            back_all = back if back_all is None else back_all + back
            gm = gate * m
            up_back = (gm * act).astype(BF)
            pre_back = (gm * w * sig * (1.0 + u * (1.0 - sig))).astype(BF)
            term = lax.dot_general(
                pre_back, wg_ref[j], NT, preferred_element_type=F32
            ) + lax.dot_general(up_back, wu_ref[j], NT, preferred_element_type=F32)
            dx = term if dx is None else dx + term
            chosen = masks(ids_ref, rows, e, half, u.shape[1])
            for kind, value in enumerate(((mid * gate).astype(BF), pre_back, up_back)):
                for c in range(2):
                    part = value * chosen[c]
                    unit = 2 * kind + c
                    parts[unit] = part if parts[unit] is None else parts[unit] + part
        dx_s[rows, :] += dx
        back_s[rows, :] += back_all
        for unit in range(6):
            ent_ref[unit, rows, :] += parts[unit]

    @pl.when(step == pl.num_programs(0) - 1)
    def _():
        dx_keep_ref[:, :width] = dx_s[:half, :]
        dx_send_ref[:, :width] = dx_s[half:, :].astype(BF)
        pad = jnp.zeros((half, 128 - experts), F32)
        dx_keep_ref[:, width:] = jnp.concatenate([back_s[:half, :], pad], axis=1)
        dx_send_ref[:, width:] = jnp.concatenate([back_s[half:, :], pad], axis=1).astype(BF)


def whole(*shape):
    return pl.BlockSpec(shape, lambda e: (0,) * len(shape))


def some_of(*shape):
    return pl.BlockSpec(shape, lambda e: (e,) + (0,) * (len(shape) - 1))


def experts_call(core, ids, mine, theirs, g, wr, wg, wu, wd, first=()):
    half, width = mine.shape
    tok = 2 * half
    experts, _, hidden = wg.shape
    per = 2
    return pl.pallas_call(
        drop_first(functools.partial(experts_kernel, per), 9, len(first)),
        out_shape=(
            jax.ShapeDtypeStruct((half, width + 128), F32),
            jax.ShapeDtypeStruct((half, width + 128), BF),
            jax.ShapeDtypeStruct((tok, experts), F32),
            jax.ShapeDtypeStruct((6, tok, hidden), BF),
        ),
        grid=(experts // per,),
        in_specs=[
            pl.BlockSpec(memory_space=pltpu.SMEM),
            whole(tok, 2),
            whole(half, width),
            whole(half, width),
            whole(tok, width),
            whole(experts, width),
            some_of(per, width, hidden),
            some_of(per, width, hidden),
            some_of(per, hidden, width),
        ]
        + anywhere(len(first)),
        out_specs=(
            whole(half, width + 128),
            whole(half, width + 128),
            whole(tok, experts),
            whole(6, tok, hidden),
        ),
        scratch_shapes=[
            pltpu.VMEM((tok, width), BF),
            pltpu.VMEM((tok, width), BF),
            pltpu.VMEM((tok, width), F32),
            pltpu.VMEM((tok, experts), F32),
        ],
        compiler_params=params(dimension_semantics=("arbitrary",)),
        name="experts",
        cost_estimate=cost(26),
    )(core, ids, mine, theirs, g, wr, wg, wu, wd, *first)


def mix_kernel(per, ids_ref, ent_ref, wd_ref, keep_ref, send_ref, mix_s):
    step = pl.program_id(0)
    half, width = keep_ref.shape

    @pl.when(step == 0)
    def _():
        mix_s[...] = jnp.zeros(mix_s.shape, F32)

    for i in range(2):
        rows = pl.ds(i * half, half)
        out = None
        for j in range(per):
            one, two = masks(ids_ref, rows, step * per + j, half, ent_ref.shape[2])
            mid = ent_ref[0, rows, :] * one + ent_ref[1, rows, :] * two
            term = jnp.dot(mid, wd_ref[j], preferred_element_type=F32)
            out = term if out is None else out + term
        mix_s[rows, :] += out

    @pl.when(step == pl.num_programs(0) - 1)
    def _():
        keep_ref[...] = mix_s[:half, :]
        send_ref[...] = mix_s[half:, :].astype(BF)


def mix_call(ids, ent, wd, first=()):
    _, tok, hidden = ent.shape
    experts, _, width = wd.shape
    half = tok // 2
    per = 2
    return pl.pallas_call(
        drop_first(functools.partial(mix_kernel, per), 3, len(first)),
        out_shape=(
            jax.ShapeDtypeStruct((half, width), F32),
            jax.ShapeDtypeStruct((half, width), BF),
        ),
        grid=(experts // per,),
        in_specs=[
            whole(tok, 2),
            pl.BlockSpec((2, tok, hidden), lambda e: (0, 0, 0)),
            some_of(per, hidden, width),
        ]
        + anywhere(len(first)),
        out_specs=(whole(half, width), whole(half, width)),
        scratch_shapes=[pltpu.VMEM((tok, width), F32)],
        compiler_params=params(dimension_semantics=("arbitrary",)),
        name="mix",
        cost_estimate=cost(8),
    )(ids, ent, wd, *first)


def expert_grads_kernel(count, base, places, ids_ref, *refs):
    x_refs = refs[0:2]
    g_refs = refs[2:4]
    ents = refs[4 : 4 + count]
    outs, theirs_ref = refs[-4:-1], refs[-1]
    e = (pl.program_id(0) + base).astype(F32)
    cols = outs[0].shape[1]
    sums = [None, None, None]
    for b in range(count):
        half = x_refs[0].shape[2]
        hidden = ents[b].shape[2]
        for i in range(2):
            rows = pl.ds(i * half, half)
            one = jnp.where(ids_ref[places[b], rows, 0:1] == e, 1.0, 0.0).astype(BF)
            two = jnp.where(ids_ref[places[b], rows, 1:2] == e, 1.0, 0.0).astype(BF)
            one = jnp.broadcast_to(one, (half, hidden))
            two = jnp.broadcast_to(two, (half, hidden))
            xt = x_refs[i][b]
            gt = g_refs[i][b]
            for kind in range(3):
                value = ents[b][2 * kind, rows, :] * one + ents[b][2 * kind + 1, rows, :] * two
                term = jnp.dot(gt if kind == 0 else xt, value, preferred_element_type=F32)
                sums[kind] = term if sums[kind] is None else sums[kind] + term
    for kind in range(3):
        outs[kind][0] = sums[kind][:cols]
        theirs_ref[kind, 0] = sums[kind][cols:].astype(BF)


def expert_grads(base, experts, ids, places, xm, xo, gm, go, ents, first=()):
    cols = xm.shape[1] // 2
    hidden = ents[0].shape[-1]
    operands = [ids, xm, xo, gm, go] + list(ents)
    specs = [pl.BlockSpec(x.shape, lambda e, nd=x.ndim: (0,) * nd) for x in operands]
    out_spec = pl.BlockSpec((1, cols, hidden), lambda e: (e, 0, 0))
    kernel = functools.partial(expert_grads_kernel, len(ents), base, places)
    return pl.pallas_call(
        drop_first(kernel, len(operands), len(first)),
        out_shape=(jax.ShapeDtypeStruct((experts, cols, hidden), F32),) * 3
        + (jax.ShapeDtypeStruct((3, experts, cols, hidden), BF),),
        grid=(experts,),
        in_specs=specs + anywhere(len(first)),
        out_specs=(out_spec,) * 3
        + (pl.BlockSpec((3, 1, cols, hidden), lambda e: (0, e, 0, 0)),),
        compiler_params=params(dimension_semantics=("arbitrary",)),
        name="expert_grads",
        cost_estimate=cost(1.2 * experts),
    )(*operands, *first)


def finish_kernel(*refs):
    mine, got_ref, outs = refs[:3], refs[3], refs[-3:]
    for kind in range(3):
        value = mine[kind][0] + got_ref[kind, 0].astype(F32)
        outs[kind][0] = value


def finish(base, experts, mine, got, outs=None, first=()):
    some, cols, hidden = mine[0].shape
    kept = [] if outs is None else list(outs)
    part = pl.BlockSpec((1, cols, hidden), lambda e: (e, 0, 0))
    place = pl.BlockSpec((1, cols, hidden), lambda e: (base + e, 0, 0))
    waits = kept + list(first)
    return pl.pallas_call(
        drop_first(finish_kernel, 4, len(waits)),
        out_shape=(jax.ShapeDtypeStruct((experts, cols, hidden), F32),) * 3,
        grid=(some,),
        in_specs=[part] * 3
        + [pl.BlockSpec((3, 1, cols, hidden), lambda e: (0, e, 0, 0))]
        + anywhere(len(waits)),
        out_specs=(place,) * 3,
        input_output_aliases={4 + i: i for i in range(len(kept))},
        compiler_params=params(dimension_semantics=("arbitrary",)),
        name="finish",
        cost_estimate=cost(3),
    )(*mine, got, *waits)


def my_rows(core_ref, ref):
    half = ref.shape[0] // 2
    return ref[pl.ds(pl.multiple_of(core_ref[0] * half, half), half), :]


def simple(kernel, name, outs, core, *operands, first=()):
    return pl.pallas_call(
        drop_first(kernel, 1 + len(operands), len(first)),
        out_shape=tuple(jax.ShapeDtypeStruct(shape, dtype) for shape, dtype in outs),
        in_specs=[pl.BlockSpec(memory_space=pltpu.SMEM)] + vspec(len(operands)) + anywhere(len(first)),
        out_specs=tuple(vspec(len(outs))),
        compiler_params=params(),
        name=name,
        cost_estimate=cost(5),
    )(core, *operands, *first)


def middle_kernel(core_ref, x_ref, gain_ref, *refs):
    parts, weights = refs[:4], refs[4:8]
    hidden_ref, a2_ref = refs[8:]
    total = my_rows(core_ref, x_ref).astype(F32)
    for part, weight in zip(parts, weights):
        total = total + jnp.dot(part[...], weight[...], preferred_element_type=F32)
    inv = lax.rsqrt(jnp.mean(total * total, axis=-1, keepdims=True) + eps)
    hidden_ref[...] = total
    a2_ref[...] = (total * inv * gain_ref[...][None, :]).astype(BF)


def back_kernel(
    core_ref,
    near_ref,
    got_ref,
    hidden_ref,
    a2_ref,
    gates_ref,
    ids_ref,
    wr_ref,
    gain_ref,
    g_ref,
    grad_ref,
    att_ref,
    misc_ref,
):
    half, width = hidden_ref.shape
    experts = wr_ref.shape[0]
    total = near_ref[...].astype(F32) + got_ref[...].astype(F32)
    gate_back = total[:, width:][:, :experts]
    gates = gates_ref[:half, :]
    lane = lax.broadcasted_iota(jnp.int32, (half, experts), 1)
    picked = (lane == ids_ref[:half, 0:1]) | (lane == ids_ref[:half, 1:2])
    logit = gates * (gate_back - jnp.sum(gates * gate_back, axis=-1, keepdims=True))
    logit = jnp.where(picked, logit, 0.0).astype(BF)
    back = total[:, :width] + jnp.dot(logit, wr_ref[...], preferred_element_type=F32)
    hidden = hidden_ref[...]
    inv = lax.rsqrt(jnp.mean(hidden * hidden, axis=-1, keepdims=True) + eps)
    upstream = my_rows(core_ref, g_ref).astype(F32)
    scaled = back * gain_ref[...][None, :]
    grad = upstream + inv * (
        scaled - hidden * inv * inv * jnp.mean(scaled * hidden, axis=-1, keepdims=True)
    )
    grad_ref[...] = grad
    att_ref[...] = grad.astype(BF)
    misc_ref[:8, :] = lax.dot_general(logit, a2_ref[...], TN, preferred_element_type=F32)
    ffn = jnp.sum(back * hidden * inv, axis=0, keepdims=True)
    misc_ref[8:, :] = jnp.broadcast_to(ffn, (8, width))


def query_back_kernel(core_ref, *refs):
    pairs, weights, out_ref = refs[:2], refs[2:6], refs[6]
    total = None
    for i, weight in enumerate(weights):
        term = lax.dot_general(
            pairs[i // 2][i % 2], weight[...], NT, preferred_element_type=F32
        )
        total = term if total is None else total + term
    out_ref[...] = total


def input_kernel(core_ref, x_ref, gain_ref, grad_ref, query_ref, *refs):
    parts, weights = refs[:4], refs[4:8]
    out_ref, norm_ref = refs[8:]
    back = query_ref[...]
    for part, weight in zip(parts, weights):
        start = weight.shape[1] - part.shape[1]
        back = back + lax.dot_general(
            part[...], weight[:, start:], NT, preferred_element_type=F32
        )
    x = my_rows(core_ref, x_ref).astype(F32)
    inv = lax.rsqrt(jnp.mean(x * x, axis=-1, keepdims=True) + eps)
    scaled = back * gain_ref[...][None, :]
    out_ref[...] = grad_ref[...] + inv * (
        scaled - x * inv * inv * jnp.mean(scaled * x, axis=-1, keepdims=True)
    )
    norm = jnp.sum(back * x * inv, axis=0, keepdims=True)
    norm_ref[...] = jnp.broadcast_to(norm, norm_ref.shape)


def place_kernel(core_ref, mine_ref, theirs_ref, out_ref):
    half = mine_ref.shape[0]
    out_ref[pl.ds(pl.multiple_of(core_ref[0] * half, half), half), :] = mine_ref[...]
    out_ref[pl.ds(pl.multiple_of((1 - core_ref[0]) * half, half), half), :] = theirs_ref[...]


def columns_kernel(waits, owner_ref, core_ref, x_ref, *refs):
    outs, turned = refs[waits:-1], refs[-1]
    per, rows_out, half = outs[0].shape
    side = owner_ref.shape[0] // (per * len(outs))
    cols = rows_out // side
    x = my_rows(core_ref, x_ref) if x_ref.shape[0] != half else x_ref[...]
    turned[...] = x.T
    for r, out_ref in enumerate(outs):
        for i in range(per * side):
            rows = pl.ds(pl.multiple_of(owner_ref[r * per * side + i] * cols, 16), cols)
            out_ref[i // side, (i % side) * cols : (i % side + 1) * cols, :] = turned[rows, :]


def columns(owner, core, x, half, groups, side, first=()):
    n = owner.shape[0]
    width = x.shape[1]
    smem = pl.BlockSpec(memory_space=pltpu.SMEM)
    out = jax.ShapeDtypeStruct((n // (groups * side), side * (width // n), half), BF)
    return pl.pallas_call(
        functools.partial(columns_kernel, len(first)),
        out_shape=(out,) * groups,
        in_specs=[smem, smem] + vspec(1) + [pl.BlockSpec(memory_space=pl.ANY)] * len(first),
        out_specs=tuple(vspec(groups)),
        scratch_shapes=[pltpu.VMEM((width, half), BF)],
        compiler_params=params(),
        name="columns",
        cost_estimate=cost(2.5),
    )(owner, core, x, *first)


def weight_kernel(shape, extra, owner_ref, *refs):
    out_ref, turned, misc_turned = refs[-3:]
    n, cols, _ = out_ref.shape
    at = 0
    column = 0
    for group, pairs in enumerate(shape):
        lefts, rights = refs[at : at + pairs], refs[at + pairs : at + 2 * pairs]
        at += 2 * pairs
        row = 0
        for left in lefts:
            turned[group, :, row : row + left.shape[0]] = left[...].T
            row += left.shape[0]
        right = jnp.concatenate([r[...] for r in rights], axis=0) if pairs > 1 else rights[0][...]
        for i in range(n):
            rows = pl.ds(pl.multiple_of(owner_ref[i] * cols, 16), cols)
            out_ref[i, :, column : column + right.shape[1]] = jnp.dot(
                turned[group, rows, :], right, preferred_element_type=F32
            ).astype(BF)
        column += right.shape[1]
    if extra:
        misc = refs[at][...]
        spare = jnp.zeros((128 - misc.shape[0], misc.shape[1]), F32)
        misc_turned[...] = jnp.concatenate([misc, spare], axis=0).T
        for i in range(n):
            rows = pl.ds(pl.multiple_of(owner_ref[i] * cols, 16), cols)
            out_ref[i, :, column:] = misc_turned[rows, :].astype(BF)


def weight_terms(owner, groups, misc=None, us=4, first=()):
    n = owner.shape[0]
    width = groups[0][0][0].shape[1]
    rows = sum(x.shape[0] for x in groups[0][0])
    out_width = sum(rights[0].shape[1] for _, rights in groups)
    operands = []
    for lefts, rights in groups:
        operands += list(lefts) + list(rights)
    if misc is not None:
        operands.append(misc)
        out_width += 128
    shape = tuple(len(lefts) for lefts, _ in groups)
    return pl.pallas_call(
        drop_first(
            functools.partial(weight_kernel, shape, misc is not None),
            1 + len(operands),
            len(first),
        ),
        out_shape=jax.ShapeDtypeStruct((n, width // n, out_width), BF),
        in_specs=[pl.BlockSpec(memory_space=pltpu.SMEM)]
        + vspec(len(operands))
        + anywhere(len(first)),
        out_specs=vspec(1)[0],
        scratch_shapes=[pltpu.VMEM((len(groups), width, rows), BF), pltpu.VMEM((width, 128), F32)],
        compiler_params=params(),
        name="weight_terms",
        cost_estimate=cost(us),
    )(owner, *operands, *first)


def per_device(
    n_ctx,
    layer_input,
    segment_ids,
    expert_ids,
    norm_gain,
    query_weight,
    key_weight,
    value_weight,
    output_weight,
    ffn_gain,
    router_weight,
    gate_weight,
    up_weight,
    down_weight,
    cotangent,
):
    tok, width = layer_input.shape
    half = tok // 2
    groups = H // KV
    kv_local = key_weight.shape[1] // HD
    heads = kv_local * groups
    kvw = key_weight.shape[1]
    experts = gate_weight.shape[0]
    cols = width // n_ctx
    digits = digits_of(n_ctx)
    keys = rel_keys(digits)
    upper_first = list(range(1, len(digits))) + [0]
    lower_first = list(range(len(digits)))
    me = lax.axis_index("ctx")
    core = lax.axis_index("wa") % 2
    core_arr = jnp.full((1,), core, jnp.int32)
    owner_to = jnp.stack([digit_offset(me, k, digits, 1) for k in keys]).astype(jnp.int32)
    owner_from = jnp.stack([digit_offset(me, k, digits, -1) for k in keys]).astype(jnp.int32)
    gain_one, gain_two = norm_gain, ffn_gain
    router = router_weight.T

    def mine_first(x):
        return jnp.where(core == 0, x, jnp.concatenate([x[half:], x[:half]], axis=0))

    segs = mine_first(segment_ids).astype(BF)
    ids = mine_first(expert_ids)
    extra = jnp.concatenate([segs, ids[:, 0].astype(BF), ids[:, 1].astype(BF)])
    extra = jnp.pad(extra, (0, EXTRA * 2 * kvw - extra.shape[0])).reshape(EXTRA, 2 * kvw)
    a1, q, kv = project(
        core_arr, layer_input, gain_one, query_weight, key_weight, value_weight, extra
    )
    tops = digits[-1][1]
    staged = len(digits) == 2
    side = digits[0][1]
    low, top = digits[0], digits[-1]
    turned_digits = digits[1:] + digits[:1]
    turned_keys = [(k[-1],) + k[:-1] for k in rel_keys(turned_digits)]
    owner_turned = jnp.stack(
        [digit_offset(me, k, digits, -1) for k in turned_keys]
    ).astype(jnp.int32)

    wo_chip = other_chip(output_weight)
    kv_weight = jnp.concatenate([key_weight, value_weight], axis=1)
    kv_core = other_core(kv_weight)
    wq_core = other_core(query_weight)
    g_out = columns(owner_to, core_arr, cotangent, half, tops, side, [kv])
    if staged:
        z, y = [kv], []
        for r in range(tops - 1):
            aside = [g_out[0], kv_core, wq_core] if r == tops - 2 else []
            z_next, y_next = tie([hop(z[r], n_ctx, top), hop(z[r], n_ctx, low)], aside)
            z.append(z_next)
            y.append(y_next)
        y.append(hop(z[-1], n_ctx, low))
        kv_list = [block for pair in zip(z, y) for block in pair]
    else:
        kv_blocks = gather_ctx(kv, n_ctx, digits, upper_first)
        kv_list = [kv_blocks[k] for k in keys]

    g_top = exchange_top(g_out, n_ctx, digits)

    heads_f32, heads_near, heads_far, lse = attend(
        q, kv_list, heads, groups, first=[g_out[0]]
    )
    heads_near, heads_far, wo_chip, *rest = tie(
        [heads_near, heads_far, wo_chip] + list(g_top[1:]), []
    )
    g_top = [g_top[0]] + list(rest)
    wo_parts = [output_weight, other_core(output_weight), wo_chip, other_core(wo_chip)]

    parts = all_parts(heads_near, heads_far)
    g_pieces = exchange_rest(g_top, n_ctx, digits)
    hidden_one, a2_mine = simple(
        middle_kernel,
        "middle",
        [((half, width), F32), ((half, width), BF)],
        core_arr,
        layer_input,
        gain_two,
        *parts,
        *wo_parts,
    )
    a2_far = other_core(a2_mine)
    a2_out = columns(owner_to, core_arr, a2_mine, half, tops, side)
    a2_top = exchange_top(a2_out, n_ctx, digits)
    wq_chip = other_chip(query_weight)

    dx_keep, dx_send, gates, ent = experts_call(
        core_arr,
        ids,
        a2_mine,
        a2_far,
        cotangent,
        router,
        gate_weight,
        up_weight,
        down_weight,
        first=[a2_out[0]],
    )
    dx_send, wq_chip, *rest = tie(
        [dx_send, wq_chip] + list(a2_top[1:]), [array for array, _ in g_pieces]
    )
    a2_top = [a2_top[0]] + list(rest)

    near = (dx_keep + other_core(dx_send).astype(F32)).astype(BF)
    got = other_chip(near)
    if staged:
        z = [ent]
        z_next = hop(ent, n_ctx, top)
    wq_parts = [query_weight, wq_core, wq_chip, other_core(wq_chip)]
    hidden_grad, att_near, misc = simple(
        back_kernel,
        "back",
        [((half, width), F32), ((half, width), BF), ((16, width), F32)],
        core_arr,
        near,
        got,
        hidden_one,
        a2_mine,
        gates,
        ids,
        router,
        gain_two,
        cotangent,
        first=[wq_parts[3]],
    )
    att_far = other_core(att_near)
    mix_keep, mix_send = mix_call(ids, ent, down_weight, [att_near])
    mix_near = (mix_keep + other_core(mix_send).astype(F32)).astype(BF)
    (kv_weight,) = tie([kv_weight], [got])
    kv_chip = other_chip(kv_weight)
    a2_pieces = exchange_rest(a2_top, n_ctx, digits)
    if staged:
        (z_next,) = tie([z_next], [mix_send])
        z.append(z_next)
        z_next = hop(z[1], n_ctx, top)

    begin = [att_near, att_far, output_weight, heads_f32]
    sides = [[kv_list[i] for i, k in enumerate(keys) if k[0] == r] for r in range(side)]
    dkv_far, head_grad, delta, dq_going = attend_back(
        q,
        kv_list[0],
        lse,
        [block for r in range(1, side) for block in sides[r]],
        heads,
        groups,
        start=begin,
        end=False,
        first=[z[1]] if staged else [],
    )
    mix_near, kv_chip = tie([mix_near, kv_chip], [dq_going])
    mix_got = other_chip(mix_near)
    dkv_far_got = hop(dkv_far, n_ctx, low)
    ids_all = routes(sides[0], tok, [dq_going])
    a2_stack, a2_stack_far = swapped(a2_pieces, [dq_going])
    g_stack, g_stack_far = swapped(g_pieces, [dq_going])
    terms_o = weight_terms(
        owner_turned,
        [([att_near, att_far], [heads_near, heads_far])],
        misc,
        first=[dq_going, a2_stack, g_stack],
    )
    waits = [ids_all, a2_stack_far, g_stack_far, terms_o]
    if staged:
        (z_next,) = tie([z_next], [terms_o])
        z.append(z_next)
        z_next = hop(z[2], n_ctx, top)
        waits = waits + [z[2]]
    o_sides = cut(terms_o, side)
    o_got = hop(o_sides[1], n_ctx, low)
    dkv_near, dq_near, dq_far = attend_back(
        q,
        kv_list[0],
        lse,
        sides[0],
        heads,
        groups,
        going=[head_grad, delta, dq_going],
        first=waits,
    )
    dkv_far_got, mix_got = tie([dkv_far_got, mix_got], [dq_near])
    kv_weights = [kv_weight, kv_core, kv_chip, other_core(kv_chip)]


    dkv_sides = [
        total([dkv_far_got[i : i + 1], dkv_near[i : i + 1]]).astype(BF)
        for i in range(dkv_near.shape[0])
    ]
    if staged:
        dkv_sent = scatter_sends(dkv_sides, n_ctx, top)
    dq_core = other_core(dq_far)

    terms_q = weight_terms(
        owner_turned,
        [([a1], [jnp.concatenate([dq_near, dq_far], axis=0)])],
        first=[dkv_sides[1 % len(dkv_sides)]],
    )
    dq_core, o_got = tie([dq_core, o_got], [terms_q, kv_weights[3]])
    dq_pair = jnp.stack([dq_near, dq_core], axis=0)
    q_sides = cut(terms_q, side)
    q_got = hop(q_sides[1], n_ctx, low)

    if staged:
        z_next, dq_pair = tie([z_next, dq_pair], [terms_q])
        z.append(z_next)
        ents = z
    else:
        upper = gather_ctx(ent, n_ctx, digits, upper_first[:-1])
        ents = [upper[k] for k in keys if k[0] == 0]
    dq_chip = other_chip(dq_pair)
    some = experts // 2
    places = tuple(range(len(ents)))
    shared = [a2_stack, a2_stack_far, g_stack, g_stack_far, ents]
    *grads_a, send_a = expert_grads(0, some, ids_all, places, *shared)
    (q_got,) = tie([q_got], [send_a])
    got_a = hop(send_a, n_ctx, low)
    (dq_chip,) = tie([dq_chip], [send_a])
    (query_back,) = simple(
        query_back_kernel,
        "query_back",
        [((half, width), F32)],
        core_arr,
        dq_pair,
        dq_chip,
        *wq_parts,
    )
    if staged:
        more = tie(dkv_sent[1:], [query_back])
        dkv_own = total([dkv_sent[0]] + list(more))[0].astype(BF)
    else:
        dkv_own = scatter_ctx(jnp.concatenate(dkv_sides, axis=0), n_ctx, digits[1:]).astype(BF)

    terms = jnp.concatenate(
        [total([o_sides[0], o_got]), total([q_sides[0], q_got])], axis=2
    ).astype(BF)
    dkv_parts = all_parts(dkv_own[:half], dkv_own[half:])
    late = weight_terms(owner_from, [([a1], [dkv_own])])
    *grads_b, send_b = expert_grads(
        some,
        experts - some,
        ids_all,
        places,
        *shared,
        first=[send_a, dkv_own, terms, late],
    )
    got_b = hop(send_b, n_ctx, low)
    *dkv_rest, got_a = tie(dkv_parts[1:] + [got_a], [send_b])
    dkv_parts = [dkv_parts[0]] + dkv_rest
    in_mine, norm_row = simple(
        input_kernel,
        "input",
        [((half, width), F32), ((8, width), F32)],
        core_arr,
        layer_input,
        gain_one,
        hidden_grad,
        query_back,
        *dkv_parts,
        *kv_weights,
    )
    in_far = other_core(in_mine)
    done = finish(0, experts, grads_a, got_a, first=[norm_row])
    (late,) = tie([late], [send_b])
    (mix_got,) = tie([mix_got], [norm_row])
    out_mine = hidden_one + mix_near.astype(F32) + mix_got.astype(F32)
    out_far = other_core(out_mine)
    (layer_output,) = simple(
        place_kernel, "place", [((tok, width), F32)], core_arr, out_mine, out_far
    )
    (input_grad,) = simple(
        place_kernel, "place", [((tok, width), F32)], core_arr, in_mine, in_far
    )
    if staged:
        blocks = cut(terms, tops)
        moving = blocks[1]
        waits = [[in_mine], [input_grad], [layer_output]]
        for r in range(2, tops + 1):
            (moving,) = tie([hop(moving, n_ctx, top)], waits[r - 2])
            moving = total([moving, blocks[r % tops]]).astype(BF if r < tops else F32)
        terms_own = moving[0]
    else:
        terms_own = scatter_ctx(terms, n_ctx, digits[1:])
    late_own = scatter_ctx(
        late, n_ctx, digits, lambda at, xs: tie(xs, [done[0]] if at else [input_grad])
    )
    norm_rel = norm_row[0].reshape(n_ctx, cols)[owner_from]
    norm_own = scatter_ctx(norm_rel, n_ctx, digits, kind=F32)
    down_grad, gate_grad, up_grad = finish(some, experts, grads_b, got_b, done)

    qw = heads * HD
    output_grad = terms_own[:, :qw].T
    small = jnp.concatenate(
        [terms_own[:, qw : qw + experts + 1], norm_own[:, None]], axis=1
    )
    small = small + other_core(small)
    return (
        layer_output,
        input_grad,
        small[:, experts + 1],
        terms_own[:, qw + 128 :],
        late_own[:, :kvw],
        late_own[:, kvw:],
        output_grad,
        small[:, experts],
        small[:, :experts],
        gate_grad,
        up_grad,
        jnp.swapaxes(down_grad, 1, 2),
    )


def solution(mesh):
    in_specs = (
        P("ctx", None),
        P("ctx"),
        P("ctx", None),
        P(),
        P(None, "wa"),
        P(None, "wa"),
        P(None, "wa"),
        P("wa", None),
        P(),
        P(),
        P(None, None, "wa"),
        P(None, None, "wa"),
        P(None, "wa", None),
        P("ctx", None),
    )
    out_specs = (
        P("ctx", None),
        P("ctx", None),
        P("ctx"),
        P("ctx", "wa"),
        P("ctx", "wa"),
        P("ctx", "wa"),
        P("wa", "ctx"),
        P("ctx"),
        P("ctx", None),
        P(None, "ctx", "wa"),
        P(None, "ctx", "wa"),
        P(None, "wa", "ctx"),
    )
    return jax.shard_map(
        functools.partial(per_device, mesh.shape["ctx"]),
        mesh=mesh,
        in_specs=in_specs,
        out_specs=out_specs,
        check_vma=False,
    )
```
